256 devices in a mesh: frame: 16 (over z_lo, y), patch: 16 (over x, z_hi, core).
Axes of the slice: x: 4, y: 4, z: 8 (z_hi: 2, z_lo: 4; z = z_hi * 4 + z_lo), core: 2. Of those that a mesh axis runs over, the one named last changes fastest.
Arguments:
- latents: bfloat16 [2, 16, 1024, 1152], P(None, 'frame', 'patch'), may hold values from -6 to 6
- mod_spatial: float32 [2, 3, 1152], replicated, may hold values from -3 to 3
- mod_temporal: float32 [2, 3, 1152], replicated, may hold values from -3 to 3
- qkv_spatial: bfloat16 [1152, 1728], replicated, may hold values from -0.1875 to 0.1875
- out_spatial: bfloat16 [576, 1152], replicated, may hold values from -0.25 to 0.25
- qkv_temporal: bfloat16 [1152, 1728], replicated, may hold values from -0.1875 to 0.1875
- out_temporal: bfloat16 [576, 1152], replicated, may hold values from -0.25 to 0.25
- cotangent: bfloat16 [2, 16, 1024, 1152], P(None, 'frame', 'patch'), may hold values from -6 to 6
Outputs:
- grad_latents: bfloat16 [2, 16, 1024, 1152], P(None, 'frame', 'patch')
- grad_qkv_spatial: float32 [1152, 1728], P('frame', 'patch')
- grad_out_spatial: float32 [576, 1152], P('frame', 'patch')
- grad_qkv_temporal: float32 [1152, 1728], P('frame', 'patch')
- grad_out_temporal: float32 [576, 1152], P('frame', 'patch')
The draws below stay inside these ranges and needn't reach their ends.
All inputs are finite; a program needn't handle non-finite values.
Results may differ from the reference program's by a relative error of at most 0.03.
Values may be sent and summed in bfloat16 or wider, within the bound.
A program may use at most 128 MiB of HBM per device.

```python
import jax
import jax.numpy as jnp
from jax import lax

D = 1152
HEAD_DIM = 72
HEADS = 8
CLIPS = 2
ATT = 576
FRAMES = 16
PATCHES = 1024


def spiked(values, rng, source, target, blocks, factor):
    def block_of(axis_at):
        return (jnp.arange(values.shape[axis_at]) // (values.shape[axis_at] // blocks)).reshape((-1,) + (1,) * (values.ndim - 1 - axis_at))

    first = jax.random.permutation(rng, blocks)[block_of(target)]
    other_side = (block_of(target) + blocks // 2) % blocks
    return jnp.where((block_of(source) == first) | (block_of(source) == other_side), factor * values, values)


def steps_of(key, extent, split, smallest, top_value):
    loudness = 1.0
    for axis_at, parts in split:
        steps = jax.random.uniform(jax.random.fold_in(jax.random.fold_in(key, 6), axis_at), (parts,), jnp.float32, smallest / len(split), top_value / len(split))
        loudness = loudness * jnp.repeat(jnp.exp(steps), extent[axis_at] // parts).reshape((-1,) + (1,) * (len(extent) - 1 - axis_at))
    return loudness


def normal_values(stream_key, extent, scale, limit, cuts=(), dtype=jnp.bfloat16):
    array = jax.random.normal(stream_key, extent, jnp.float32) * scale
    if len(cuts) > 0:
        array = steps_of(stream_key, extent, cuts, -0.22, 0.18) * array
    return jnp.clip(array, min=-limit, max=limit).astype(dtype)


def noise_with(key, extent, scale, limit, pieces, heavy, held_as=jnp.bfloat16):
    values = scale * jax.random.normal(key, extent, jnp.float32)
    if pieces:
        values = values * steps_of(key, extent, pieces, -0.22, 0.18)
    return jnp.clip(spiked(values, jax.random.fold_in(key, 3), *heavy), -limit, limit).astype(held_as)


def setup_inputs(seed: int = 0) -> dict:
    splits = jax.random.split(jax.random.key(seed), 9)
    return {
        "latents": noise_with(splits[0], (CLIPS, FRAMES, PATCHES, D), 1.0, 6.0, ((1, 16), (2, 16)), (1, 3, 16, 2.0)),
        "mod_spatial": normal_values(splits[1], (CLIPS, 3, D), 0.5, 3.0, (), jnp.float32),
        "mod_temporal": normal_values(splits[2], (CLIPS, 3, D), 0.5, 3.0, (), jnp.float32),
        "qkv_spatial": normal_values(splits[3], (D, 3 * ATT), D ** -0.5, 0.1875),
        "out_spatial": normal_values(splits[4], (ATT, D), ATT ** -0.5, 0.25),
        "qkv_temporal": normal_values(splits[5], (D, 3 * ATT), D ** -0.5, 0.1875),
        "out_temporal": normal_values(splits[6], (ATT, D), ATT ** -0.5, 0.25),
        "cotangent": noise_with(splits[7], (CLIPS, FRAMES, PATCHES, D), 1.0, 6.0, ((1, 16), (2, 16)), (2, 3, 16, 2.0)),
    }


epsilon = 1e-06

def modulate(source, offset, stretch):
    centre = source - lax.optimization_barrier(jnp.mean(source, axis=-1, keepdims=True))
    spread = lax.optimization_barrier(jnp.mean(centre * centre, axis=-1, keepdims=True))
    return centre * lax.rsqrt(spread + epsilon) * (1.0 + stretch) + offset

def head_norm(projected):
    shaped = projected.reshape(projected.shape[:-1] + (3, HEADS, HEAD_DIM))
    paired = shaped[..., :2, :, :]
    paired = paired * lax.rsqrt(lax.optimization_barrier(jnp.mean(paired * paired, axis=-1, keepdims=True)) + epsilon)
    return jnp.concatenate([paired, shaped[..., 2:, :, :]], axis=-3).reshape(projected.shape)

def contract(left, right):
    return lax.dot_general(left.astype(jnp.float32), right.astype(jnp.float32), (((0, 1, 2), (0, 1, 2)), ((), ())), preferred_element_type=jnp.float32)

def attend_forward(packed):
    packed = packed.astype(jnp.float32)
    queries = packed[..., :HEAD_DIM]
    key_rows = packed[..., HEAD_DIM:2 * HEAD_DIM]
    values = packed[..., 2 * HEAD_DIM:]
    scores = jnp.einsum('nqd,nkd->nqk', queries, key_rows) * HEAD_DIM ** (-0.5)
    raised = jnp.exp(scores)
    softmax = raised / lax.optimization_barrier(jnp.sum(raised, axis=-1, keepdims=True))
    rounded = lax.optimization_barrier(softmax.astype(jnp.bfloat16)).astype(jnp.float32)
    return jnp.einsum('nqk,nkd->nqd', rounded, values).astype(jnp.bfloat16)

def attend_backward(packed, dout):
    packed = packed.astype(jnp.float32)
    dout = dout.astype(jnp.float32)
    queries = packed[..., :HEAD_DIM]
    key_rows = packed[..., HEAD_DIM:2 * HEAD_DIM]
    values = packed[..., 2 * HEAD_DIM:]
    scale_factor = HEAD_DIM ** (-0.5)
    scores = jnp.einsum('nqd,nkd->nqk', queries, key_rows) * scale_factor
    raised = jnp.exp(scores)
    softmax = raised / lax.optimization_barrier(jnp.sum(raised, axis=-1, keepdims=True))
    rounded = lax.optimization_barrier(softmax.astype(jnp.bfloat16)).astype(jnp.float32)
    dvalues = jnp.einsum('nqk,nqd->nkd', rounded, dout).astype(jnp.bfloat16)
    dweights = jnp.einsum('nqd,nkd->nqk', dout, values)
    dscores = softmax * (dweights - lax.optimization_barrier(jnp.sum(dweights * softmax, axis=-1, keepdims=True))) * scale_factor
    dscores = lax.optimization_barrier(dscores.astype(jnp.bfloat16)).astype(jnp.float32)
    dqueries = jnp.einsum('nqk,nkd->nqd', dscores, key_rows).astype(jnp.bfloat16)
    dkey_rows = jnp.einsum('nqk,nqd->nkd', dscores, queries).astype(jnp.bfloat16)
    return jnp.concatenate([dqueries, dkey_rows, dvalues], axis=-1)

def branch_in(source, modulation, weight):
    offset = modulation[:, 0, None, None, :]
    stretch = modulation[:, 1, None, None, :]
    normed = modulate(source.astype(jnp.float32), offset, stretch).astype(jnp.bfloat16)
    projected = jnp.dot(normed, weight, preferred_element_type=jnp.float32)
    return (normed, projected, head_norm(projected).astype(jnp.bfloat16))

def branch_out(source, attended, modulation, weight):
    projected = jnp.dot(attended, weight, preferred_element_type=jnp.float32)
    return (source.astype(jnp.float32) + modulation[:, 2, None, None, :] * projected).astype(jnp.bfloat16)

def branch_back(source, normed, projected, dpacked, modulation, weight, upstream):
    pullback = jax.vjp(head_norm, projected)[1]
    dprojected = pullback(dpacked.astype(jnp.float32))[0].astype(jnp.bfloat16)
    grad_weight = contract(normed, dprojected)
    dnormed = lax.dot_general(dprojected, weight, (((3,), (1,)), ((), ())), preferred_element_type=jnp.float32)
    offset = modulation[:, 0, None, None, :]
    stretch = modulation[:, 1, None, None, :]

    def shaped(source_value):
        return modulate(source_value, offset, stretch)
    dsource = jax.vjp(shaped, source.astype(jnp.float32))[1](dnormed)[0]
    return (grad_weight, (upstream + dsource).astype(jnp.bfloat16))

def gate_back(upstream, attended, modulation, weight):
    scaled = (upstream * modulation[:, 2, None, None, :]).astype(jnp.bfloat16)
    grad_out = contract(attended, scaled)
    dattended = lax.dot_general(scaled, weight, (((3,), (1,)), ((), ())), preferred_element_type=jnp.float32).astype(jnp.bfloat16)
    return (grad_out, dattended)

def spatial_rows(packed):
    clip_count, frames, patches = packed.shape[:3]
    return packed.reshape(clip_count, frames, patches, 3, HEADS, HEAD_DIM).transpose(0, 1, 4, 2, 3, 5).reshape(clip_count * frames, HEADS, patches, 3 * HEAD_DIM)

def temporal_rows(packed):
    clip_count, frames, patches = packed.shape[:3]
    return packed.reshape(clip_count, frames, patches, 3, HEADS, HEAD_DIM).transpose(0, 2, 4, 1, 3, 5).reshape(clip_count * patches * HEADS, frames, 3 * HEAD_DIM)

def pair_backward(paired_items):
    return attend_backward(paired_items[0], paired_items[1])

def reference(latents, mod_spatial, mod_temporal, qkv_spatial, out_spatial, qkv_temporal, out_temporal, cotangent):
    clip_count, frames, patches = latents.shape[:3]
    width_att = HEADS * HEAD_DIM
    normed_s, projected_s, packed_s = branch_in(latents, mod_spatial, qkv_spatial)
    rows_s = spatial_rows(packed_s)
    outputs_s = lax.map(attend_forward, rows_s)
    attended_s = outputs_s.reshape(clip_count, frames, HEADS, patches, HEAD_DIM).transpose(0, 1, 3, 2, 4).reshape(clip_count, frames, patches, width_att)
    middle = branch_out(latents, attended_s, mod_spatial, out_spatial)
    normed_t, projected_t, packed_t = branch_in(middle, mod_temporal, qkv_temporal)
    rows_t = temporal_rows(packed_t)
    outputs_t = attend_forward(rows_t)
    attended_t = outputs_t.reshape(clip_count, patches, HEADS, frames, HEAD_DIM).transpose(0, 3, 1, 2, 4).reshape(clip_count, frames, patches, width_att)
    upstream = cotangent.astype(jnp.float32)
    grad_out_t, dattended_t = gate_back(upstream, attended_t, mod_temporal, out_temporal)
    dframe = dattended_t.reshape(clip_count, frames, patches, HEADS, HEAD_DIM).transpose(0, 2, 3, 1, 4).reshape(clip_count * patches * HEADS, frames, HEAD_DIM)
    dflat = attend_backward(rows_t, dframe)
    dpacked_t = dflat.reshape(clip_count, patches, HEADS, frames, 3, HEAD_DIM).transpose(0, 3, 1, 4, 2, 5).reshape(clip_count, frames, patches, 3 * width_att)
    grad_qkv_t, dmiddle = branch_back(middle, normed_t, projected_t, dpacked_t, mod_temporal, qkv_temporal, upstream)
    upstream_s = dmiddle.astype(jnp.float32)
    grad_out_s, dattended_s = gate_back(upstream_s, attended_s, mod_spatial, out_spatial)
    dpatch = dattended_s.reshape(clip_count, frames, patches, HEADS, HEAD_DIM).transpose(0, 1, 3, 2, 4).reshape(clip_count * frames, HEADS, patches, HEAD_DIM)
    dgrouped = lax.map(pair_backward, (rows_s, dpatch))
    dpacked_s = dgrouped.reshape(clip_count, frames, HEADS, patches, 3, HEAD_DIM).transpose(0, 1, 3, 4, 2, 5).reshape(clip_count, frames, patches, 3 * width_att)
    grad_qkv_s, grad_latents = branch_back(latents, normed_s, projected_s, dpacked_s, mod_spatial, qkv_spatial, upstream_s)
    return (grad_latents, grad_qkv_s, grad_out_s, grad_qkv_t, grad_out_t)
```

```python
import jax
import jax.numpy as jnp
from jax import lax
from jax.experimental import pallas as pl
from jax.experimental.pallas import tpu as pltpu
from jax.sharding import PartitionSpec as P

F32 = jnp.float32
BF = jnp.bfloat16
MESH = pl.DeviceIdType.MESH
HD = 72
HEADS = 8
ATT = 576
D = 1152
QKV = 1728
EPS = 1e-06
SCALE = HD**-0.5


def nn(a, b):
    return lax.dot_general(a, b, (((1,), (0,)), ((), ())), preferred_element_type=F32)


def nt(a, b):
    return lax.dot_general(a, b, (((1,), (1,)), ((), ())), preferred_element_type=F32)


def tn(a, b):
    return lax.dot_general(a, b, (((0,), (0,)), ((), ())), preferred_element_type=F32)


def owner(c, h):
    return (h // 2) * 4 + c * 2 + h % 2


def normalise(x):
    centre = x - jnp.mean(x, axis=-1, keepdims=True)
    r = lax.rsqrt(jnp.mean(centre * centre, axis=-1, keepdims=True) + EPS)
    return centre * r, r


def normalise_back(dn, stretch, xh, r):
    dx = dn * (1.0 + stretch)
    dx = dx - xh * jnp.mean(dx * xh, axis=-1, keepdims=True)
    dx = r * dx
    return dx - jnp.mean(dx, axis=-1, keepdims=True)


def inverse_norm(x):
    return lax.rsqrt(jnp.sum(x * x, axis=-1, keepdims=True) * (1.0 / HD) + EPS)


def head_back(dy, y, r):
    return r * (dy - y * (jnp.sum(dy * y, axis=-1, keepdims=True) * (1.0 / HD)))


def rounded(x):
    return x.astype(BF).astype(F32)


def zeros(*shape):
    return jnp.zeros(shape, F32)


def fold(x, near):
    n, _, w = x.shape
    far = x[:, :, near:]
    pad = 2 * near - w
    far = jnp.concatenate([far, zeros(n, 8, pad)], axis=-1)
    return jnp.concatenate([x[:, :, :near], far], axis=1)


def unfold(x, w):
    near = x.shape[-1]
    return jnp.concatenate([x[:, :8, :], x[:, 8:, : w - near]], axis=-1)


def widen(x, width):
    return jnp.concatenate([x, zeros(x.shape[0], width - x.shape[1])], axis=-1)


class Exchange:
    def __init__(self, send, recv, ssem, rsem, n, me, place):
        self.send, self.recv, self.ssem, self.rsem = send, recv, ssem, rsem
        self.n, self.me, self.place = n, me, place

    def copy(self, to, slot):
        return pltpu.make_async_remote_copy(
            src_ref=self.send.at[to],
            dst_ref=self.recv.at[slot],
            send_sem=self.ssem.at[to],
            recv_sem=self.rsem.at[slot],
            device_id=self.place(to),
            device_id_type=MESH,
        )

    def start(self):
        def step(i, carry):
            self.copy(lax.rem(self.me + i, self.n), self.me).start()
            return carry

        lax.fori_loop(1, self.n, step, 0)
        self.recv[self.me] = self.send[self.me]

    def wait(self):
        def step(i, carry):
            other = lax.rem(self.me + self.n - i, self.n)
            self.copy(other, other).wait()
            return carry

        lax.fori_loop(1, self.n, step, 0)


def kernel(
    lat, cot, mod_s, mod_t, wqs_h, wos_h, wqt_h, wot_h,
    gl, gqs, gos, gqt, got,
    wqs, wos, wqt, wot, wsem,
    normed, proj,
    a_s, a_r, b1_s, b1_r, b2_s, b2_r, t1_s, t1_r, t2_s, t2_r,
    c2_s, c2_r, c1_s, c1_r, dm_s, dm_r, d_s, d_r, xsems,
    q_b, k_b, v_b, rqk, att, do_b, kt_b, dq_f, dk_f, dv_f,
    ng, ngsem,
    xl, xrv, xr, xsem, lt,
    sx, rx, syq, ryq, syo, ryo, sxo, rxo, gys, gyr, sem4,
    szq, rzq, szo, rzo, gzs, gzr, sem8,
    fs, fr, fsem,
):
    f = lax.axis_index("frame")
    p = lax.axis_index("patch")
    core = lax.rem(p, 2)
    zh = lax.rem(lax.div(p, 2), 2)
    x = lax.div(p, 4)
    y = lax.rem(f, 4)
    zl = lax.div(f, 4)
    head = 2 * x + core
    clip_t = lax.div(f, 8)
    z = zh * 4 + zl

    loads = [
        pltpu.make_async_copy(src, dst, wsem.at[i])
        for i, (src, dst) in enumerate(
            ((wqs_h, wqs), (wos_h, wos), (wqt_h, wqt), (wot_h, wot))
        )
    ]
    for load in loads:
        load.start()

    barrier = pltpu.get_barrier_semaphore()

    def greet(i, carry):
        pl.semaphore_signal(
            barrier, inc=1, device_id={"frame": lax.rem(f + i, 16)}, device_id_type=MESH
        )
        pl.semaphore_signal(
            barrier, inc=1, device_id={"patch": lax.rem(p + i, 16)}, device_id_type=MESH
        )
        return carry

    lax.fori_loop(1, 16, greet, 0)

    def greet_z(i, carry):
        pl.semaphore_signal(
            barrier,
            inc=1,
            device_id={
                "frame": 4 * lax.rem(zl + i, 4) + y,
                "patch": 4 * x + 2 * (1 - zh) + core,
            },
            device_id_type=MESH,
        )
        return carry

    lax.fori_loop(1, 4, greet_z, 0)

    def on_patch(i):
        return {"patch": i}

    def on_frame(i):
        return {"frame": i}

    def on_x(i):
        return {"patch": 4 * i + 2 * zh + core}

    def on_y(i):
        return {"frame": 4 * zl + i}

    def on_z(i):
        return {
            "frame": 4 * lax.rem(i, 4) + y,
            "patch": 4 * x + 2 * lax.div(i, 4) + core,
        }

    ex_a = Exchange(a_s, a_r, xsems.at[0, 0], xsems.at[0, 1], 16, p, on_patch)
    ex_b1 = Exchange(b1_s, b1_r, xsems.at[1, 0], xsems.at[1, 1], 16, p, on_patch)
    ex_b2 = Exchange(b2_s, b2_r, xsems.at[2, 0], xsems.at[2, 1], 16, f, on_frame)
    ex_t1 = Exchange(t1_s, t1_r, xsems.at[3, 0], xsems.at[3, 1], 16, f, on_frame)
    ex_t2 = Exchange(t2_s, t2_r, xsems.at[4, 0], xsems.at[4, 1], 16, f, on_frame)
    ex_c2 = Exchange(c2_s, c2_r, xsems.at[5, 0], xsems.at[5, 1], 16, f, on_frame)
    ex_c1 = Exchange(c1_s, c1_r, xsems.at[6, 0], xsems.at[6, 1], 16, p, on_patch)
    ex_dm = Exchange(dm_s, dm_r, xsems.at[7, 0], xsems.at[7, 1], 16, f, on_frame)
    ex_d = Exchange(d_s, d_r, xsems.at[8, 0], xsems.at[8, 1], 16, p, on_patch)
    ex_xq = Exchange(sx, rx, sem4.at[0, 0], sem4.at[0, 1], 4, x, on_x)
    ex_yq = Exchange(syq, ryq, sem4.at[1, 0], sem4.at[1, 1], 4, y, on_y)
    ex_yo = Exchange(syo, ryo, sem4.at[2, 0], sem4.at[2, 1], 4, y, on_y)
    ex_xo = Exchange(sxo, rxo, sem4.at[3, 0], sem4.at[3, 1], 4, x, on_x)
    ex_gy = Exchange(gys, gyr, sem4.at[4, 0], sem4.at[4, 1], 4, y, on_y)
    ex_zq = Exchange(szq, rzq, sem8.at[0, 0], sem8.at[0, 1], 8, z, on_z)
    ex_zo = Exchange(szo, rzo, sem8.at[1, 0], sem8.at[1, 1], 8, z, on_z)
    ex_gz = Exchange(gzs, gzr, sem8.at[2, 0], sem8.at[2, 1], 8, z, on_z)

    for c in range(2):
        xh, _ = normalise(lat[c].astype(F32))
        normed[c] = (xh * (1.0 + mod_s[1, c : c + 1, :]) + mod_s[0, c : c + 1, :]).astype(BF)
    loads[0].wait()
    proj[...] = nt(normed[...].reshape(128, D), wqs[...])
    lane = lax.broadcasted_iota(jnp.int32, (128, 256), 1)
    for h in range(HEADS):
        q = proj[:, HD * h : HD * h + HD]
        k = proj[:, ATT + HD * h : ATT + HD * h + HD]
        v = proj[:, 2 * ATT + HD * h : 2 * ATT + HD * h + HD]
        rq = inverse_norm(q)
        rk = inverse_norm(k)
        row = jnp.concatenate([q * rq, k * rk, v, zeros(128, 40)], axis=-1)
        row = jnp.where(lane == 216, rq, row)
        row = jnp.where(lane == 217, rq - rounded(rq), row)
        row = jnp.where(lane == 218, rk, row)
        row = jnp.where(lane == 219, rk - rounded(rk), row)
        row = row.astype(BF)
        a_s[owner(0, h)] = row[:64]
        a_s[owner(1, h)] = row[64:]
    pl.semaphore_wait(barrier, 33)
    ex_a.start()

    for c in range(2):
        t1_s[8 * c : 8 * c + 8] = fold(lat[c].astype(F32).reshape(8, 8, D), 640).astype(BF)
        t2_s[8 * c : 8 * c + 8] = fold(cot[c].astype(F32).reshape(8, 8, D), 640).astype(BF)

    ex_a.wait()
    ex_t1.start()
    ex_t2.start()
    ng[p] = normed[zh]
    gather_z = pltpu.make_async_remote_copy(
        src_ref=normed.at[1 - zh],
        dst_ref=ng.at[p],
        send_sem=ngsem.at[0, 0],
        recv_sem=ngsem.at[1, 0],
        device_id={"patch": 4 * x + 2 * (1 - zh) + core},
        device_id_type=MESH,
    )
    gather_z.start()

    for part in range(4):
        rows = a_r[4 * part : 4 * part + 4].reshape(256, 256).astype(F32)
        at = pl.ds(256 * part, 256)
        q_b[at, :] = rows[:, 0:HD].astype(BF)
        k_b[at, :] = rows[:, HD : 2 * HD].astype(BF)
        v_b[at, :] = rows[:, 2 * HD : 3 * HD].astype(BF)
        rqk[at, 0:1] = rows[:, 216:217] + rows[:, 217:218]
        rqk[at, 1:2] = rows[:, 218:219] + rows[:, 219:220]

    def attend(i, carry):
        at = pl.ds(pl.multiple_of(i * 256, 256), 256)
        e = jnp.exp(nt(q_b[at, :], k_b[...]) * SCALE)
        weights = (e * (1.0 / jnp.sum(e, axis=-1, keepdims=True))).astype(BF)
        att[at, :] = nn(weights, v_b[...])
        return carry

    lax.fori_loop(0, 4, attend, 0)
    pieces = att[...].reshape(16, 4, 16, HD)
    row = [pieces[:, j].reshape(256, HD) for j in range(4)] + [zeros(256, 96)]
    b1_s[...] = jnp.concatenate(row, axis=-1).astype(BF).reshape(16, 16, 384)
    ex_b1.start()
    ex_b1.wait()
    for c in range(2):
        blocks = [b1_r[owner(c, h)].astype(F32) for h in range(HEADS)]
        rows = [
            jnp.concatenate([b[:, HD * j : HD * j + HD] for b in blocks], axis=-1)
            for j in range(4)
        ]
        tokens = jnp.concatenate(rows, axis=0).reshape(8, 8, ATT)
        b2_s[8 * c : 8 * c + 8] = fold(tokens, 384).astype(BF)
    ex_b2.start()

    gather_z.wait()

    def gather_copy(block, other, slot):
        return pltpu.make_async_remote_copy(
            src_ref=ng.at[block],
            dst_ref=ng.at[block],
            send_sem=ngsem.at[0, slot],
            recv_sem=ngsem.at[1, slot],
            device_id={"patch": other},
            device_id_type=MESH,
        )

    def gather_x(i, s, back):
        other = lax.rem(x + i, 4)
        block = lax.rem(x + 4 - i, 4) if back else x
        return gather_copy(4 * block + 2 * s + core, 4 * other + 2 * zh + core, 2 * i - 1 + s)

    for i in range(1, 4):
        for s in range(2):
            gather_x(i, s, False).start()

    def pick(ref, i):
        return jnp.where(clip_t == 0, ref[i, 0:1, :], ref[i, 1:2, :])

    gate_s = pick(mod_s, 2)
    shift_t, stretch_t, gate_t = pick(mod_t, 0), pick(mod_t, 1), pick(mod_t, 2)
    ex_t1.wait()
    ex_t2.wait()
    lat_t = unfold(t1_r[...].astype(F32), D).reshape(128, D)
    cot_t = unfold(t2_r[...].astype(F32), D).reshape(128, D)
    scaled_t = (cot_t * gate_t).astype(BF)
    for load in loads[1:]:
        load.wait()
    dout_t = nt(scaled_t, wot[...])
    ex_b2.wait()
    att_s = unfold(b2_r[...].astype(F32), ATT).reshape(128, ATT)
    middle = rounded(lat_t + gate_s * nn(att_s.astype(BF), wos[...]))
    xh_t, r_t = normalise(middle)
    normed_t = (xh_t * (1.0 + stretch_t) + shift_t).astype(BF)
    proj[...] = nt(normed_t, wqt[...])
    same = lax.rem(lax.broadcasted_iota(jnp.int32, (128, 128), 0), 8) == lax.rem(
        lax.broadcasted_iota(jnp.int32, (128, 128), 1), 8
    )
    att_parts, dq_parts, dk_parts, dv_parts = [], [], [], []
    for h in range(HEADS):
        q = proj[:, HD * h : HD * h + HD]
        k = proj[:, ATT + HD * h : ATT + HD * h + HD]
        v = proj[:, 2 * ATT + HD * h : 2 * ATT + HD * h + HD].astype(BF)
        rq = inverse_norm(q)
        rk = inverse_norm(k)
        q = q * rq
        k = k * rk
        qb, kb = q.astype(BF), k.astype(BF)
        e = jnp.where(same, jnp.exp(nt(qb, kb) * SCALE), 0.0)
        soft = e * (1.0 / jnp.sum(e, axis=-1, keepdims=True))
        soft_b = soft.astype(BF)
        att_parts.append(nn(soft_b, v))
        do = dout_t[:, HD * h : HD * h + HD].astype(BF)
        dp = nt(do, v)
        ds = (soft * (dp - jnp.sum(dp * soft, axis=-1, keepdims=True)) * SCALE).astype(BF)
        dq_parts.append(head_back(rounded(nn(ds, kb)), q, rq))
        dk_parts.append(head_back(rounded(tn(ds, qb)), k, rk))
        dv_parts.append(tn(soft_b, do))
    att_t = jnp.concatenate(att_parts, axis=-1)
    dproj_t = jnp.concatenate(dq_parts + dk_parts + dv_parts, axis=-1)
    dn = nn(dproj_t.astype(BF), wqt[...])
    dmiddle = rounded(cot_t + normalise_back(dn, stretch_t, xh_t, r_t))
    scaled_s = (dmiddle * gate_s).astype(BF)
    datt = nt(scaled_s, wos[...])
    c2_s[...] = fold(datt.reshape(16, 8, ATT), 384).astype(BF)
    ex_c2.start()

    for i in range(1, 4):
        for s in range(2):
            gather_x(i, s, True).wait()

    def spread_rows(a):
        parts = []
        for yy in range(4):
            for zz in range(4):
                at = 36 * (4 * zz + yy)
                parts += [a[:, at : at + 36], zeros(128, 4)]
        return parts

    xl[core] = jnp.concatenate(
        [normed_t.astype(F32)] + spread_rows(att_t) + spread_rows(att_s), axis=-1
    ).astype(BF)
    st, ss = scaled_t.astype(F32), scaled_s.astype(F32)
    for cc in range(2):
        parts = []
        for b in range(8):
            at = 108 * (2 * b + cc)
            parts += [dproj_t[:, at : at + 108], zeros(128, 20)]
        for full in (st, ss):
            parts += [full[:, HD * (2 * b + cc) : HD * (2 * b + cc) + HD] for b in range(8)]
            parts += [zeros(128, 64)]
        xrv[cc] = jnp.concatenate(parts, axis=-1).astype(BF)
    xr[core] = xrv[core]

    def pair_copies(slot):
        there = {"patch": p + 1 - 2 * core}
        return [
            pltpu.make_async_remote_copy(
                src_ref=src,
                dst_ref=dst.at[slot],
                send_sem=xsem.at[0, i],
                recv_sem=xsem.at[1, i],
                device_id=there,
                device_id_type=MESH,
            )
            for i, (src, dst) in enumerate(((xl.at[core], xl), (xrv.at[1 - core], xr)))
        ]

    for copy in pair_copies(core):
        copy.start()
    dm_s[...] = fold(dmiddle.reshape(16, 8, D), 640).astype(BF)
    ex_c2.wait()
    tokens = unfold(c2_r[...].astype(F32), ATT).reshape(2, 64, ATT)
    for c in range(2):
        for h in range(HEADS):
            part = tokens[c][:, HD * h : HD * h + HD].reshape(4, 16, HD)
            row = jnp.concatenate([part[j] for j in range(4)] + [zeros(16, 96)], axis=-1)
            c1_s[owner(c, h)] = row.astype(BF)
    ex_c1.start()
    ex_dm.start()

    def gather_core(i, back):
        side = 1 - core if back else core
        return gather_copy(2 * i + side, p + 1 - 2 * core, 7 + i)

    for i in range(8):
        gather_core(i, False).start()

    for copy in pair_copies(1 - core):
        copy.wait()
    lt[...] = jnp.transpose(xl[...].reshape(256, 2432).astype(F32)).astype(BF)
    right = xr[...].reshape(256, 2304)
    for i in range(4):
        g = nn(lt[0:D, :], right[:, 256 * i : 256 * i + 256]).astype(F32)
        g = g.reshape(4, 4, HD, 256)
        for yy in range(4):
            sx[i, 288 * yy : 288 * yy + 288, :] = g[:, yy].reshape(288, 256).astype(BF)
    ex_xq.start()
    for i in range(2):
        g = nn(lt[D + 640 * i : D + 640 * i + 640, :], right[:, 1024 + 640 * i : 1664 + 640 * i])
        for yy in range(4):
            syo[yy, 160 * i : 160 * i + 160, :] = g[160 * yy : 160 * yy + 160].astype(BF)
    ex_yo.start()

    for part in range(4):
        at = pl.ds(256 * part, 256)
        kt_b[:, at] = jnp.transpose(widen(k_b[at, :].astype(F32), 128)).astype(BF)
    ex_c1.wait()
    got_do = c1_r[...].astype(F32)
    parts = [got_do[:, :, HD * j : HD * j + HD] for j in range(4)]
    do_b[...] = jnp.stack(parts, axis=1).reshape(1024, HD).astype(BF)
    dk_f[...] = jnp.zeros_like(dk_f)
    dv_f[...] = jnp.zeros_like(dv_f)

    def attend_back(i, carry):
        at = pl.ds(pl.multiple_of(i * 256, 256), 256)
        qb, dob = q_b[at, :], do_b[at, :]
        e = jnp.exp(nt(k_b[...], qb) * SCALE)
        soft = e * (1.0 / jnp.sum(e, axis=0, keepdims=True))
        dv_f[...] += nn(soft.astype(BF), dob)
        dp = nt(v_b[...], dob)
        ds = (soft * (dp - jnp.sum(dp * soft, axis=0, keepdims=True)) * SCALE).astype(BF)
        dk_f[...] += nn(ds, qb)
        dq_f[at, :] = jnp.transpose(nn(kt_b[...], ds))[:, :HD]
        return carry

    lax.fori_loop(0, 4, attend_back, 0)
    for part in range(4):
        at = pl.ds(256 * part, 256)
        dq = head_back(rounded(dq_f[at, :]), q_b[at, :].astype(F32), rqk[at, 0:1])
        dk = head_back(rounded(dk_f[at, :]), k_b[at, :].astype(F32), rqk[at, 1:2])
        row = jnp.concatenate([dq, dk, dv_f[at, :], zeros(256, 40)], axis=-1).astype(BF)
        d_s[4 * part : 4 * part + 4] = row.reshape(4, 64, 256)
    ex_d.start()

    ex_xq.wait()
    for yy in range(4):
        at = pl.ds(288 * yy, 288)
        syq[yy] = sum(rx[i, at, :].astype(F32) for i in range(4)).astype(BF)
    ex_yq.start()
    ex_yo.wait()
    total = sum(ryo[i].astype(F32) for i in range(4))
    for i in range(4):
        sxo[i] = widen(total[:, 144 * i : 144 * i + 144], 256).astype(BF)
    ex_xo.start()

    for i in range(8):
        gather_core(i, True).wait()
    g = tn(ng[...].reshape(1024, D), d_s[...].reshape(1024, 256)).reshape(4, 4, HD, 256)
    for yy in range(4):
        gys[yy] = g[:, yy].reshape(288, 256).astype(BF)
    ex_gy.start()

    ex_yq.wait()
    total = sum(ryq[i].astype(F32) for i in range(4))
    for i in range(8):
        zz, s = i % 4, i // 4
        part = total[HD * zz : HD * zz + HD, 128 * s : 128 * s + 128]
        szq[i] = jnp.concatenate([part, zeros(8, 128)], axis=0).astype(BF)
    ex_zq.start()
    ex_xo.wait()
    total = sum(rxo[i].astype(F32) for i in range(4))
    for i in range(8):
        zz, s = i % 4, i // 4
        part = total[:, HD * s : HD * s + HD]
        part = jnp.concatenate(
            [part[40 * zz : 40 * zz + 40], part[160 + 40 * zz : 200 + 40 * zz]], axis=0
        )
        szo[i] = widen(part, 128).astype(BF)
    ex_zo.start()

    ex_d.wait()
    parts = []
    for c in range(2):
        blocks = [d_r[owner(c, h)].astype(F32) for h in range(HEADS)]
        parts.append(
            jnp.concatenate(
                [b[:, HD * j : HD * j + HD] for j in range(3) for b in blocks], axis=-1
            )
        )
    dn = nn(jnp.concatenate(parts, axis=0).astype(BF), wqs[...])
    ex_dm.wait()
    dmid = unfold(dm_r[...].astype(F32), D).reshape(2, 64, D)
    for c in range(2):
        xh, r = normalise(lat[c].astype(F32))
        back = normalise_back(dn[64 * c : 64 * c + 64], mod_s[1, c : c + 1, :], xh, r)
        gl[c] = (dmid[c] + back).astype(BF)

    ex_gy.wait()
    total = sum(gyr[i].astype(F32) for i in range(4))
    cols = [total[:, 36 * b : 36 * b + 36] for b in range(6)]
    sides = [
        jnp.concatenate([cols[s], cols[2 + s], cols[4 + s], zeros(288, 20)], axis=-1)
        for s in range(2)
    ]
    for i in range(8):
        zz, s = i % 4, i // 4
        part = sides[s][HD * zz : HD * zz + HD]
        gzs[i] = jnp.concatenate([part, zeros(8, 128)], axis=0).astype(BF)
    ex_gz.start()

    ex_zq.wait()
    total = sum(rzq[i].astype(F32) for i in range(8))
    gqt[...] = total[:HD, :108]
    ex_zo.wait()
    total = sum(rzo[i].astype(F32) for i in range(8))
    got[...] = total[:36, :HD]
    gos[...] = total[40:76, :HD]

    ex_gz.wait()
    total = sum(gzr[i].astype(F32) for i in range(8))
    for j in range(3):
        fs[j] = widen(total[:HD, 36 * j : 36 * j + 36], 128)

    def final_send(j):
        block = 16 * j + 2 * head + zh
        to, slot = lax.div(block, 3), lax.rem(block, 3)
        return to, slot, pltpu.make_async_remote_copy(
            src_ref=fs.at[j],
            dst_ref=fr.at[slot],
            send_sem=fsem.at[0, j],
            recv_sem=fsem.at[1, slot],
            device_id={"patch": to},
            device_id_type=MESH,
        )

    for j in range(3):
        to, slot, copy = final_send(j)

        @pl.when(to != p)
        def _():
            copy.start()

        @pl.when(to == p)
        def _():
            fr[slot] = fs[j]

    for j in range(3):
        to, slot, copy = final_send(j)

        @pl.when(to != p)
        def _():
            copy.wait_send()

    for slot in range(3):
        block = 3 * p + slot
        left = lax.rem(block, 16)
        src = lax.div(left, 4) * 4 + lax.rem(left, 2) * 2 + lax.rem(lax.div(left, 2), 2)

        @pl.when(src != p)
        def _():
            pltpu.make_async_remote_copy(
                src_ref=fs.at[0],
                dst_ref=fr.at[slot],
                send_sem=fsem.at[0, 0],
                recv_sem=fsem.at[1, slot],
                device_id={"patch": src},
                device_id_type=MESH,
            ).wait_recv()

    gqs[...] = jnp.concatenate([fr[j][:, :36] for j in range(3)], axis=-1)


def body(lat, mod_s, mod_t, wqs, wos, wqt, wot, cot):
    vmem = pl.BlockSpec(memory_space=pltpu.VMEM)
    hbm = pl.BlockSpec(memory_space=pl.ANY)
    dma = pltpu.SemaphoreType.DMA

    def buf(*shape):
        return pltpu.VMEM(shape, BF)

    def wide(*shape):
        return pltpu.VMEM(shape, F32)

    outs = pl.pallas_call(
        kernel,
        out_shape=(
            jax.ShapeDtypeStruct((2, 64, D), BF),
            jax.ShapeDtypeStruct((72, 108), F32),
            jax.ShapeDtypeStruct((36, 72), F32),
            jax.ShapeDtypeStruct((72, 108), F32),
            jax.ShapeDtypeStruct((36, 72), F32),
        ),
        in_specs=[vmem] * 4 + [hbm] * 4,
        out_specs=(vmem,) * 5,
        scratch_shapes=[
            buf(QKV, D), buf(ATT, D), buf(QKV, D), buf(ATT, D), dma((4,)),
            buf(2, 64, D), wide(128, QKV),
            buf(16, 64, 256), buf(16, 64, 256),
            buf(16, 16, 384), buf(16, 16, 384),
            buf(16, 16, 384), buf(16, 16, 384),
            buf(16, 16, 640), buf(16, 16, 640),
            buf(16, 16, 640), buf(16, 16, 640),
            buf(16, 16, 384), buf(16, 16, 384),
            buf(16, 16, 384), buf(16, 16, 384),
            buf(16, 16, 640), buf(16, 16, 640),
            buf(16, 64, 256), buf(16, 64, 256),
            dma((9, 2, 16)),
            buf(1024, HD), buf(1024, HD), buf(1024, HD), wide(1024, 2), wide(1024, HD),
            buf(1024, HD), buf(128, 1024), wide(1024, HD), wide(1024, HD), wide(1024, HD),
            buf(16, 64, D), dma((2, 15)),
            buf(2, 128, 2432), buf(2, 128, 2304), buf(2, 128, 2304), dma((2, 2)),
            buf(2432, 256),
            buf(4, 1152, 256), buf(4, 1152, 256),
            buf(4, 288, 256), buf(4, 288, 256),
            buf(4, 320, 640), buf(4, 320, 640),
            buf(4, 320, 256), buf(4, 320, 256),
            buf(4, 288, 256), buf(4, 288, 256),
            dma((5, 2, 4)),
            buf(8, 80, 128), buf(8, 80, 128),
            buf(8, 80, 128), buf(8, 80, 128),
            buf(8, 80, 128), buf(8, 80, 128),
            dma((3, 2, 8)),
            wide(3, 72, 128), wide(3, 72, 128), dma((2, 3)),
        ],
        compiler_params=pltpu.CompilerParams(
            collective_id=0, has_side_effects=True, vmem_limit_bytes=60 * 1024 * 1024
        ),
    )(
        lat.reshape(2, 64, D),
        cot.reshape(2, 64, D),
        mod_s.transpose(1, 0, 2),
        mod_t.transpose(1, 0, 2),
        wqs.T,
        wos,
        wqt.T,
        wot,
    )
    return (outs[0].reshape(2, 1, 64, D),) + tuple(outs[1:])


def solution(mesh):
    tokens = P(None, "frame", "patch", None)
    return jax.shard_map(
        body,
        mesh=mesh,
        in_specs=(tokens,) + (P(),) * 6 + (tokens,),
        out_specs=(tokens,) + (P("frame", "patch"),) * 4,
        check_vma=False,
    )
```

```python
import jax
import jax.numpy as jnp
from jax import lax
from jax.experimental import pallas as pl
from jax.experimental.pallas import tpu as pltpu
from jax.sharding import PartitionSpec as P

F32 = jnp.float32
BF = jnp.bfloat16
MESH = pl.DeviceIdType.MESH
HD = 72
HEADS = 8
ATT = 576
D = 1152
QKV = 1728
EPS = 1e-06
SCALE = HD**-0.5


def nn(a, b):
    return lax.dot_general(a, b, (((1,), (0,)), ((), ())), preferred_element_type=F32)


def nt(a, b):
    return lax.dot_general(a, b, (((1,), (1,)), ((), ())), preferred_element_type=F32)


def tn(a, b):
    return lax.dot_general(a, b, (((0,), (0,)), ((), ())), preferred_element_type=F32)


def owner(c, h):
    return (h // 2) * 4 + c * 2 + h % 2


def normalise(x):
    centre = x - jnp.mean(x, axis=-1, keepdims=True)
    r = lax.rsqrt(jnp.mean(centre * centre, axis=-1, keepdims=True) + EPS)
    return centre * r, r


def normalise_back(dn, stretch, xh, r):
    dx = dn * (1.0 + stretch)
    dx = dx - xh * jnp.mean(dx * xh, axis=-1, keepdims=True)
    dx = r * dx
    return dx - jnp.mean(dx, axis=-1, keepdims=True)


def inverse_norm(x):
    return lax.rsqrt(jnp.sum(x * x, axis=-1, keepdims=True) * (1.0 / HD) + EPS)


def head_back(dy, y, r):
    return r * (dy - y * (jnp.sum(dy * y, axis=-1, keepdims=True) * (1.0 / HD)))


def rounded(x):
    return x.astype(BF).astype(F32)


def zeros(*shape):
    return jnp.zeros(shape, F32)


def fold(x, near):
    n, _, w = x.shape
    far = x[:, :, near:]
    pad = 2 * near - w
    far = jnp.concatenate([far, zeros(n, 8, pad)], axis=-1)
    return jnp.concatenate([x[:, :, :near], far], axis=1)


def unfold(x, w):
    near = x.shape[-1]
    return jnp.concatenate([x[:, :8, :], x[:, 8:, : w - near]], axis=-1)


def widen(x, width):
    return jnp.concatenate([x, zeros(x.shape[0], width - x.shape[1])], axis=-1)


class Exchange:
    def __init__(self, send, recv, ssem, rsem, n, me, place):
        self.send, self.recv, self.ssem, self.rsem = send, recv, ssem, rsem
        self.n, self.me, self.place = n, me, place

    def copy(self, to, slot):
        return pltpu.make_async_remote_copy(
            src_ref=self.send.at[to],
            dst_ref=self.recv.at[slot],
            send_sem=self.ssem.at[to],
            recv_sem=self.rsem.at[slot],
            device_id=self.place(to),
            device_id_type=MESH,
        )

    def start(self):
        def step(i, carry):
            self.copy(lax.rem(self.me + i, self.n), self.me).start()
            return carry

        lax.fori_loop(1, self.n, step, 0)
        self.recv[self.me] = self.send[self.me]

    def wait(self):
        def step(i, carry):
            other = lax.rem(self.me + self.n - i, self.n)
            self.copy(other, other).wait()
            return carry

        lax.fori_loop(1, self.n, step, 0)


def kernel(
    lat, cot, mod_s, mod_t, wqs_h, wos_h, wqt_h, wot_h,
    gl, gqs, gos, gqt, got,
    wqs, wos, wqt, wot, wsem,
    normed, proj,
    a_s, a_r, b1_s, b1_r, att_s, scaled, dmid, t1_s, t1_r, t2_s, t2_r,
    c2_s, c2_r, c1_s, c1_r, dm_s, dm_r, d_s, d_r, dg, ngt, xsems,
    q_b, k_b, v_b, rqk, do_b, kt_b, dq_f, dk_f, dv_f,
    ng, ngsem, xn, xnsem, dt_s, dt_r, dtsem,
    xl, xrv, xr, xsem, lt,
    syq, ryq, syo, ryo, sxo, rxo, sxs, rxs, sys, rys, gys, gyr, sem4,
    szq, rzq, szo, rzo, sem8,
    fs, fr, fs_sem, fr_sem,
):
    f = lax.axis_index("frame")
    p = lax.axis_index("patch")
    core = lax.rem(p, 2)
    zh = lax.rem(lax.div(p, 2), 2)
    x = lax.div(p, 4)
    y = lax.rem(f, 4)
    zl = lax.div(f, 4)
    head = 2 * x + core
    clip_t = lax.div(f, 8)
    z = zh * 4 + zl

    loads = [
        pltpu.make_async_copy(src, dst, wsem.at[i])
        for i, (src, dst) in enumerate(
            ((wqs_h, wqs), (wot_h, wot), (wos_h, wos), (wqt_h, wqt))
        )
    ]
    loads[0].start()

    barrier = pltpu.get_barrier_semaphore()

    def greet(i, carry):
        pl.semaphore_signal(
            barrier, inc=1, device_id={"frame": lax.rem(f + i, 16)}, device_id_type=MESH
        )
        pl.semaphore_signal(
            barrier, inc=1, device_id={"patch": lax.rem(p + i, 16)}, device_id_type=MESH
        )
        return carry

    lax.fori_loop(1, 16, greet, 0)

    def greet_far(i, carry):
        pl.semaphore_signal(
            barrier,
            inc=1,
            device_id={
                "frame": 4 * lax.rem(zl + 1 + lax.div(i, 15), 4) + y,
                "patch": lax.rem(p + 1 + lax.rem(i, 15), 16),
            },
            device_id_type=MESH,
        )
        return carry

    lax.fori_loop(0, 45, greet_far, 0)

    def on_patch(i):
        return {"patch": i}

    def on_frame(i):
        return {"frame": i}

    def on_x(i):
        return {"patch": 4 * i + 2 * zh + core}

    def on_y(i):
        return {"frame": 4 * zl + i}

    def on_column(i):
        return {"patch": 4 * lax.rem(i, 4) + 2 * zh + lax.div(i, 4)}

    def on_z(i):
        return {
            "frame": 4 * lax.rem(i, 4) + y,
            "patch": 4 * x + 2 * lax.div(i, 4) + core,
        }

    ex_a = Exchange(a_s, a_r, xsems.at[0, 0], xsems.at[0, 1], 16, p, on_patch)
    ex_b1 = Exchange(b1_s, b1_r, xsems.at[1, 0], xsems.at[1, 1], 16, p, on_patch)
    ex_t1 = Exchange(t1_s, t1_r, xsems.at[3, 0], xsems.at[3, 1], 16, f, on_frame)
    ex_t2 = Exchange(t2_s, t2_r, xsems.at[4, 0], xsems.at[4, 1], 16, f, on_frame)
    ex_c2 = Exchange(c2_s, c2_r, xsems.at[5, 0], xsems.at[5, 1], 16, f, on_frame)
    ex_c1 = Exchange(c1_s, c1_r, xsems.at[6, 0], xsems.at[6, 1], 16, p, on_patch)
    ex_dm = Exchange(dm_s, dm_r, xsems.at[7, 0], xsems.at[7, 1], 16, f, on_frame)
    ex_d = Exchange(d_s, d_r, xsems.at[8, 0], xsems.at[8, 1], 16, p, on_patch)
    ex_dt = Exchange(dt_s, dt_r, dtsem.at[0], dtsem.at[1], 8, 4 * core + x, on_column)
    ex_yq = Exchange(syq, ryq, sem4.at[0, 0], sem4.at[0, 1], 4, y, on_y)
    ex_yo = Exchange(syo, ryo, sem4.at[1, 0], sem4.at[1, 1], 4, y, on_y)
    ex_xo = Exchange(sxo, rxo, sem4.at[2, 0], sem4.at[2, 1], 4, x, on_x)
    ex_xs = Exchange(sxs, rxs, sem4.at[4, 0], sem4.at[4, 1], 4, x, on_x)
    ex_ys = Exchange(sys, rys, sem4.at[5, 0], sem4.at[5, 1], 4, y, on_y)
    ex_gy = Exchange(gys, gyr, sem4.at[3, 0], sem4.at[3, 1], 4, y, on_y)
    ex_zq = Exchange(szq, rzq, sem8.at[0, 0], sem8.at[0, 1], 8, z, on_z)
    ex_zo = Exchange(szo, rzo, sem8.at[1, 0], sem8.at[1, 1], 8, z, on_z)

    for c in range(2):
        xh, _ = normalise(lat[c].astype(F32))
        normed[c] = (xh * (1.0 + mod_s[1, c : c + 1, :]) + mod_s[0, c : c + 1, :]).astype(BF)
    loads[0].wait()
    for load in loads[1:]:
        load.start()
    proj[...] = nt(normed[...].reshape(128, D), wqs[...])
    lane = lax.broadcasted_iota(jnp.int32, (128, 224), 1)
    for h in range(HEADS):
        q = proj[:, HD * h : HD * h + HD]
        k = proj[:, ATT + HD * h : ATT + HD * h + HD]
        v = proj[:, 2 * ATT + HD * h : 2 * ATT + HD * h + HD]
        rq = inverse_norm(q)
        rk = inverse_norm(k)
        row = jnp.concatenate([q * rq, k * rk, v, zeros(128, 8)], axis=-1)
        row = jnp.where(lane == 216, rq, row)
        row = jnp.where(lane == 217, rq - rounded(rq), row)
        row = jnp.where(lane == 218, rk, row)
        row = jnp.where(lane == 219, rk - rounded(rk), row)
        row = row.reshape(2, 4, 16, 224)
        for c in range(2):
            quarters = [row[c, j] for j in range(4)]
            a_s[owner(c, h)] = jnp.concatenate(quarters, axis=-1).astype(BF)
    pl.semaphore_wait(barrier, 75)
    ex_a.start()

    loads[1].wait()
    for c in range(2):
        scaled[c] = (cot[c].astype(F32) * mod_t[2, c : c + 1, :]).astype(BF)
    dout = nt(scaled[...].reshape(128, D), wot[...])
    for c in range(2):
        part = dout[64 * c : 64 * c + 64].reshape(8, 8, ATT)
        t2_s[8 * c : 8 * c + 8] = fold(part, 384).astype(BF)
    ex_a.wait()
    ng[core, x, zh] = normed[zh]
    gather_z = pltpu.make_async_remote_copy(
        src_ref=normed.at[1 - zh],
        dst_ref=ng.at[core, x, zh],
        send_sem=ngsem.at[0, 0],
        recv_sem=ngsem.at[1, 0],
        device_id={"patch": 4 * x + 2 * (1 - zh) + core},
        device_id_type=MESH,
    )
    gather_z.start()

    for part in range(4):
        rows = a_r[4 * part : 4 * part + 4].astype(F32)
        rows = [rows[:, :, 224 * j : 224 * j + 224] for j in range(4)]
        rows = jnp.stack(rows, axis=1).reshape(256, 224)
        at = pl.ds(256 * part, 256)
        q_b[at, :] = rows[:, 0:HD].astype(BF)
        k_b[at, :] = rows[:, HD : 2 * HD].astype(BF)
        v_b[at, :] = rows[:, 2 * HD : 3 * HD].astype(BF)
        rqk[at, 0:1] = rows[:, 216:217] + rows[:, 217:218]
        rqk[at, 1:2] = rows[:, 218:219] + rows[:, 219:220]

    def attend(i, carry):
        part = lax.rem(x + 1 + i, 4)
        at = pl.ds(pl.multiple_of(part * 256, 256), 256)
        e = jnp.exp(nt(q_b[at, :], k_b[...]) * SCALE)
        weights = (e * (1.0 / jnp.sum(e, axis=-1, keepdims=True))).astype(BF)
        pieces = nn(weights, v_b[...]).reshape(4, 4, 16, HD)
        row = [pieces[:, j].reshape(64, HD) for j in range(4)] + [zeros(64, 96)]
        row = jnp.concatenate(row, axis=-1).astype(BF).reshape(4, 16, 384)
        b1_s[pl.ds(4 * part, 4)] = row
        for j in range(4):
            to = 4 * part + j

            @pl.when(to != p)
            def _():
                ex_b1.copy(to, p).start()

        return carry

    lax.fori_loop(0, 4, attend, 0)
    b1_r[p] = b1_s[p]
    ex_t2.start()
    loads[2].wait()
    ex_b1.wait()
    atts = []
    for c in range(2):
        blocks = [b1_r[owner(c, h)].astype(F32) for h in range(HEADS)]
        rows = [
            jnp.concatenate([b[:, HD * j : HD * j + HD] for b in blocks], axis=-1)
            for j in range(4)
        ]
        atts.append(jnp.concatenate(rows, axis=0))
    att_s[...] = jnp.concatenate(atts, axis=0).astype(BF)
    added = nn(att_s[...], wos[...])
    for c in range(2):
        middle = lat[c].astype(F32) + mod_s[2, c : c + 1, :] * added[64 * c : 64 * c + 64]
        t1_s[8 * c : 8 * c + 8] = fold(middle.reshape(8, 8, D), 640).astype(BF)
    ex_t1.start()

    gather_z.wait()

    def gather_x(i, back):
        block = lax.rem(x + 4 - i, 4) if back else x
        return pltpu.make_async_remote_copy(
            src_ref=ng.at[core, block],
            dst_ref=ng.at[core, block],
            send_sem=ngsem.at[0, i],
            recv_sem=ngsem.at[1, i],
            device_id=on_x(lax.rem(x + i, 4)),
            device_id_type=MESH,
        )

    def gather_core(back):
        side = 1 - core if back else core
        return pltpu.make_async_remote_copy(
            src_ref=ng.at[side],
            dst_ref=ng.at[side],
            send_sem=ngsem.at[0, 4],
            recv_sem=ngsem.at[1, 4],
            device_id={"patch": p + 1 - 2 * core},
            device_id_type=MESH,
        )

    for i in range(1, 4):
        gather_x(i, False).start()

    def pick(ref, i):
        return jnp.where(clip_t == 0, ref[i, 0:1, :], ref[i, 1:2, :])

    shift_t, stretch_t = pick(mod_t, 0), pick(mod_t, 1)

    def spread_rows(a):
        parts = []
        for yy in range(4):
            for zz in range(4):
                at = 36 * (4 * zz + yy)
                parts += [a[:, at : at + 36], zeros(128, 4)]
        return parts

    def core_columns(full, cc):
        parts = [full[:, HD * (2 * b + cc) : HD * (2 * b + cc) + HD] for b in range(8)]
        return jnp.concatenate(parts + [zeros(128, 64)], axis=-1).astype(BF)

    xl[core, :, 640:1280] = jnp.concatenate(
        spread_rows(att_s[...].astype(F32)), axis=-1
    ).astype(BF)
    for cc in range(2):
        xrv[cc, :, 0:640] = core_columns(scaled[...].reshape(128, D).astype(F32), cc)

    loads[3].wait()
    ex_t1.wait()
    middle = unfold(t1_r[...].astype(F32), D).reshape(128, D)
    xh_t, r_t = normalise(middle)
    normed_t = (xh_t * (1.0 + stretch_t) + shift_t).astype(BF)
    xn[4 * core + x] = normed_t

    def normed_x(i, back):
        block = 4 * core + (lax.rem(x + 4 - i, 4) if back else x)
        return pltpu.make_async_remote_copy(
            src_ref=xn.at[block],
            dst_ref=xn.at[block],
            send_sem=xnsem.at[0, i],
            recv_sem=xnsem.at[1, i],
            device_id=on_x(lax.rem(x + i, 4)),
            device_id_type=MESH,
        )

    def normed_core(back):
        side = pl.ds(4 * (1 - core if back else core), 4)
        return pltpu.make_async_remote_copy(
            src_ref=xn.at[side],
            dst_ref=xn.at[side],
            send_sem=xnsem.at[0, 0],
            recv_sem=xnsem.at[1, 0],
            device_id={"patch": p + 1 - 2 * core},
            device_id_type=MESH,
        )

    for i in range(1, 4):
        normed_x(i, False).start()
    proj[...] = nt(normed_t, wqt[...])
    ex_t2.wait()
    dout_t = unfold(t2_r[...].astype(F32), ATT).reshape(128, ATT)
    same = lax.rem(lax.broadcasted_iota(jnp.int32, (128, 128), 0), 8) == lax.rem(
        lax.broadcasted_iota(jnp.int32, (128, 128), 1), 8
    )
    att_parts, dq_parts, dk_parts, dv_parts = [], [], [], []
    for h in range(HEADS):
        q = proj[:, HD * h : HD * h + HD]
        k = proj[:, ATT + HD * h : ATT + HD * h + HD]
        v = proj[:, 2 * ATT + HD * h : 2 * ATT + HD * h + HD].astype(BF)
        rq = inverse_norm(q)
        rk = inverse_norm(k)
        q = q * rq
        k = k * rk
        qb, kb = q.astype(BF), k.astype(BF)
        e = jnp.where(same, jnp.exp(nt(qb, kb) * SCALE), 0.0)
        soft = e * (1.0 / jnp.sum(e, axis=-1, keepdims=True))
        soft_b = soft.astype(BF)
        att_parts.append(nn(soft_b, v))
        do = dout_t[:, HD * h : HD * h + HD].astype(BF)
        dp = nt(do, v)
        ds = (soft * (dp - jnp.sum(dp * soft, axis=-1, keepdims=True)) * SCALE).astype(BF)
        dq_parts.append(head_back(rounded(nn(ds, kb)), q, rq))
        dk_parts.append(head_back(rounded(tn(ds, qb)), k, rk))
        dv_parts.append(tn(soft_b, do))
    att_t = jnp.concatenate(att_parts, axis=-1)
    dproj_t = jnp.concatenate(dq_parts + dk_parts + dv_parts, axis=-1)
    dn = nn(dproj_t.astype(BF), wqt[...])
    back = normalise_back(dn, stretch_t, xh_t, r_t)
    dm_s[...] = fold(back.reshape(16, 8, D), 640).astype(BF)
    ex_dm.start()
    c2_s[...] = fold(att_t.reshape(16, 8, ATT), 384).astype(BF)

    for cc in range(2):
        for xx in range(4):
            at = 108 * (4 * xx + cc)
            row = [dproj_t[:, at : at + 108], zeros(128, 20)]
            row += [dproj_t[:, at + 216 : at + 324], zeros(128, 20)]
            dt_s[4 * cc + xx] = jnp.concatenate(row, axis=-1).astype(BF)
    ex_dt.start()
    ex_c2.start()

    for i in range(1, 4):
        gather_x(i, True).wait()
    gather_core(False).start()
    for i in range(1, 4):
        normed_x(i, True).wait()
    normed_core(False).start()
    gather_core(True).wait()
    for i in range(8):
        block = ng[i // 4, i % 4].reshape(128, D).astype(F32)
        ngt[:, 128 * i : 128 * i + 128] = jnp.transpose(block).astype(BF)

    ex_dm.wait()
    back = unfold(dm_r[...].astype(F32), D).reshape(2, 64, D)
    parts = []
    for c in range(2):
        total = rounded(cot[c].astype(F32) + back[c])
        dmid[c] = total.astype(BF)
        parts.append((total * mod_s[2, c : c + 1, :]).astype(BF))
    scaled_s = jnp.concatenate(parts, axis=0)
    tokens = nt(scaled_s, wos[...]).reshape(2, 64, ATT)
    for c in range(2):
        for h in range(HEADS):
            part = tokens[c][:, HD * h : HD * h + HD].reshape(4, 16, HD)
            row = jnp.concatenate([part[j] for j in range(4)] + [zeros(16, 96)], axis=-1)
            c1_s[owner(c, h)] = row.astype(BF)
    ex_c1.start()

    ex_c2.wait()
    att_t = unfold(c2_r[...].astype(F32), ATT).reshape(128, ATT)
    xl[core, :, 0:640] = jnp.concatenate(spread_rows(att_t), axis=-1).astype(BF)
    for cc in range(2):
        xrv[cc, :, 640:1280] = core_columns(scaled_s.astype(F32), cc)
    xr[core] = xrv[core]

    def pair_copies(slot):
        there = {"patch": p + 1 - 2 * core}
        return [
            pltpu.make_async_remote_copy(
                src_ref=src,
                dst_ref=dst.at[slot],
                send_sem=xsem.at[0, i],
                recv_sem=xsem.at[1, i],
                device_id=there,
                device_id_type=MESH,
            )
            for i, (src, dst) in enumerate(((xl.at[core], xl), (xrv.at[1 - core], xr)))
        ]

    for copy in pair_copies(core):
        copy.start()

    for part in range(4):
        at = pl.ds(256 * part, 256)
        kt_b[:, at] = jnp.transpose(widen(k_b[at, :].astype(F32), 128)).astype(BF)
    normed_core(True).wait()
    ex_dt.wait()
    g = tn(xn[...].reshape(1024, D), dt_r[...].reshape(1024, 256)).reshape(4, 4, HD, 256)
    for yy in range(4):
        syq[yy] = g[:, yy].reshape(288, 256).astype(BF)
    ex_yq.start()
    for copy in pair_copies(1 - core):
        copy.wait()
    left = xl[...].reshape(256, 1280)
    right = xr[...].reshape(256, 1280)
    lt[0:640, :] = jnp.transpose(left[:, 0:640].astype(F32)).astype(BF)
    lt[640:1280, :] = jnp.transpose(right[:, 640:1280].astype(F32)).astype(BF)
    g = nn(lt[0:640, :], right[:, 0:640])
    for yy in range(4):
        syo[yy] = g[160 * yy : 160 * yy + 160].astype(BF)
    ex_yo.start()
    g = nn(lt[640:1280, :], left[:, 640:1280])
    for i in range(4):
        sxs[i] = g[144 * i : 144 * i + 144].astype(BF)
    ex_xs.start()
    ex_c1.wait()
    got_do = c1_r[...].astype(F32)
    parts = [got_do[:, :, HD * j : HD * j + HD] for j in range(4)]
    do_b[...] = jnp.stack(parts, axis=1).reshape(1024, HD).astype(BF)
    dk_f[...] = jnp.zeros_like(dk_f)
    dv_f[...] = jnp.zeros_like(dv_f)

    def attend_back(i, carry):
        at = pl.ds(pl.multiple_of(i * 256, 256), 256)
        qb, dob = q_b[at, :], do_b[at, :]
        e = jnp.exp(nt(k_b[...], qb) * SCALE)
        soft = e * (1.0 / jnp.sum(e, axis=0, keepdims=True))
        dv_f[...] += nn(soft.astype(BF), dob)
        dp = nt(v_b[...], dob)
        ds = (soft * (dp - jnp.sum(dp * soft, axis=0, keepdims=True)) * SCALE).astype(BF)
        dk_f[...] += nn(ds, qb)
        dq_f[at, :] = jnp.transpose(nn(kt_b[...], ds))[:, :HD]
        return carry

    lax.fori_loop(0, 4, attend_back, 0)
    for part in range(4):
        at = pl.ds(256 * part, 256)
        dq = head_back(rounded(dq_f[at, :]), q_b[at, :].astype(F32), rqk[at, 0:1])
        dk = head_back(rounded(dk_f[at, :]), k_b[at, :].astype(F32), rqk[at, 1:2])
        row = jnp.concatenate([dq, dk, dv_f[at, :], zeros(256, 8)], axis=-1)
        dg[4 * part : 4 * part + 4] = row.astype(BF).reshape(4, 64, 224)
        row = row.reshape(4, 4, 16, 224)
        row = jnp.concatenate([row[:, j].reshape(64, 224) for j in range(4)], axis=-1)
        d_s[4 * part : 4 * part + 4] = row.astype(BF).reshape(4, 16, 896)
    ex_d.start()

    ex_yq.wait()
    total = sum(ryq[i].astype(F32) for i in range(4))
    for i in range(8):
        zz, s = i % 4, i // 4
        part = total[HD * zz : HD * zz + HD, 128 * s : 128 * s + 128]
        szq[i] = jnp.concatenate([part, zeros(8, 128)], axis=0).astype(BF)
    ex_zq.start()

    blocks = [dg[4 * xx + 2 * s + cc] for cc in range(2) for xx in range(4) for s in range(2)]
    g = nn(ngt[...], jnp.concatenate(blocks, axis=0)).reshape(4, 4, HD, 224)
    for yy in range(4):
        gys[yy] = g[:, yy].reshape(288, 224).astype(BF)
    ex_gy.start()

    ex_yo.wait()
    total = sum(ryo[i].astype(F32) for i in range(4))
    for i in range(4):
        sxo[i] = widen(total[:, 144 * i : 144 * i + 144], 256).astype(BF)
    ex_xo.start()
    ex_xs.wait()
    total = sum(rxs[i].astype(F32) for i in range(4))
    for i in range(4):
        sys[i] = widen(total[:, 160 * i : 160 * i + 160], 256).astype(BF)
    ex_ys.start()

    ex_gy.wait()
    total = sum(gyr[i].astype(F32) for i in range(4)).reshape(4, 3, 24, 224)
    for b in range(6):
        cols = [total[:, r, :, 36 * b : 36 * b + 36] for r in range(3)] + [zeros(4, 24, 20)]
        cols = jnp.concatenate(cols, axis=-1)
        fs[:, b] = jnp.concatenate([cols, zeros(4, 8, 128)], axis=1).astype(BF)

    def piece(i, b):
        to_z = lax.rem(zl + i, 4)
        block = 16 * (b // 2) + 2 * head + b % 2
        to, slot = lax.div(block, 3), lax.rem(block, 3)
        copy = pltpu.make_async_remote_copy(
            src_ref=fs.at[to_z, b],
            dst_ref=fr.at[slot, z],
            send_sem=fs_sem.at[to_z, b],
            recv_sem=fr_sem.at[slot, z],
            device_id={"frame": 4 * to_z + y, "patch": to},
            device_id_type=MESH,
        )
        return to, slot, copy

    for i in range(4):
        for b in range(6):
            to, slot, copy = piece(i, b)
            if i > 0:
                copy.start()
            else:

                @pl.when(to != p)
                def _():
                    copy.start()

                @pl.when(to == p)
                def _():
                    fr[slot, z] = fs[zl, b]

    ex_xo.wait()
    ex_ys.wait()
    total = sum(rxo[i].astype(F32) for i in range(4))
    other = sum(rys[i].astype(F32) for i in range(4))
    other = jnp.transpose(jnp.concatenate([other, zeros(112, 256)], axis=0))
    for i in range(8):
        zz, s = i % 4, i // 4
        rows, cols = slice(40 * zz, 40 * zz + 40), slice(HD * s, HD * s + HD)
        part = jnp.concatenate([total[rows, cols], other[rows, cols]], axis=0)
        szo[i] = widen(part, 128).astype(BF)
    ex_zo.start()

    ex_d.wait()
    parts = []
    for c in range(2):
        blocks = [d_r[owner(c, h)].astype(F32) for h in range(HEADS)]
        for i in range(4):
            at = [224 * i + HD * j for j in range(3)]
            row = [b[:, a : a + HD] for a in at for b in blocks]
            parts.append(jnp.concatenate(row, axis=-1))
    dn = nn(jnp.concatenate(parts, axis=0).astype(BF), wqs[...])
    for c in range(2):
        xh, r = normalise(lat[c].astype(F32))
        back = normalise_back(dn[64 * c : 64 * c + 64], mod_s[1, c : c + 1, :], xh, r)
        gl[c] = (dmid[c].astype(F32) + back).astype(BF)


    ex_zq.wait()
    total = sum(rzq[i].astype(F32) for i in range(8))
    gqt[...] = total[:HD, :108]
    ex_zo.wait()
    total = sum(rzo[i].astype(F32) for i in range(8))
    got[...] = total[:36, :HD]
    gos[...] = total[40:76, :HD]

    for i in range(4):
        for b in range(6):
            to, slot, copy = piece(i, b)
            if i > 0:
                copy.wait_send()
            else:

                @pl.when(to != p)
                def _():
                    copy.wait_send()

    for slot in range(3):
        left = lax.rem(3 * p + slot, 16)
        source = lax.div(left, 4) * 4 + lax.rem(lax.div(left, 2), 2)
        for i in range(4):
            for c in range(2):
                from_z = lax.rem(zl + i, 4)
                at = 4 * c + from_z
                copy = pltpu.make_async_remote_copy(
                    src_ref=fs.at[0, 0],
                    dst_ref=fr.at[slot, at],
                    send_sem=fs_sem.at[0, 0],
                    recv_sem=fr_sem.at[slot, at],
                    device_id={"frame": 4 * from_z + y, "patch": source + 2 * c},
                    device_id_type=MESH,
                )
                if i > 0:
                    copy.wait_recv()
                else:

                    @pl.when(source + 2 * c != p)
                    def _():
                        copy.wait_recv()

    cols = []
    for slot in range(3):
        total = sum(fr[slot, i].astype(F32) for i in range(8))
        cols.append(
            jnp.concatenate([total[:24, 36 * r : 36 * r + 36] for r in range(3)], axis=0)
        )
    gqs[...] = jnp.concatenate(cols, axis=-1)


def hand_over(*refs):
    for src, dst in zip(refs[:5], refs[5:]):
        dst[...] = src[...]


def body(lat, mod_s, mod_t, wqs, wos, wqt, wot, cot):
    vmem = pl.BlockSpec(memory_space=pltpu.VMEM)
    hbm = pl.BlockSpec(memory_space=pl.ANY)
    dma = pltpu.SemaphoreType.DMA

    def buf(*shape):
        return pltpu.VMEM(shape, BF)

    def wide(*shape):
        return pltpu.VMEM(shape, F32)

    outs = pl.pallas_call(
        kernel,
        out_shape=(
            jax.ShapeDtypeStruct((2, 64, D), BF),
            jax.ShapeDtypeStruct((72, 108), F32),
            jax.ShapeDtypeStruct((36, 72), F32),
            jax.ShapeDtypeStruct((72, 108), F32),
            jax.ShapeDtypeStruct((36, 72), F32),
        ),
        in_specs=[vmem] * 4 + [hbm] * 4,
        out_specs=(vmem,) * 5,
        scratch_shapes=[
            buf(QKV, D), buf(ATT, D), buf(QKV, D), buf(ATT, D), dma((4,)),
            buf(2, 64, D), wide(128, QKV),
            buf(16, 16, 896), buf(16, 16, 896),
            buf(16, 16, 384), buf(16, 16, 384),
            buf(128, ATT), buf(2, 64, D), buf(2, 64, D),
            buf(16, 16, 640), buf(16, 16, 640),
            buf(16, 16, 384), buf(16, 16, 384),
            buf(16, 16, 384), buf(16, 16, 384),
            buf(16, 16, 384), buf(16, 16, 384),
            buf(16, 16, 640), buf(16, 16, 640),
            buf(16, 16, 896), buf(16, 16, 896), buf(16, 64, 224), buf(1152, 1024),
            dma((9, 2, 16)),
            buf(1024, HD), buf(1024, HD), buf(1024, HD), wide(1024, 2),
            buf(1024, HD), buf(128, 1024), wide(1024, HD), wide(1024, HD), wide(1024, HD),
            buf(2, 4, 2, 64, D), dma((2, 5)),
            buf(8, 128, D), dma((2, 4)), buf(8, 128, 256), buf(8, 128, 256), dma((2, 8)),
            buf(2, 128, 1280), buf(2, 128, 1280), buf(2, 128, 1280), dma((2, 2)),
            buf(1280, 256),
            buf(4, 288, 256), buf(4, 288, 256),
            buf(4, 160, 640), buf(4, 160, 640),
            buf(4, 160, 256), buf(4, 160, 256),
            buf(4, 144, 640), buf(4, 144, 640),
            buf(4, 144, 256), buf(4, 144, 256),
            buf(4, 288, 224), buf(4, 288, 224),
            dma((6, 2, 4)),
            buf(8, 80, 128), buf(8, 80, 128),
            buf(8, 80, 128), buf(8, 80, 128),
            dma((2, 2, 8)),
            buf(4, 6, 32, 128), buf(3, 8, 32, 128), dma((4, 6)), dma((3, 8)),
        ],
        compiler_params=pltpu.CompilerParams(
            collective_id=0, has_side_effects=True, vmem_limit_bytes=60 * 1024 * 1024
        ),
    )(
        lat.reshape(2, 64, D),
        cot.reshape(2, 64, D),
        mod_s.transpose(1, 0, 2),
        mod_t.transpose(1, 0, 2),
        wqs.T,
        wos,
        wqt.T,
        wot,
    )
    outs = pl.pallas_call(
        hand_over,
        out_shape=tuple(jax.ShapeDtypeStruct(o.shape, o.dtype) for o in outs),
        in_specs=[vmem] * 5,
        out_specs=(vmem,) * 5,
    )(*outs)
    return (outs[0].reshape(2, 1, 64, D),) + tuple(outs[1:])


def solution(mesh):
    tokens = P(None, "frame", "patch", None)
    return jax.shard_map(
        body,
        mesh=mesh,
        in_specs=(tokens,) + (P(),) * 6 + (tokens,),
        out_specs=(tokens,) + (P("frame", "patch"),) * 4,
        check_vma=False,
    )
```

```python
import jax
import jax.numpy as jnp
from jax import lax
from jax.experimental import pallas as pl
from jax.experimental.pallas import tpu as pltpu
from jax.sharding import PartitionSpec as P

F32 = jnp.float32
BF = jnp.bfloat16
MESH = pl.DeviceIdType.MESH
HD = 72
HEADS = 8
ATT = 576
D = 1152
QKV = 1728
EPS = 1e-06
SCALE = HD**-0.5
LOG2E = 1.4426950408889634


def nn(a, b):
    return lax.dot_general(a, b, (((1,), (0,)), ((), ())), preferred_element_type=F32)


def nt(a, b):
    return lax.dot_general(a, b, (((1,), (1,)), ((), ())), preferred_element_type=F32)


def tn(a, b):
    return lax.dot_general(a, b, (((0,), (0,)), ((), ())), preferred_element_type=F32)


def owner(c, h):
    return (h // 2) * 4 + c * 2 + h % 2


def normalise(x):
    centre = x - jnp.mean(x, axis=-1, keepdims=True)
    r = lax.rsqrt(jnp.mean(centre * centre, axis=-1, keepdims=True) + EPS)
    return centre * r, r


def normalise_back(dn, stretch, xh, r):
    dx = dn * (1.0 + stretch)
    dx = dx - xh * jnp.mean(dx * xh, axis=-1, keepdims=True)
    dx = r * dx
    return dx - jnp.mean(dx, axis=-1, keepdims=True)


def inverse_norm(x):
    return lax.rsqrt(jnp.sum(x * x, axis=-1, keepdims=True) * (1.0 / HD) + EPS)


def head_back(dy, y, r):
    return r * (dy - y * (jnp.sum(dy * y, axis=-1, keepdims=True) * (1.0 / HD)))


def rounded(x):
    return x.astype(BF).astype(F32)


def zeros(*shape):
    return jnp.zeros(shape, F32)


def fold(x, near):
    n, _, w = x.shape
    far = x[:, :, near:]
    pad = 2 * near - w
    far = jnp.concatenate([far, zeros(n, 8, pad)], axis=-1)
    return jnp.concatenate([x[:, :, :near], far], axis=1)


def unfold(x, w):
    near = x.shape[-1]
    return jnp.concatenate([x[:, :8, :], x[:, 8:, : w - near]], axis=-1)


def widen(x, width):
    return jnp.concatenate([x, zeros(x.shape[0], width - x.shape[1])], axis=-1)


class Exchange:
    def __init__(self, send, recv, ssem, rsem, n, me, place):
        self.send, self.recv, self.ssem, self.rsem = send, recv, ssem, rsem
        self.n, self.me, self.place = n, me, place

    def copy(self, to, slot):
        return pltpu.make_async_remote_copy(
            src_ref=self.send.at[to],
            dst_ref=self.recv.at[slot],
            send_sem=self.ssem,
            recv_sem=self.rsem,
            device_id=self.place(to),
            device_id_type=MESH,
        )

    def start(self):
        def step(i, carry):
            self.copy(lax.rem(self.me + i, self.n), self.me).start()
            return carry

        lax.fori_loop(1, self.n, step, 0)
        self.recv[self.me] = self.send[self.me]

    def wait(self):
        for ref, sem in ((self.send, self.ssem), (self.recv, self.rsem)):
            blocks = ref.at[pl.ds(0, self.n - 1)]
            pltpu.make_async_copy(blocks, blocks, sem).wait()


def kernel(
    lat_h, cot_h, mod_s_h, mod_t_h, wqs_h, wos_h, wqt_h, wot_h,
    gl_h, gqs_h, gos_h, gqt_h, got_h,
    lat, cot, mod_s, mod_t, gl, gqs, gos, gqt, got, iosem,
    wqs, wos, wqt, wot, wsem,
    normed, proj,
    a_s, a_r, b1_s, b1_r, att_s, scaled, dmid, t1_s, t1_r, t2_s, t2_r,
    c2_s, c2_r, c1_s, c1_r, dm_s, dm_r, d_s, d_r, dg, ngt, xsems,
    q_b, k_b, v_b, rqk, rl, rrow, do_b, kt_b, dq_f, dk_f, dv_f,
    ng, ngsem, xn, xnsem, dt_s, dt_r, dtsem,
    xl, xrv, xr, xsem, lt,
    syq, ryq, syo, ryo, sxo, rxo, sxs, rxs, sys, rys, gys, gyr, sem4,
    szq, rzq, szo, rzo, sem8,
    fs, fr, fs_sem, fr_sem,
):
    f = lax.axis_index("frame")
    p = lax.axis_index("patch")
    core = lax.rem(p, 2)
    zh = lax.rem(lax.div(p, 2), 2)
    x = lax.div(p, 4)
    y = lax.rem(f, 4)
    zl = lax.div(f, 4)
    head = 2 * x + core
    clip_t = lax.div(f, 8)
    z = zh * 4 + zl

    loads = [
        pltpu.make_async_copy(src, dst, wsem.at[i])
        for i, (src, dst) in enumerate(
            ((wqs_h, wqs), (wot_h, wot), (wos_h, wos), (wqt_h, wqt))
        )
    ]
    reads = [
        pltpu.make_async_copy(src, dst, iosem.at[i])
        for i, (src, dst) in enumerate(
            ((lat_h, lat), (mod_s_h, mod_s), (cot_h, cot), (mod_t_h, mod_t))
        )
    ]
    writes = [
        pltpu.make_async_copy(src, dst, iosem.at[4 + i])
        for i, (src, dst) in enumerate(
            ((gl, gl_h), (gqt, gqt_h), (got, got_h), (gos, gos_h), (gqs, gqs_h))
        )
    ]
    for read in reads[:2]:
        read.start()
    loads[0].start()
    for read in reads[2:]:
        read.start()

    barrier = pltpu.get_barrier_semaphore()

    def greet(i, carry):
        pl.semaphore_signal(
            barrier, inc=1, device_id={"frame": lax.rem(f + i, 16)}, device_id_type=MESH
        )
        pl.semaphore_signal(
            barrier, inc=1, device_id={"patch": lax.rem(p + i, 16)}, device_id_type=MESH
        )
        return carry

    lax.fori_loop(1, 16, greet, 0)

    def greet_far(i, carry):
        pl.semaphore_signal(
            barrier,
            inc=1,
            device_id={
                "frame": 4 * lax.rem(zl + 1 + lax.div(i, 15), 4) + y,
                "patch": lax.rem(p + 1 + lax.rem(i, 15), 16),
            },
            device_id_type=MESH,
        )
        return carry

    lax.fori_loop(0, 45, greet_far, 0)

    def on_patch(i):
        return {"patch": i}

    def on_frame(i):
        return {"frame": i}

    def on_x(i):
        return {"patch": 4 * i + 2 * zh + core}

    def on_y(i):
        return {"frame": 4 * zl + i}

    def on_column(i):
        return {"patch": 4 * lax.rem(i, 4) + 2 * zh + lax.div(i, 4)}

    def on_z(i):
        return {
            "frame": 4 * lax.rem(i, 4) + y,
            "patch": 4 * x + 2 * lax.div(i, 4) + core,
        }

    ex_a = Exchange(a_s, a_r, xsems.at[0, 0], xsems.at[0, 1], 16, p, on_patch)
    ex_b1 = Exchange(b1_s, b1_r, xsems.at[1, 0], xsems.at[1, 1], 16, p, on_patch)
    ex_t1 = Exchange(t1_s, t1_r, xsems.at[3, 0], xsems.at[3, 1], 16, f, on_frame)
    ex_t2 = Exchange(t2_s, t2_r, xsems.at[4, 0], xsems.at[4, 1], 16, f, on_frame)
    ex_c2 = Exchange(c2_s, c2_r, xsems.at[5, 0], xsems.at[5, 1], 16, f, on_frame)
    ex_c1 = Exchange(c1_s, c1_r, xsems.at[6, 0], xsems.at[6, 1], 16, p, on_patch)
    ex_dm = Exchange(dm_s, dm_r, xsems.at[7, 0], xsems.at[7, 1], 16, f, on_frame)
    ex_d = Exchange(d_s, d_r, xsems.at[8, 0], xsems.at[8, 1], 16, p, on_patch)
    ex_dt = Exchange(dt_s, dt_r, dtsem.at[0], dtsem.at[1], 8, 4 * core + x, on_column)
    ex_yq = Exchange(syq, ryq, sem4.at[0, 0], sem4.at[0, 1], 4, y, on_y)
    ex_yo = Exchange(syo, ryo, sem4.at[1, 0], sem4.at[1, 1], 4, y, on_y)
    ex_xo = Exchange(sxo, rxo, sem4.at[2, 0], sem4.at[2, 1], 4, x, on_x)
    ex_xs = Exchange(sxs, rxs, sem4.at[4, 0], sem4.at[4, 1], 4, x, on_x)
    ex_ys = Exchange(sys, rys, sem4.at[5, 0], sem4.at[5, 1], 4, y, on_y)
    ex_gy = Exchange(gys, gyr, sem4.at[3, 0], sem4.at[3, 1], 4, y, on_y)
    ex_zq = Exchange(szq, rzq, sem8.at[0, 0], sem8.at[0, 1], 8, z, on_z)
    ex_zo = Exchange(szo, rzo, sem8.at[1, 0], sem8.at[1, 1], 8, z, on_z)

    reads[0].wait()
    reads[1].wait()
    for c in range(2):
        xh, _ = normalise(lat[c].astype(F32))
        normed[c] = (xh * (1.0 + mod_s[1, c : c + 1, :]) + mod_s[0, c : c + 1, :]).astype(BF)
    loads[0].wait()
    for load in loads[1:]:
        load.start()
    proj[...] = nt(normed[...].reshape(128, D), wqs[...])
    lane = lax.broadcasted_iota(jnp.int32, (128, 224), 1)
    for h in range(HEADS):
        q = proj[:, HD * h : HD * h + HD]
        k = proj[:, ATT + HD * h : ATT + HD * h + HD]
        v = proj[:, 2 * ATT + HD * h : 2 * ATT + HD * h + HD]
        rq = inverse_norm(q)
        rk = inverse_norm(k)
        row = jnp.concatenate([q * rq, k * rk, v, zeros(128, 8)], axis=-1)
        row = jnp.where(lane == 216, rq, row)
        row = jnp.where(lane == 217, rq - rounded(rq), row)
        row = jnp.where(lane == 218, rk, row)
        row = jnp.where(lane == 219, rk - rounded(rk), row)
        row = row.reshape(2, 4, 16, 224)
        for c in range(2):
            quarters = [row[c, j] for j in range(4)]
            a_s[owner(c, h)] = jnp.concatenate(quarters, axis=-1).astype(BF)
    pl.semaphore_wait(barrier, 75)
    ex_a.start()

    reads[2].wait()
    reads[3].wait()
    loads[1].wait()
    for c in range(2):
        scaled[c] = (cot[c].astype(F32) * mod_t[2, c : c + 1, :]).astype(BF)
    dout = nt(scaled[...].reshape(128, D), wot[...])
    for c in range(2):
        part = dout[64 * c : 64 * c + 64].reshape(8, 8, ATT)
        t2_s[8 * c : 8 * c + 8] = fold(part, 384).astype(BF)
    ng[core, x, zh] = normed[zh]
    gather_z = pltpu.make_async_remote_copy(
        src_ref=normed.at[1 - zh],
        dst_ref=ng.at[core, x, zh],
        send_sem=ngsem.at[0, 0],
        recv_sem=ngsem.at[1, 0],
        device_id={"patch": 4 * x + 2 * (1 - zh) + core},
        device_id_type=MESH,
    )
    ex_a.wait()
    gather_z.start()

    for part in range(4):
        rows = a_r[4 * part : 4 * part + 4].astype(F32)
        rows = [rows[:, :, 224 * j : 224 * j + 224] for j in range(4)]
        rows = jnp.stack(rows, axis=1).reshape(256, 224)
        at = pl.ds(256 * part, 256)
        q_b[at, :] = rows[:, 0:HD].astype(BF)
        k_b[at, :] = rows[:, HD : 2 * HD].astype(BF)
        v_b[at, :] = rows[:, 2 * HD : 3 * HD].astype(BF)
        rqk[at, 0:1] = rows[:, 216:217] + rows[:, 217:218]
        rqk[at, 1:2] = rows[:, 218:219] + rows[:, 219:220]

    def attend(i, carry):
        part = lax.rem(x + 1 + i, 4)
        at = pl.ds(pl.multiple_of(part * 256, 256), 256)
        e = jnp.exp2(nt(q_b[at, :], k_b[...]) * (SCALE * LOG2E))
        r = 1.0 / jnp.sum(e, axis=-1, keepdims=True)
        rl[at, :] = r
        pieces = (nn(e.astype(BF), v_b[...]) * r).reshape(4, 4, 16, HD)
        row = [pieces[:, j].reshape(64, HD) for j in range(4)] + [zeros(64, 96)]
        row = jnp.concatenate(row, axis=-1).astype(BF).reshape(4, 16, 384)
        b1_s[pl.ds(4 * part, 4)] = row
        for j in range(4):
            to = 4 * part + j

            @pl.when(to != p)
            def _():
                ex_b1.copy(to, p).start()

        return carry

    lax.fori_loop(0, 4, attend, 0)
    b1_r[p] = b1_s[p]
    ex_t2.start()
    for part in range(4):
        at = pl.ds(256 * part, 256)
        rrow[:, at] = jnp.transpose(widen(rl[at, :], 128))[0:1, :]
    loads[2].wait()
    ex_b1.wait()
    atts = []
    for c in range(2):
        blocks = [b1_r[owner(c, h)].astype(F32) for h in range(HEADS)]
        rows = [
            jnp.concatenate([b[:, HD * j : HD * j + HD] for b in blocks], axis=-1)
            for j in range(4)
        ]
        atts.append(jnp.concatenate(rows, axis=0))
    att_s[...] = jnp.concatenate(atts, axis=0).astype(BF)
    added = nn(att_s[...], wos[...])
    for c in range(2):
        middle = lat[c].astype(F32) + mod_s[2, c : c + 1, :] * added[64 * c : 64 * c + 64]
        t1_s[8 * c : 8 * c + 8] = fold(middle.reshape(8, 8, D), 640).astype(BF)
    ex_t1.start()

    gather_z.wait()

    def gather_x(i, back):
        block = lax.rem(x + 4 - i, 4) if back else x
        return pltpu.make_async_remote_copy(
            src_ref=ng.at[core, block],
            dst_ref=ng.at[core, block],
            send_sem=ngsem.at[0, i],
            recv_sem=ngsem.at[1, i],
            device_id=on_x(lax.rem(x + i, 4)),
            device_id_type=MESH,
        )

    def gather_core(back):
        side = 1 - core if back else core
        return pltpu.make_async_remote_copy(
            src_ref=ng.at[side],
            dst_ref=ng.at[side],
            send_sem=ngsem.at[0, 4],
            recv_sem=ngsem.at[1, 4],
            device_id={"patch": p + 1 - 2 * core},
            device_id_type=MESH,
        )

    for i in range(1, 4):
        gather_x(i, False).start()

    def pick(ref, i):
        return jnp.where(clip_t == 0, ref[i, 0:1, :], ref[i, 1:2, :])

    shift_t, stretch_t = pick(mod_t, 0), pick(mod_t, 1)

    def spread_rows(a):
        parts = []
        for yy in range(4):
            for zz in range(4):
                at = 36 * (4 * zz + yy)
                parts += [a[:, at : at + 36], zeros(128, 4)]
        return parts

    def core_columns(full, cc):
        parts = [full[:, HD * (2 * b + cc) : HD * (2 * b + cc) + HD] for b in range(8)]
        return jnp.concatenate(parts + [zeros(128, 64)], axis=-1).astype(BF)

    xl[1, core] = jnp.concatenate(spread_rows(att_s[...].astype(F32)), axis=-1).astype(BF)
    for cc in range(2):
        xrv[0, cc] = core_columns(scaled[...].reshape(128, D).astype(F32), cc)
    xr[0, core] = xrv[0, core]

    def pair_copies(which, slot):
        there = {"patch": p + 1 - 2 * core}
        pairs = ((xl.at[which, core], xl), (xrv.at[which, 1 - core], xr))
        return [
            pltpu.make_async_remote_copy(
                src_ref=src,
                dst_ref=dst.at[which, slot],
                send_sem=xsem.at[0, 2 * which + i],
                recv_sem=xsem.at[1, 2 * which + i],
                device_id=there,
                device_id_type=MESH,
            )
            for i, (src, dst) in enumerate(pairs)
        ]

    for part in range(4):
        at = pl.ds(256 * part, 256)
        kt_b[:, at] = jnp.transpose(widen(k_b[at, :].astype(F32), 128)).astype(BF)
    loads[3].wait()
    ex_t1.wait()
    middle = unfold(t1_r[...].astype(F32), D).reshape(128, D)
    xh_t, r_t = normalise(middle)
    normed_t = (xh_t * (1.0 + stretch_t) + shift_t).astype(BF)
    xn[4 * core + x] = normed_t

    def normed_x(i, back):
        block = 4 * core + (lax.rem(x + 4 - i, 4) if back else x)
        return pltpu.make_async_remote_copy(
            src_ref=xn.at[block],
            dst_ref=xn.at[block],
            send_sem=xnsem.at[0, i],
            recv_sem=xnsem.at[1, i],
            device_id=on_x(lax.rem(x + i, 4)),
            device_id_type=MESH,
        )

    def normed_core(back):
        side = pl.ds(4 * (1 - core if back else core), 4)
        return pltpu.make_async_remote_copy(
            src_ref=xn.at[side],
            dst_ref=xn.at[side],
            send_sem=xnsem.at[0, 0],
            recv_sem=xnsem.at[1, 0],
            device_id={"patch": p + 1 - 2 * core},
            device_id_type=MESH,
        )

    for i in range(1, 4):
        normed_x(i, False).start()
    proj[...] = nt(normed_t, wqt[...])
    same = lax.rem(lax.broadcasted_iota(jnp.int32, (128, 128), 0), 8) == lax.rem(
        lax.broadcasted_iota(jnp.int32, (128, 128), 1), 8
    )
    heads, att_parts, dq_parts, dk_parts, dv_parts = [], [], [], [], []
    for h in range(HEADS):
        q = proj[:, HD * h : HD * h + HD]
        k = proj[:, ATT + HD * h : ATT + HD * h + HD]
        v = proj[:, 2 * ATT + HD * h : 2 * ATT + HD * h + HD].astype(BF)
        rq = inverse_norm(q)
        rk = inverse_norm(k)
        q = q * rq
        k = k * rk
        e = jnp.where(same, jnp.exp(nt(q.astype(BF), k.astype(BF)) * SCALE), 0.0)
        soft = e * (1.0 / jnp.sum(e, axis=-1, keepdims=True))
        att_parts.append(nn(soft.astype(BF), v))
        heads.append((q, k, v, rq, rk, soft))
    att_t = jnp.concatenate(att_parts, axis=-1)
    c2_s[...] = fold(att_t.reshape(16, 8, ATT), 384).astype(BF)
    ex_c2.start()
    ex_t2.wait()
    dout_t = unfold(t2_r[...].astype(F32), ATT).reshape(128, ATT)
    for h, (q, k, v, rq, rk, soft) in enumerate(heads):
        do = dout_t[:, HD * h : HD * h + HD].astype(BF)
        dp = nt(do, v)
        ds = (soft * (dp - jnp.sum(dp * soft, axis=-1, keepdims=True)) * SCALE).astype(BF)
        dq_parts.append(head_back(rounded(nn(ds, k.astype(BF))), q, rq))
        dk_parts.append(head_back(rounded(tn(ds, q.astype(BF))), k, rk))
        dv_parts.append(tn(soft.astype(BF), do))
    dproj_t = jnp.concatenate(dq_parts + dk_parts + dv_parts, axis=-1)
    dn = nn(dproj_t.astype(BF), wqt[...])
    back = normalise_back(dn, stretch_t, xh_t, r_t)
    dm_s[...] = fold(back.reshape(16, 8, D), 640).astype(BF)
    ex_dm.start()

    for cc in range(2):
        for xx in range(4):
            at = 108 * (4 * xx + cc)
            row = [dproj_t[:, at : at + 108], zeros(128, 20)]
            row += [dproj_t[:, at + 216 : at + 324], zeros(128, 20)]
            dt_s[4 * cc + xx] = jnp.concatenate(row, axis=-1).astype(BF)
    ex_dt.start()

    ex_c2.wait()
    att_t = unfold(c2_r[...].astype(F32), ATT).reshape(128, ATT)
    xl[0, core] = jnp.concatenate(spread_rows(att_t), axis=-1).astype(BF)
    for copy in pair_copies(0, core):
        copy.start()
    for i in range(1, 4):
        gather_x(i, True).wait()
    gather_core(False).start()
    for copy in pair_copies(0, 1 - core):
        copy.wait()
    lt[...] = jnp.transpose(xl[0].reshape(256, 640).astype(F32)).astype(BF)
    g = nn(lt[...], xr[0].reshape(256, 640))
    for yy in range(4):
        syo[yy] = g[160 * yy : 160 * yy + 160].astype(BF)
    ex_yo.start()
    gather_core(True).wait()
    for i in range(8):
        block = ng[i // 4, i % 4].reshape(128, D).astype(F32)
        ngt[:, 128 * i : 128 * i + 128] = jnp.transpose(block).astype(BF)

    ex_dm.wait()
    back = unfold(dm_r[...].astype(F32), D).reshape(2, 64, D)
    parts = []
    for c in range(2):
        total = rounded(cot[c].astype(F32) + back[c])
        dmid[c] = total.astype(BF)
        parts.append((total * mod_s[2, c : c + 1, :]).astype(BF))
    scaled_s = jnp.concatenate(parts, axis=0)
    tokens = nt(scaled_s, wos[...]).reshape(2, 64, ATT)
    for c in range(2):
        for h in range(HEADS):
            part = tokens[c][:, HD * h : HD * h + HD].reshape(4, 16, HD)
            row = jnp.concatenate([part[j] for j in range(4)] + [zeros(16, 96)], axis=-1)
            c1_s[owner(c, h)] = row.astype(BF)
    ex_c1.start()

    for cc in range(2):
        xrv[1, cc] = core_columns(scaled_s.astype(F32), cc)
    xr[1, core] = xrv[1, core]
    for copy in pair_copies(1, core):
        copy.start()
    for i in range(1, 4):
        normed_x(i, True).wait()
    normed_core(False).start()
    for copy in pair_copies(1, 1 - core):
        copy.wait()
    lt[...] = jnp.transpose(xr[1].reshape(256, 640).astype(F32)).astype(BF)
    g = nn(lt[...], xl[1].reshape(256, 640))
    for i in range(4):
        sxs[i] = g[144 * i : 144 * i + 144].astype(BF)
    ex_xs.start()
    normed_core(True).wait()
    ex_dt.wait()
    g = tn(xn[...].reshape(1024, D), dt_r[...].reshape(1024, 256)).reshape(4, 4, HD, 256)
    for yy in range(4):
        syq[yy] = g[:, yy].reshape(288, 256).astype(BF)
    ex_yq.start()
    ex_yo.wait()
    total = sum(ryo[i].astype(F32) for i in range(4))
    for i in range(4):
        sxo[i] = widen(total[:, 144 * i : 144 * i + 144], 256).astype(BF)
    ex_xo.start()
    ex_c1.wait()
    got_do = c1_r[...].astype(F32)
    parts = [got_do[:, :, HD * j : HD * j + HD] for j in range(4)]
    do_b[...] = (jnp.stack(parts, axis=1).reshape(1024, HD) * rl[...]).astype(BF)
    dk_f[...] = jnp.zeros_like(dk_f)
    dv_f[...] = jnp.zeros_like(dv_f)

    def attend_back(i, carry):
        at = pl.ds(pl.multiple_of(i * 256, 256), 256)
        qb, dob = q_b[at, :], do_b[at, :]
        e = jnp.exp2(nt(k_b[...], qb) * (SCALE * LOG2E))
        dp = nt(v_b[...], dob)
        shift = rrow[:, at] * jnp.sum(dp * e, axis=0, keepdims=True)
        ds = (e * (dp - shift)).astype(BF)
        dv_f[...] += nn(e.astype(BF), dob)
        dk_f[...] += nn(ds, qb)
        dq_f[at, :] = jnp.transpose(nn(kt_b[...], ds))[:, :HD]
        return carry

    lax.fori_loop(0, 4, attend_back, 0)
    for part in range(4):
        at = pl.ds(256 * part, 256)
        dq = head_back(rounded(dq_f[at, :] * SCALE), q_b[at, :].astype(F32), rqk[at, 0:1])
        dk = head_back(rounded(dk_f[at, :] * SCALE), k_b[at, :].astype(F32), rqk[at, 1:2])
        row = jnp.concatenate([dq, dk, dv_f[at, :], zeros(256, 8)], axis=-1)
        dg[4 * part : 4 * part + 4] = row.astype(BF).reshape(4, 64, 224)
        row = row.reshape(4, 4, 16, 224)
        row = jnp.concatenate([row[:, j].reshape(64, 224) for j in range(4)], axis=-1)
        d_s[4 * part : 4 * part + 4] = row.astype(BF).reshape(4, 16, 896)
    ex_d.start()
    ex_xs.wait()
    total = sum(rxs[i].astype(F32) for i in range(4))
    for i in range(4):
        sys[i] = widen(total[:, 160 * i : 160 * i + 160], 256).astype(BF)
    ex_ys.start()

    blocks = [dg[4 * xx + 2 * s + cc] for cc in range(2) for xx in range(4) for s in range(2)]
    g = nn(ngt[...], jnp.concatenate(blocks, axis=0)).reshape(4, 4, HD, 224)
    for yy in range(4):
        gys[yy] = g[:, yy].reshape(288, 224).astype(BF)
    ex_gy.start()
    ex_yq.wait()
    total = sum(ryq[i].astype(F32) for i in range(4))
    for i in range(8):
        zz, s = i % 4, i // 4
        part = total[HD * zz : HD * zz + HD, 128 * s : 128 * s + 108]
        rest = [part[64:, 18 * j : 18 * j + 18] for j in range(6)] + [zeros(16, 18)]
        rest = jnp.concatenate(rest, axis=0)
        szq[i] = jnp.concatenate([part[:64], rest, zeros(64, 2)], axis=-1).astype(BF)
    ex_zq.start()


    ex_xo.wait()
    ex_ys.wait()
    total = sum(rxo[i].astype(F32) for i in range(4))
    other = sum(rys[i].astype(F32) for i in range(4))
    other = jnp.transpose(jnp.concatenate([other, zeros(112, 256)], axis=0))
    for i in range(8):
        zz, s = i % 4, i // 4
        rows, cols = slice(40 * zz, 40 * zz + 36), slice(HD * s, HD * s + HD)
        part = jnp.concatenate([total[rows, cols], other[rows, cols]], axis=0)
        rest = jnp.concatenate([part[48:, :36], part[48:, 36:]], axis=0)
        szo[i] = jnp.concatenate([part[:48], rest, zeros(48, 20)], axis=-1).astype(BF)
    ex_zo.start()

    ex_gy.wait()
    total = sum(gyr[i].astype(F32) for i in range(4)).reshape(4, 3, 24, 224)
    for b in range(6):
        cols = [total[:, r, :, 36 * b : 36 * b + 36] for r in range(3)] + [zeros(4, 24, 20)]
        cols = jnp.concatenate(cols, axis=-1)
        fs[:, b] = jnp.concatenate([cols, zeros(4, 8, 128)], axis=1).astype(BF)

    def piece(i, b):
        to_z = lax.rem(zl + i, 4)
        block = 16 * (b // 2) + 2 * head + b % 2
        to, slot = lax.div(block, 3), lax.rem(block, 3)
        copy = pltpu.make_async_remote_copy(
            src_ref=fs.at[to_z, b],
            dst_ref=fr.at[slot, z],
            send_sem=fs_sem.at[b if i == 0 else 6],
            recv_sem=fr_sem.at[2 * slot + zh if i == 0 else 6],
            device_id={"frame": 4 * to_z + y, "patch": to},
            device_id_type=MESH,
        )
        return to, slot, copy

    for i in range(4):
        for b in range(6):
            to, slot, copy = piece(i, b)
            if i > 0:
                copy.start()
            else:

                @pl.when(to != p)
                def _():
                    copy.start()

                @pl.when(to == p)
                def _():
                    fr[slot, z] = fs[zl, b]

    ex_d.wait()
    parts = []
    for c in range(2):
        blocks = [d_r[owner(c, h)].astype(F32) for h in range(HEADS)]
        for i in range(4):
            at = [224 * i + HD * j for j in range(3)]
            row = [b[:, a : a + HD] for a in at for b in blocks]
            parts.append(jnp.concatenate(row, axis=-1))
    dn = nn(jnp.concatenate(parts, axis=0).astype(BF), wqs[...])
    for c in range(2):
        xh, r = normalise(lat[c].astype(F32))
        back = normalise_back(dn[64 * c : 64 * c + 64], mod_s[1, c : c + 1, :], xh, r)
        gl[c] = (dmid[c].astype(F32) + back).astype(BF)
    writes[0].start()


    ex_zq.wait()
    total = sum(rzq[i].astype(F32) for i in range(8))
    rest = [total[8 * j : 8 * j + 8, 108:126] for j in range(6)]
    rest = jnp.concatenate(rest, axis=-1)
    gqt[...] = jnp.concatenate([total[:, :108], rest], axis=0)
    writes[1].start()
    ex_zo.wait()
    total = sum(rzo[i].astype(F32) for i in range(8))
    rest = jnp.concatenate([total[:24, 72:108], total[24:, 72:108]], axis=-1)
    total = jnp.concatenate([total[:, :HD], rest], axis=0)
    got[...] = total[:36]
    gos[...] = total[36:]
    writes[2].start()
    writes[3].start()

    for b in range(6):
        to, slot, copy = piece(0, b)

        @pl.when(to != p)
        def _():
            copy.wait_send()

    for slot in range(3):
        left = lax.rem(3 * p + slot, 16)
        source = lax.div(left, 4) * 4 + lax.rem(lax.div(left, 2), 2)
        for c in range(2):
            at = 4 * c + zl
            copy = pltpu.make_async_remote_copy(
                src_ref=fs.at[0, 0],
                dst_ref=fr.at[slot, at],
                send_sem=fs_sem.at[0],
                recv_sem=fr_sem.at[2 * slot + c],
                device_id={"patch": source + 2 * c},
                device_id_type=MESH,
            )

            @pl.when(source + 2 * c != p)
            def _():
                copy.wait_recv()

    for ref, sem in ((fs.at[pl.ds(0, 3)], fs_sem.at[6]), (fr.at[:, pl.ds(0, 6)], fr_sem.at[6])):
        pltpu.make_async_copy(ref, ref, sem).wait()

    cols = []
    for slot in range(3):
        total = sum(fr[slot, i].astype(F32) for i in range(8))
        cols.append(
            jnp.concatenate([total[:24, 36 * r : 36 * r + 36] for r in range(3)], axis=0)
        )
    gqs[...] = jnp.concatenate(cols, axis=-1)
    writes[4].start()
    for write in writes:
        write.wait()


def hand_over(*refs):
    for src, dst in zip(refs[:5], refs[5:]):
        dst[...] = src[...]


def body(lat, mod_s, mod_t, wqs, wos, wqt, wot, cot):
    vmem = pl.BlockSpec(memory_space=pltpu.VMEM)
    hbm = pl.BlockSpec(memory_space=pl.ANY)
    dma = pltpu.SemaphoreType.DMA

    def buf(*shape):
        return pltpu.VMEM(shape, BF)

    def wide(*shape):
        return pltpu.VMEM(shape, F32)

    outs = pl.pallas_call(
        kernel,
        out_shape=(
            jax.ShapeDtypeStruct((2, 64, D), BF),
            jax.ShapeDtypeStruct((72, 108), F32),
            jax.ShapeDtypeStruct((36, 72), F32),
            jax.ShapeDtypeStruct((72, 108), F32),
            jax.ShapeDtypeStruct((36, 72), F32),
        ),
        in_specs=[hbm] * 8,
        out_specs=(hbm,) * 5,
        scratch_shapes=[
            buf(2, 64, D), buf(2, 64, D), wide(3, 2, D), wide(3, 2, D),
            buf(2, 64, D), wide(72, 108), wide(36, 72), wide(72, 108), wide(36, 72), dma((9,)),
            buf(QKV, D), buf(ATT, D), buf(QKV, D), buf(ATT, D), dma((4,)),
            buf(2, 64, D), wide(128, QKV),
            buf(16, 16, 896), buf(16, 16, 896),
            buf(16, 16, 384), buf(16, 16, 384),
            buf(128, ATT), buf(2, 64, D), buf(2, 64, D),
            buf(16, 16, 640), buf(16, 16, 640),
            buf(16, 16, 384), buf(16, 16, 384),
            buf(16, 16, 384), buf(16, 16, 384),
            buf(16, 16, 384), buf(16, 16, 384),
            buf(16, 16, 640), buf(16, 16, 640),
            buf(16, 16, 896), buf(16, 16, 896), buf(16, 64, 224), buf(1152, 1024),
            dma((9, 2)),
            buf(1024, HD), buf(1024, HD), buf(1024, HD), wide(1024, 2), wide(1024, 1), wide(1, 1024),
            buf(1024, HD), buf(128, 1024), wide(1024, HD), wide(1024, HD), wide(1024, HD),
            buf(2, 4, 2, 64, D), dma((2, 5)),
            buf(8, 128, D), dma((2, 4)), buf(8, 128, 256), buf(8, 128, 256), dma((2,)),
            buf(2, 2, 128, 640), buf(2, 2, 128, 640), buf(2, 2, 128, 640), dma((2, 4)),
            buf(640, 256),
            buf(4, 288, 256), buf(4, 288, 256),
            buf(4, 160, 640), buf(4, 160, 640),
            buf(4, 160, 256), buf(4, 160, 256),
            buf(4, 144, 640), buf(4, 144, 640),
            buf(4, 144, 256), buf(4, 144, 256),
            buf(4, 288, 224), buf(4, 288, 224),
            dma((6, 2)),
            buf(8, 64, 128), buf(8, 64, 128),
            buf(8, 48, 128), buf(8, 48, 128),
            dma((2, 2)),
            buf(4, 6, 32, 128), buf(3, 8, 32, 128), dma((7,)), dma((7,)),
        ],
        compiler_params=pltpu.CompilerParams(
            collective_id=0, has_side_effects=True, vmem_limit_bytes=60 * 1024 * 1024
        ),
    )(
        lat.reshape(2, 64, D),
        cot.reshape(2, 64, D),
        mod_s.transpose(1, 0, 2),
        mod_t.transpose(1, 0, 2),
        wqs.T,
        wos,
        wqt.T,
        wot,
    )
    outs = pl.pallas_call(
        hand_over,
        out_shape=tuple(jax.ShapeDtypeStruct(o.shape, o.dtype) for o in outs),
        in_specs=[vmem] * 5,
        out_specs=(vmem,) * 5,
    )(*outs)
    return (outs[0].reshape(2, 1, 64, D),) + tuple(outs[1:])


def solution(mesh):
    tokens = P(None, "frame", "patch", None)
    return jax.shard_map(
        body,
        mesh=mesh,
        in_specs=(tokens,) + (P(),) * 6 + (tokens,),
        out_specs=(tokens,) + (P("frame", "patch"),) * 4,
        check_vma=False,
    )
```

```python
import jax
import jax.numpy as jnp
from jax import lax
from jax.experimental import pallas as pl
from jax.experimental.pallas import tpu as pltpu
from jax.sharding import PartitionSpec as P

F32 = jnp.float32
BF = jnp.bfloat16
MESH = pl.DeviceIdType.MESH
HD = 72
HEADS = 8
ATT = 576
D = 1152
QKV = 1728
EPS = 1e-06
SCALE = HD**-0.5
LOG2E = 1.4426950408889634


def nn(a, b):
    return lax.dot_general(a, b, (((1,), (0,)), ((), ())), preferred_element_type=F32)


def nt(a, b):
    return lax.dot_general(a, b, (((1,), (1,)), ((), ())), preferred_element_type=F32)


def tn(a, b):
    return lax.dot_general(a, b, (((0,), (0,)), ((), ())), preferred_element_type=F32)


def owner(c, h):
    return (h // 2) * 4 + c * 2 + h % 2


def normalise(x):
    centre = x - jnp.mean(x, axis=-1, keepdims=True)
    r = lax.rsqrt(jnp.mean(centre * centre, axis=-1, keepdims=True) + EPS)
    return centre * r, r


def normalise_back(dn, stretch, xh, r):
    dx = dn * (1.0 + stretch)
    dx = dx - xh * jnp.mean(dx * xh, axis=-1, keepdims=True)
    dx = r * dx
    return dx - jnp.mean(dx, axis=-1, keepdims=True)


def inverse_norm(x):
    return lax.rsqrt(jnp.sum(x * x, axis=-1, keepdims=True) * (1.0 / HD) + EPS)


def head_back(dy, y, r):
    return r * (dy - y * (jnp.sum(dy * y, axis=-1, keepdims=True) * (1.0 / HD)))


def rounded(x):
    return x.astype(BF).astype(F32)


def zeros(*shape, dtype=F32):
    return jnp.zeros(shape, dtype)


def fold(x, near):
    n, _, w = x.shape
    far = x[:, :, near:]
    pad = 2 * near - w
    far = jnp.concatenate([far, zeros(n, 8, pad)], axis=-1)
    return jnp.concatenate([x[:, :, :near], far], axis=1)


def unfold(x, w):
    near = x.shape[-1]
    return jnp.concatenate([x[:, :8, :], x[:, 8:, : w - near]], axis=-1)


def widen(x, width):
    return jnp.concatenate([x, zeros(x.shape[0], width - x.shape[1], dtype=x.dtype)], axis=-1)


class Exchange:
    def __init__(self, send, recv, ssem, rsem, n, me, place):
        self.send, self.recv, self.ssem, self.rsem = send, recv, ssem, rsem
        self.n, self.me, self.place = n, me, place

    def copy(self, to, slot):
        return pltpu.make_async_remote_copy(
            src_ref=self.send.at[to],
            dst_ref=self.recv.at[slot],
            send_sem=self.ssem,
            recv_sem=self.rsem,
            device_id=self.place(to),
            device_id_type=MESH,
        )

    def start(self):
        def step(i, carry):
            self.copy(lax.rem(self.me + i, self.n), self.me).start()
            return carry

        lax.fori_loop(1, self.n, step, 0)
        self.recv[self.me] = self.send[self.me]

    def wait(self):
        for ref, sem in ((self.send, self.ssem), (self.recv, self.rsem)):
            blocks = ref.at[pl.ds(0, self.n - 1)]
            pltpu.make_async_copy(blocks, blocks, sem).wait()


def kernel(
    lat_h, cot_h, mod_s_h, mod_t_h, wqs_h, wos_h, wqt_h, wot_h,
    gl_h, gqs_h, gos_h, gqt_h, got_h,
    lat, cot, mod_s, mod_t, gl, gqs, gos, gqt, got, iosem,
    wqs, wos, wqt, wot, wsem,
    normed, proj,
    a_s, a_r, b1_s, b1_r, att_s, scaled, dmid, t1_s, t1_r, t2_s, t2_r,
    c2_s, c2_r, c1_s, c1_r, dm_s, dm_r, dq_s, dq_r, d_s, d_r, dgq, dg, ngt, xsems,
    q_b, k_b, v_b, rqk, rl, rrow, do_b, kt_b, dk_f, dv_f,
    ng, ngsem, xn, xnsem, dt_s, dt_r, dtsem,
    xl, xrv, xr, xsem, lt,
    syq, ryq, syo, ryo, sxo, rxo, sxs, rxs, sys, rys, gys, gyr, sem4,
    szq, rzq, szo, rzo, sem8,
    fs, fr, fs_sem, fr_sem,
):
    f = lax.axis_index("frame")
    p = lax.axis_index("patch")
    core = lax.rem(p, 2)
    zh = lax.rem(lax.div(p, 2), 2)
    x = lax.div(p, 4)
    y = lax.rem(f, 4)
    zl = lax.div(f, 4)
    head = 2 * x + core
    clip_t = lax.div(f, 8)
    z = zh * 4 + zl

    loads = [
        pltpu.make_async_copy(src, dst, wsem.at[i])
        for i, (src, dst) in enumerate(
            ((wqs_h, wqs), (wot_h, wot), (wos_h, wos), (wqt_h, wqt))
        )
    ]
    reads = [
        pltpu.make_async_copy(src, dst, iosem.at[i])
        for i, (src, dst) in enumerate(
            ((lat_h, lat), (mod_s_h, mod_s), (cot_h, cot), (mod_t_h, mod_t))
        )
    ]
    writes = [
        pltpu.make_async_copy(src, dst, iosem.at[4 + i])
        for i, (src, dst) in enumerate(
            ((gl, gl_h), (gqt, gqt_h), (got, got_h), (gos, gos_h), (gqs, gqs_h))
        )
    ]
    for read in reads[:2]:
        read.start()
    loads[0].start()
    for read in reads[2:]:
        read.start()

    barrier = pltpu.get_barrier_semaphore()

    def greet(i, carry):
        pl.semaphore_signal(
            barrier, inc=1, device_id={"frame": lax.rem(f + i, 16)}, device_id_type=MESH
        )
        pl.semaphore_signal(
            barrier, inc=1, device_id={"patch": lax.rem(p + i, 16)}, device_id_type=MESH
        )
        return carry

    lax.fori_loop(1, 16, greet, 0)

    def greet_far(i, carry):
        pl.semaphore_signal(
            barrier,
            inc=1,
            device_id={
                "frame": 4 * lax.rem(zl + 1 + lax.div(i, 15), 4) + y,
                "patch": lax.rem(p + 1 + lax.rem(i, 15), 16),
            },
            device_id_type=MESH,
        )
        return carry

    lax.fori_loop(0, 45, greet_far, 0)

    def on_patch(i):
        return {"patch": i}

    def on_frame(i):
        return {"frame": i}

    def on_x(i):
        return {"patch": 4 * i + 2 * zh + core}

    def on_y(i):
        return {"frame": 4 * zl + i}

    def on_column(i):
        return {"patch": 4 * lax.rem(i, 4) + 2 * zh + lax.div(i, 4)}

    def on_z(i):
        return {
            "frame": 4 * lax.rem(i, 4) + y,
            "patch": 4 * x + 2 * lax.div(i, 4) + core,
        }

    ex_a = Exchange(a_s, a_r, xsems.at[0, 0], xsems.at[0, 1], 16, p, on_patch)
    ex_b1 = Exchange(b1_s, b1_r, xsems.at[1, 0], xsems.at[1, 1], 16, p, on_patch)
    ex_t1 = Exchange(t1_s, t1_r, xsems.at[3, 0], xsems.at[3, 1], 16, f, on_frame)
    ex_t2 = Exchange(t2_s, t2_r, xsems.at[4, 0], xsems.at[4, 1], 16, f, on_frame)
    ex_c2 = Exchange(c2_s, c2_r, xsems.at[5, 0], xsems.at[5, 1], 16, f, on_frame)
    ex_c1 = Exchange(c1_s, c1_r, xsems.at[6, 0], xsems.at[6, 1], 16, p, on_patch)
    ex_dm = Exchange(dm_s, dm_r, xsems.at[7, 0], xsems.at[7, 1], 16, f, on_frame)
    ex_dq = Exchange(dq_s, dq_r, xsems.at[2, 0], xsems.at[2, 1], 16, p, on_patch)
    ex_d = Exchange(d_s, d_r, xsems.at[8, 0], xsems.at[8, 1], 16, p, on_patch)
    ex_dt = Exchange(dt_s, dt_r, dtsem.at[0], dtsem.at[1], 8, 4 * core + x, on_column)
    ex_yq = Exchange(syq, ryq, sem4.at[0, 0], sem4.at[0, 1], 4, y, on_y)
    ex_yo = Exchange(syo, ryo, sem4.at[1, 0], sem4.at[1, 1], 4, y, on_y)
    ex_xo = Exchange(sxo, rxo, sem4.at[2, 0], sem4.at[2, 1], 4, x, on_x)
    ex_xs = Exchange(sxs, rxs, sem4.at[4, 0], sem4.at[4, 1], 4, x, on_x)
    ex_ys = Exchange(sys, rys, sem4.at[5, 0], sem4.at[5, 1], 4, y, on_y)
    ex_gy = Exchange(gys, gyr, sem4.at[3, 0], sem4.at[3, 1], 4, y, on_y)
    ex_zq = Exchange(szq, rzq, sem8.at[0, 0], sem8.at[0, 1], 8, z, on_z)
    ex_zo = Exchange(szo, rzo, sem8.at[1, 0], sem8.at[1, 1], 8, z, on_z)

    reads[0].wait()
    reads[1].wait()
    for c in range(2):
        xh, _ = normalise(lat[c].astype(F32))
        normed[c] = (xh * (1.0 + mod_s[1, c : c + 1, :]) + mod_s[0, c : c + 1, :]).astype(BF)
    loads[0].wait()
    for load in loads[1:]:
        load.start()
    proj[...] = nt(normed[...].reshape(128, D), wqs[...])
    lane = lax.broadcasted_iota(jnp.int32, (128, 224), 1)
    for h in range(HEADS):
        q = proj[:, HD * h : HD * h + HD]
        k = proj[:, ATT + HD * h : ATT + HD * h + HD]
        v = proj[:, 2 * ATT + HD * h : 2 * ATT + HD * h + HD]
        rq = inverse_norm(q)
        rk = inverse_norm(k)
        row = jnp.concatenate([q * rq, k * rk, v, zeros(128, 8)], axis=-1)
        row = jnp.where(lane == 216, rq, row)
        row = jnp.where(lane == 217, rq - rounded(rq), row)
        row = jnp.where(lane == 218, rk, row)
        row = jnp.where(lane == 219, rk - rounded(rk), row)
        row = row.astype(BF).reshape(2, 4, 16, 224)
        for c in range(2):
            quarters = [row[c, j] for j in range(4)]
            a_s[owner(c, h)] = jnp.concatenate(quarters, axis=-1)
    pl.semaphore_wait(barrier, 75)
    ex_a.start()

    reads[2].wait()
    reads[3].wait()
    loads[1].wait()
    for c in range(2):
        scaled[c] = (cot[c].astype(F32) * mod_t[2, c : c + 1, :]).astype(BF)
    dout = nt(scaled[...].reshape(128, D), wot[...])
    for c in range(2):
        part = dout[64 * c : 64 * c + 64].reshape(8, 8, ATT)
        t2_s[8 * c : 8 * c + 8] = fold(part, 384).astype(BF)
    ng[core, x, zh] = normed[zh]
    gather_z = pltpu.make_async_remote_copy(
        src_ref=normed.at[1 - zh],
        dst_ref=ng.at[core, x, zh],
        send_sem=ngsem.at[0, 0],
        recv_sem=ngsem.at[1, 0],
        device_id={"patch": 4 * x + 2 * (1 - zh) + core},
        device_id_type=MESH,
    )
    ex_t2.start()
    ex_a.wait()
    gather_z.start()

    for part in range(4):
        rows = a_r[4 * part : 4 * part + 4]
        rows = [rows[:, :, 224 * j : 224 * j + 224] for j in range(4)]
        rows = jnp.stack(rows, axis=1).reshape(256, 224)
        at = pl.ds(256 * part, 256)
        q_b[at, :] = rows[:, 0:HD]
        k_b[at, :] = rows[:, HD : 2 * HD]
        v_b[at, :] = rows[:, 2 * HD : 3 * HD]
        r = rows[:, 216:220].astype(F32)
        rqk[at, 0:1] = r[:, 0:1] + r[:, 1:2]
        rqk[at, 1:2] = r[:, 2:3] + r[:, 3:4]

    def attend(i, carry):
        part = lax.rem(x + 1 + i, 4)
        at = pl.ds(pl.multiple_of(part * 256, 256), 256)
        e = jnp.exp2(nt(q_b[at, :], k_b[...]) * (SCALE * LOG2E))
        r = 1.0 / jnp.sum(e, axis=-1, keepdims=True)
        rl[at, :] = r
        pieces = (nn(e.astype(BF), v_b[...]) * r).astype(BF).reshape(4, 4, 16, HD)
        row = [pieces[:, j].reshape(64, HD) for j in range(4)] + [zeros(64, 96, dtype=BF)]
        row = jnp.concatenate(row, axis=-1).reshape(4, 16, 384)
        b1_s[pl.ds(4 * part, 4)] = row
        for j in range(4):
            to = 4 * part + j

            @pl.when(to != p)
            def _():
                ex_b1.copy(to, p).start()

        return carry

    lax.fori_loop(0, 4, attend, 0)
    b1_r[p] = b1_s[p]
    for part in range(4):
        at = pl.ds(256 * part, 256)
        rrow[:, at] = jnp.transpose(widen(rl[at, :], 128))[0:1, :]
    loads[2].wait()
    ex_b1.wait()
    atts = []
    for c in range(2):
        blocks = [b1_r[owner(c, h)] for h in range(HEADS)]
        rows = [
            jnp.concatenate([b[:, HD * j : HD * j + HD] for b in blocks], axis=-1)
            for j in range(4)
        ]
        atts.append(jnp.concatenate(rows, axis=0))
    att_s[...] = jnp.concatenate(atts, axis=0)
    added = nn(att_s[...], wos[...])
    for c in range(2):
        middle = lat[c].astype(F32) + mod_s[2, c : c + 1, :] * added[64 * c : 64 * c + 64]
        t1_s[8 * c : 8 * c + 8] = fold(middle.reshape(8, 8, D), 640).astype(BF)
    ex_t1.start()

    gather_z.wait()

    def gather_x(i, back):
        block = lax.rem(x + 4 - i, 4) if back else x
        return pltpu.make_async_remote_copy(
            src_ref=ng.at[core, block],
            dst_ref=ng.at[core, block],
            send_sem=ngsem.at[0, i],
            recv_sem=ngsem.at[1, i],
            device_id=on_x(lax.rem(x + i, 4)),
            device_id_type=MESH,
        )

    def gather_core(back):
        side = 1 - core if back else core
        return pltpu.make_async_remote_copy(
            src_ref=ng.at[side],
            dst_ref=ng.at[side],
            send_sem=ngsem.at[0, 4],
            recv_sem=ngsem.at[1, 4],
            device_id={"patch": p + 1 - 2 * core},
            device_id_type=MESH,
        )

    for i in range(1, 4):
        gather_x(i, False).start()

    def pick(ref, i):
        return jnp.where(clip_t == 0, ref[i, 0:1, :], ref[i, 1:2, :])

    shift_t, stretch_t = pick(mod_t, 0), pick(mod_t, 1)

    def spread_rows(a):
        parts = []
        for yy in range(4):
            for zz in range(4):
                at = 36 * (4 * zz + yy)
                parts += [a[:, at : at + 36], zeros(128, 4, dtype=BF)]
        return parts

    def core_columns(full, cc):
        parts = [full[:, HD * (2 * b + cc) : HD * (2 * b + cc) + HD] for b in range(8)]
        return jnp.concatenate(parts + [zeros(128, 64, dtype=BF)], axis=-1)

    xl[1, core] = jnp.concatenate(spread_rows(att_s[...]), axis=-1)
    for cc in range(2):
        xrv[0, cc] = core_columns(scaled[...].reshape(128, D), cc)
    xr[0, core] = xrv[0, core]

    def pair_copies(which, slot):
        there = {"patch": p + 1 - 2 * core}
        pairs = ((xl.at[which, core], xl), (xrv.at[which, 1 - core], xr))
        return [
            pltpu.make_async_remote_copy(
                src_ref=src,
                dst_ref=dst.at[which, slot],
                send_sem=xsem.at[0, 2 * which + i],
                recv_sem=xsem.at[1, 2 * which + i],
                device_id=there,
                device_id_type=MESH,
            )
            for i, (src, dst) in enumerate(pairs)
        ]

    for part in range(4):
        at = pl.ds(256 * part, 256)
        kt_b[:, at] = jnp.transpose(widen(k_b[at, :].astype(F32), 128)).astype(BF)
    loads[3].wait()
    ex_t1.wait()
    middle = unfold(t1_r[...].astype(F32), D).reshape(128, D)
    xh_t, r_t = normalise(middle)
    normed_t = (xh_t * (1.0 + stretch_t) + shift_t).astype(BF)
    xn[4 * core + x] = normed_t

    def normed_x(i, back):
        block = 4 * core + (lax.rem(x + 4 - i, 4) if back else x)
        return pltpu.make_async_remote_copy(
            src_ref=xn.at[block],
            dst_ref=xn.at[block],
            send_sem=xnsem.at[0, i],
            recv_sem=xnsem.at[1, i],
            device_id=on_x(lax.rem(x + i, 4)),
            device_id_type=MESH,
        )

    def normed_core(back):
        side = pl.ds(4 * (1 - core if back else core), 4)
        return pltpu.make_async_remote_copy(
            src_ref=xn.at[side],
            dst_ref=xn.at[side],
            send_sem=xnsem.at[0, 0],
            recv_sem=xnsem.at[1, 0],
            device_id={"patch": p + 1 - 2 * core},
            device_id_type=MESH,
        )

    for i in range(1, 4):
        normed_x(i, False).start()
    proj[...] = nt(normed_t, wqt[...])
    same = lax.rem(lax.broadcasted_iota(jnp.int32, (128, 128), 0), 8) == lax.rem(
        lax.broadcasted_iota(jnp.int32, (128, 128), 1), 8
    )
    heads, att_parts, dq_parts, dk_parts, dv_parts = [], [], [], [], []
    for h in range(HEADS):
        q = proj[:, HD * h : HD * h + HD]
        k = proj[:, ATT + HD * h : ATT + HD * h + HD]
        v = proj[:, 2 * ATT + HD * h : 2 * ATT + HD * h + HD].astype(BF)
        rq = inverse_norm(q)
        rk = inverse_norm(k)
        q = q * rq
        k = k * rk
        e = jnp.where(same, jnp.exp(nt(q.astype(BF), k.astype(BF)) * SCALE), 0.0)
        soft = e * (1.0 / jnp.sum(e, axis=-1, keepdims=True))
        att_parts.append(nn(soft.astype(BF), v))
        heads.append((q, k, v, rq, rk, soft))
    att_t = jnp.concatenate(att_parts, axis=-1)
    c2_s[...] = fold(att_t.reshape(16, 8, ATT), 384).astype(BF)
    ex_c2.start()
    ex_t2.wait()
    dout_t = unfold(t2_r[...].astype(F32), ATT).reshape(128, ATT)
    for h, (q, k, v, rq, rk, soft) in enumerate(heads):
        do = dout_t[:, HD * h : HD * h + HD].astype(BF)
        dp = nt(do, v)
        ds = (soft * (dp - jnp.sum(dp * soft, axis=-1, keepdims=True)) * SCALE).astype(BF)
        dq_parts.append(head_back(rounded(nn(ds, k.astype(BF))), q, rq))
        dk_parts.append(head_back(rounded(tn(ds, q.astype(BF))), k, rk))
        dv_parts.append(tn(soft.astype(BF), do))
    parts = [part.astype(BF) for part in dq_parts + dk_parts + dv_parts]
    dproj_t = jnp.concatenate(parts, axis=-1)
    dn = nn(dproj_t, wqt[...])
    back = normalise_back(dn, stretch_t, xh_t, r_t)
    dm_s[...] = fold(back.reshape(16, 8, D), 640).astype(BF)
    ex_dm.start()

    for cc in range(2):
        for xx in range(4):
            at = 108 * (4 * xx + cc)
            row = [dproj_t[:, at : at + 108], zeros(128, 20, dtype=BF)]
            row += [dproj_t[:, at + 216 : at + 324], zeros(128, 20, dtype=BF)]
            dt_s[4 * cc + xx] = jnp.concatenate(row, axis=-1)
    ex_dt.start()

    ex_c2.wait()
    att_t = unfold(c2_r[...].astype(F32), ATT).reshape(128, ATT)
    xl[0, core] = jnp.concatenate(spread_rows(att_t.astype(BF)), axis=-1)
    for copy in pair_copies(0, core):
        copy.start()
    for i in range(1, 4):
        gather_x(i, True).wait()
    gather_core(False).start()
    for copy in pair_copies(0, 1 - core):
        copy.wait()
    lt[...] = jnp.transpose(xl[0].reshape(256, 640).astype(F32)).astype(BF)
    g = nn(lt[...], xr[0].reshape(256, 640))
    for yy in range(4):
        syo[yy] = g[160 * yy : 160 * yy + 160].astype(BF)
    ex_yo.start()
    gather_core(True).wait()
    for i in range(8):
        block = ng[i // 4, i % 4].reshape(128, D).astype(F32)
        block = jnp.transpose(block).reshape(4, 4, HD, 128)
        for yy in range(4):
            rows = block[:, yy].reshape(288, 128)
            ngt[288 * yy : 288 * yy + 288, 128 * i : 128 * i + 128] = rows.astype(BF)

    ex_dm.wait()
    back = unfold(dm_r[...].astype(F32), D).reshape(2, 64, D)
    parts = []
    for c in range(2):
        total = rounded(cot[c].astype(F32) + back[c])
        dmid[c] = total.astype(BF)
        parts.append((total * mod_s[2, c : c + 1, :]).astype(BF))
    scaled_s = jnp.concatenate(parts, axis=0)
    tokens = nt(scaled_s, wos[...]).astype(BF).reshape(2, 64, ATT)
    for c in range(2):
        for h in range(HEADS):
            part = tokens[c][:, HD * h : HD * h + HD].reshape(4, 16, HD)
            row = [part[j] for j in range(4)] + [zeros(16, 96, dtype=BF)]
            c1_s[owner(c, h)] = jnp.concatenate(row, axis=-1)
    ex_c1.start()

    for cc in range(2):
        xrv[1, cc] = core_columns(scaled_s, cc)
    xr[1, core] = xrv[1, core]
    for copy in pair_copies(1, core):
        copy.start()
    for i in range(1, 4):
        normed_x(i, True).wait()
    normed_core(False).start()
    for copy in pair_copies(1, 1 - core):
        copy.wait()
    lt[...] = jnp.transpose(xr[1].reshape(256, 640).astype(F32)).astype(BF)
    g = nn(lt[...], xl[1].reshape(256, 640))
    for i in range(4):
        sxs[i] = g[144 * i : 144 * i + 144].astype(BF)
    ex_xs.start()
    normed_core(True).wait()
    ex_dt.wait()
    g = tn(xn[...].reshape(1024, D), dt_r[...].reshape(1024, 256)).reshape(4, 4, HD, 256)
    for yy in range(4):
        syq[yy] = g[:, yy].reshape(288, 256).astype(BF)
    ex_yq.start()
    ex_yo.wait()
    total = sum(ryo[i].astype(F32) for i in range(4))
    for i in range(4):
        sxo[i] = widen(total[:, 144 * i : 144 * i + 144], 256).astype(BF)
    ex_xo.start()
    ex_c1.wait()
    got_do = c1_r[...]
    parts = [got_do[:, :, HD * j : HD * j + HD] for j in range(4)]
    do_b[...] = (jnp.stack(parts, axis=1).reshape(1024, HD).astype(F32) * rl[...]).astype(BF)
    dk_f[...] = jnp.zeros_like(dk_f)
    dv_f[...] = jnp.zeros_like(dv_f)

    def attend_back(i, carry):
        part = lax.rem(x + 1 + i, 4)
        at = pl.ds(pl.multiple_of(part * 256, 256), 256)
        qb, dob = q_b[at, :], do_b[at, :]
        e = jnp.exp2(nt(k_b[...], qb) * (SCALE * LOG2E))
        dp = nt(v_b[...], dob)
        shift = rrow[:, at] * jnp.sum(dp * e, axis=0, keepdims=True)
        ds = (e * (dp - shift)).astype(BF)
        dv_f[...] += nn(e.astype(BF), dob)
        dk_f[...] += nn(ds, qb)
        dq = rounded(jnp.transpose(nn(kt_b[...], ds))[:, :HD] * SCALE)
        dq = head_back(dq, qb.astype(F32), rqk[at, 0:1]).astype(BF)
        blocks = pl.ds(4 * part, 4)
        dgq[blocks] = dq.reshape(4, 64, HD)
        dq = dq.reshape(4, 4, 16, HD)
        row = [dq[:, j].reshape(64, HD) for j in range(4)] + [zeros(64, 96, dtype=BF)]
        dq_s[blocks] = jnp.concatenate(row, axis=-1).reshape(4, 16, 384)
        for j in range(4):
            to = 4 * part + j

            @pl.when(to != p)
            def _():
                ex_dq.copy(to, p).start()

        return carry

    lax.fori_loop(0, 4, attend_back, 0)
    dq_r[p] = dq_s[p]
    for part in range(4):
        at = pl.ds(256 * part, 256)
        dk = head_back(rounded(dk_f[at, :] * SCALE), k_b[at, :].astype(F32), rqk[at, 1:2])
        row = jnp.concatenate([dk.astype(BF), dv_f[at, :].astype(BF)], axis=-1)
        dg[4 * part : 4 * part + 4] = row.reshape(4, 64, 2 * HD)
        row = row.reshape(4, 4, 16, 2 * HD)
        row = [row[:, j].reshape(64, 2 * HD) for j in range(4)] + [zeros(64, 64, dtype=BF)]
        d_s[4 * part : 4 * part + 4] = jnp.concatenate(row, axis=-1).reshape(4, 16, 640)
    ex_d.start()

    order = [4 * xx + 2 * s + cc for cc in range(2) for xx in range(4) for s in range(2)]
    right = [jnp.concatenate([ref[i] for i in order], axis=0) for ref in (dgq, dg)]
    right = jnp.concatenate(right + [zeros(1024, 8, dtype=BF)], axis=-1)
    for i in range(1, 5):
        yy = lax.rem(y + i, 4)
        rows = pl.ds(pl.multiple_of(288 * yy, 288), 288)
        gys[yy] = nn(ngt[rows, :], right).astype(BF)
        if i < 4:
            ex_gy.copy(yy, y).start()
    gyr[y] = gys[y]
    ex_xs.wait()
    total = sum(rxs[i].astype(F32) for i in range(4))
    for i in range(4):
        part = total[:, 160 * i : 160 * i + 160]
        rest = [part[48 * j : 48 * j + 48, 128:] for j in range(3)] + [zeros(48, 32)]
        rest = jnp.concatenate(rest, axis=-1)
        sys[i] = jnp.concatenate([part[:, :128], rest], axis=0).astype(BF)
    ex_ys.start()
    ex_yq.wait()
    total = sum(ryq[i].astype(F32) for i in range(4))
    for i in range(8):
        zz, s = i % 4, i // 4
        part = total[HD * zz : HD * zz + HD, 128 * s : 128 * s + 108]
        rest = [part[64:, 18 * j : 18 * j + 18] for j in range(6)] + [zeros(16, 18)]
        rest = jnp.concatenate(rest, axis=0)
        szq[i] = jnp.concatenate([part[:64], rest, zeros(64, 2)], axis=-1).astype(BF)
    ex_zq.start()


    ex_gy.wait()
    total = sum(gyr[i].astype(F32) for i in range(4)).reshape(4, 3, 24, 224)
    for b in range(6):
        cols = [total[:, r, :, 36 * b : 36 * b + 36] for r in range(3)] + [zeros(4, 24, 20)]
        cols = jnp.concatenate(cols, axis=-1)
        fs[:, b] = jnp.concatenate([cols, zeros(4, 8, 128)], axis=1).astype(BF)

    def piece(i, b):
        to_z = lax.rem(zl + i, 4)
        block = 16 * (b // 2) + 2 * head + b % 2
        to, slot = lax.div(block, 3), lax.rem(block, 3)
        copy = pltpu.make_async_remote_copy(
            src_ref=fs.at[to_z, b],
            dst_ref=fr.at[slot, z],
            send_sem=fs_sem.at[b if i == 0 else 6],
            recv_sem=fr_sem.at[2 * slot + zh if i == 0 else 6],
            device_id={"frame": 4 * to_z + y, "patch": to},
            device_id_type=MESH,
        )
        return to, slot, copy

    for i in range(4):
        for b in range(6):
            to, slot, copy = piece(i, b)
            if i > 0:
                copy.start()
            else:

                @pl.when(to != p)
                def _():
                    copy.start()

                @pl.when(to == p)
                def _():
                    fr[slot, z] = fs[zl, b]

    ex_xo.wait()
    ex_ys.wait()
    total = sum(rxo[i].astype(F32) for i in range(4))
    other = sum(rys[i].astype(F32) for i in range(4))
    rest = jnp.concatenate([other[144:, 32 * j : 32 * j + 32] for j in range(3)], axis=0)
    other = widen(jnp.concatenate([other[:144], rest], axis=-1), 256)
    other = jnp.transpose(jnp.concatenate([other, zeros(112, 256)], axis=0))
    for i in range(8):
        zz, s = i % 4, i // 4
        rows, cols = slice(40 * zz, 40 * zz + 36), slice(HD * s, HD * s + HD)
        part = jnp.concatenate([total[rows, cols], other[rows, cols]], axis=0)
        rest = jnp.concatenate([part[48:, :36], part[48:, 36:]], axis=0)
        szo[i] = jnp.concatenate([part[:48], rest, zeros(48, 20)], axis=-1).astype(BF)
    ex_zo.start()

    ex_dq.wait()
    ex_d.wait()
    parts = []
    for c in range(2):
        firsts = [dq_r[owner(c, h)] for h in range(HEADS)]
        blocks = [d_r[owner(c, h)] for h in range(HEADS)]
        for i in range(4):
            row = [b[:, HD * i : HD * i + HD] for b in firsts]
            at = [2 * HD * i + HD * j for j in range(2)]
            row += [b[:, a : a + HD] for a in at for b in blocks]
            parts.append(jnp.concatenate(row, axis=-1))
    dn = nn(jnp.concatenate(parts, axis=0), wqs[...])
    for c in range(2):
        xh, r = normalise(lat[c].astype(F32))
        back = normalise_back(dn[64 * c : 64 * c + 64], mod_s[1, c : c + 1, :], xh, r)
        gl[c] = (dmid[c].astype(F32) + back).astype(BF)
    writes[0].start()


    ex_zq.wait()
    total = sum(rzq[i].astype(F32) for i in range(8))
    rest = [total[8 * j : 8 * j + 8, 108:126] for j in range(6)]
    rest = jnp.concatenate(rest, axis=-1)
    gqt[...] = jnp.concatenate([total[:, :108], rest], axis=0)
    writes[1].start()
    ex_zo.wait()
    total = sum(rzo[i].astype(F32) for i in range(8))
    rest = jnp.concatenate([total[:24, 72:108], total[24:, 72:108]], axis=-1)
    total = jnp.concatenate([total[:, :HD], rest], axis=0)
    got[...] = total[:36]
    gos[...] = total[36:]
    writes[2].start()
    writes[3].start()

    for b in range(6):
        to, slot, copy = piece(0, b)

        @pl.when(to != p)
        def _():
            copy.wait_send()

    for slot in range(3):
        left = lax.rem(3 * p + slot, 16)
        source = lax.div(left, 4) * 4 + lax.rem(lax.div(left, 2), 2)
        for c in range(2):
            at = 4 * c + zl
            copy = pltpu.make_async_remote_copy(
                src_ref=fs.at[0, 0],
                dst_ref=fr.at[slot, at],
                send_sem=fs_sem.at[0],
                recv_sem=fr_sem.at[2 * slot + c],
                device_id={"patch": source + 2 * c},
                device_id_type=MESH,
            )

            @pl.when(source + 2 * c != p)
            def _():
                copy.wait_recv()

    for ref, sem in ((fs.at[pl.ds(0, 3)], fs_sem.at[6]), (fr.at[:, pl.ds(0, 6)], fr_sem.at[6])):
        pltpu.make_async_copy(ref, ref, sem).wait()

    cols = []
    for slot in range(3):
        total = sum(fr[slot, i].astype(F32) for i in range(8))
        cols.append(
            jnp.concatenate([total[:24, 36 * r : 36 * r + 36] for r in range(3)], axis=0)
        )
    gqs[...] = jnp.concatenate(cols, axis=-1)
    writes[4].start()
    for write in writes:
        write.wait()


def hand_over(*refs):
    given, out, held, sem = refs[:5], refs[5:10], refs[10:15], refs[15]
    into = [pltpu.make_async_copy(given[i], held[i], sem.at[0, i]) for i in range(5)]
    back = [pltpu.make_async_copy(held[i], out[i], sem.at[1, i]) for i in range(5)]
    for copy in into:
        copy.start()
    for i in range(5):
        into[i].wait()
        back[i].start()
    for copy in back:
        copy.wait()


def body(lat, mod_s, mod_t, wqs, wos, wqt, wot, cot):
    hbm = pl.BlockSpec(memory_space=pl.ANY)
    dma = pltpu.SemaphoreType.DMA

    def buf(*shape):
        return pltpu.VMEM(shape, BF)

    def wide(*shape):
        return pltpu.VMEM(shape, F32)

    outs = pl.pallas_call(
        kernel,
        out_shape=(
            jax.ShapeDtypeStruct((2, 64, D), BF),
            jax.ShapeDtypeStruct((72, 108), F32),
            jax.ShapeDtypeStruct((36, 72), F32),
            jax.ShapeDtypeStruct((72, 108), F32),
            jax.ShapeDtypeStruct((36, 72), F32),
        ),
        in_specs=[hbm] * 8,
        out_specs=(hbm,) * 5,
        scratch_shapes=[
            buf(2, 64, D), buf(2, 64, D), wide(3, 2, D), wide(3, 2, D),
            buf(2, 64, D), wide(72, 108), wide(36, 72), wide(72, 108), wide(36, 72), dma((9,)),
            buf(QKV, D), buf(ATT, D), buf(QKV, D), buf(ATT, D), dma((4,)),
            buf(2, 64, D), wide(128, QKV),
            buf(16, 16, 896), buf(16, 16, 896),
            buf(16, 16, 384), buf(16, 16, 384),
            buf(128, ATT), buf(2, 64, D), buf(2, 64, D),
            buf(16, 16, 640), buf(16, 16, 640),
            buf(16, 16, 384), buf(16, 16, 384),
            buf(16, 16, 384), buf(16, 16, 384),
            buf(16, 16, 384), buf(16, 16, 384),
            buf(16, 16, 640), buf(16, 16, 640),
            buf(16, 16, 384), buf(16, 16, 384), buf(16, 16, 640), buf(16, 16, 640),
            buf(16, 64, HD), buf(16, 64, 2 * HD), buf(1152, 1024),
            dma((9, 2)),
            buf(1024, HD), buf(1024, HD), buf(1024, HD), wide(1024, 2), wide(1024, 1), wide(1, 1024),
            buf(1024, HD), buf(128, 1024), wide(1024, HD), wide(1024, HD),
            buf(2, 4, 2, 64, D), dma((2, 5)),
            buf(8, 128, D), dma((2, 4)), buf(8, 128, 256), buf(8, 128, 256), dma((2,)),
            buf(2, 2, 128, 640), buf(2, 2, 128, 640), buf(2, 2, 128, 640), dma((2, 4)),
            buf(640, 256),
            buf(4, 288, 256), buf(4, 288, 256),
            buf(4, 160, 640), buf(4, 160, 640),
            buf(4, 160, 256), buf(4, 160, 256),
            buf(4, 144, 640), buf(4, 144, 640),
            buf(4, 192, 128), buf(4, 192, 128),
            buf(4, 288, 224), buf(4, 288, 224),
            dma((6, 2)),
            buf(8, 64, 128), buf(8, 64, 128),
            buf(8, 48, 128), buf(8, 48, 128),
            dma((2, 2)),
            buf(4, 6, 32, 128), buf(3, 8, 32, 128), dma((7,)), dma((7,)),
        ],
        compiler_params=pltpu.CompilerParams(
            collective_id=0, has_side_effects=True, vmem_limit_bytes=60 * 1024 * 1024
        ),
    )(
        lat.reshape(2, 64, D),
        cot.reshape(2, 64, D),
        mod_s.transpose(1, 0, 2),
        mod_t.transpose(1, 0, 2),
        wqs.T,
        wos,
        wqt.T,
        wot,
    )
    outs = pl.pallas_call(
        hand_over,
        out_shape=tuple(jax.ShapeDtypeStruct(o.shape, o.dtype) for o in outs),
        in_specs=[hbm] * 5,
        out_specs=(hbm,) * 5,
        scratch_shapes=[pltpu.VMEM(o.shape, o.dtype) for o in outs] + [dma((2, 5))],
    )(*outs)
    return (outs[0].reshape(2, 1, 64, D),) + tuple(outs[1:])


def solution(mesh):
    tokens = P(None, "frame", "patch", None)
    return jax.shard_map(
        body,
        mesh=mesh,
        in_specs=(tokens,) + (P(),) * 6 + (tokens,),
        out_specs=(tokens,) + (P("frame", "patch"),) * 4,
        check_vma=False,
    )
```

```python
import jax
import jax.numpy as jnp
from jax import lax
from jax.experimental import pallas as pl
from jax.experimental.pallas import tpu as pltpu
from jax.sharding import PartitionSpec as P

F32 = jnp.float32
BF = jnp.bfloat16
MESH = pl.DeviceIdType.MESH
HD = 72
HEADS = 8
ATT = 576
D = 1152
QKV = 1728
EPS = 1e-06
SCALE = HD**-0.5
LOG2E = 1.4426950408889634


def nn(a, b):
    return lax.dot_general(a, b, (((1,), (0,)), ((), ())), preferred_element_type=F32)


def nt(a, b):
    return lax.dot_general(a, b, (((1,), (1,)), ((), ())), preferred_element_type=F32)


def tn(a, b):
    return lax.dot_general(a, b, (((0,), (0,)), ((), ())), preferred_element_type=F32)


def owner(c, h):
    return (h // 2) * 4 + c * 2 + h % 2


def normalise(x):
    centre = x - jnp.mean(x, axis=-1, keepdims=True)
    r = lax.rsqrt(jnp.mean(centre * centre, axis=-1, keepdims=True) + EPS)
    return centre * r, r


def normalise_back(dn, stretch, xh, r):
    dx = dn * (1.0 + stretch)
    dx = dx - xh * jnp.mean(dx * xh, axis=-1, keepdims=True)
    dx = r * dx
    return dx - jnp.mean(dx, axis=-1, keepdims=True)


def inverse_norm(x):
    return lax.rsqrt(jnp.sum(x * x, axis=-1, keepdims=True) * (1.0 / HD) + EPS)


def head_back(dy, y, r):
    return r * (dy - y * (jnp.sum(dy * y, axis=-1, keepdims=True) * (1.0 / HD)))


def rounded(x):
    return x.astype(BF).astype(F32)


def zeros(*shape, dtype=F32):
    return jnp.zeros(shape, dtype)


def fold(x, near):
    n, _, w = x.shape
    far = x[:, :, near:]
    pad = 2 * near - w
    far = jnp.concatenate([far, zeros(n, 8, pad)], axis=-1)
    return jnp.concatenate([x[:, :, :near], far], axis=1)


def unfold(x, w):
    near = x.shape[-1]
    return jnp.concatenate([x[:, :8, :], x[:, 8:, : w - near]], axis=-1)


def widen(x, width):
    return jnp.concatenate([x, zeros(x.shape[0], width - x.shape[1], dtype=x.dtype)], axis=-1)


class Exchange:
    def __init__(self, send, recv, ssem, rsem, n, me, place):
        self.send, self.recv, self.ssem, self.rsem = send, recv, ssem, rsem
        self.n, self.me, self.place = n, me, place

    def copy(self, to, slot):
        return pltpu.make_async_remote_copy(
            src_ref=self.send.at[to],
            dst_ref=self.recv.at[slot],
            send_sem=self.ssem,
            recv_sem=self.rsem,
            device_id=self.place(to),
            device_id_type=MESH,
        )

    def start(self):
        def step(i, carry):
            self.copy(lax.rem(self.me + i, self.n), self.me).start()
            return carry

        lax.fori_loop(1, self.n, step, 0)
        self.recv[self.me] = self.send[self.me]

    def wait(self):
        for ref, sem in ((self.send, self.ssem), (self.recv, self.rsem)):
            blocks = ref.at[pl.ds(0, self.n - 1)]
            pltpu.make_async_copy(blocks, blocks, sem).wait()


def kernel(
    lat_h, cot_h, mod_s_h, mod_t_h, wqs_h, wos_h, wqt_h, wot_h,
    gl_h, gqs_h, gos_h, gqt_h, got_h,
    lat, cot, mod_s, mod_t, gl, gqs, gos, gqt, got, iosem,
    wqs, wos, wqt, wot, wsem,
    normed, proj,
    a_s, a_r, b1_s, b1_r, att_s, scaled, dmid, t1_s, t1_r, t2_s, t2_r,
    c2_s, c2_r, c1_s, c1_r, dm_s, dm_r, dq_s, dq_r, d_s, d_r, dgq, dg, ngt, xsems,
    q_b, k_b, v_b, rqk, rl, rrow, do_b, kt_b, dk_f, dv_f,
    ng, ngsem, xn, xnsem, dt_s, dt_r, dtsem,
    xl, xrv, xr, xsem, lt,
    syq, ryq, syo, ryo, sxo, rxo, sxs, rxs, sys, rys, gys, gyr, sem4,
    szq, rzq, szo, rzo, sem8,
    fs, fr, fs_sem, fr_sem,
):
    f = lax.axis_index("frame")
    p = lax.axis_index("patch")
    core = lax.rem(p, 2)
    zh = lax.rem(lax.div(p, 2), 2)
    x = lax.div(p, 4)
    y = lax.rem(f, 4)
    zl = lax.div(f, 4)
    head = 2 * x + core
    clip_t = lax.div(f, 8)
    z = zh * 4 + zl

    loads = [
        pltpu.make_async_copy(src, dst, wsem.at[i])
        for i, (src, dst) in enumerate(
            ((wqs_h, wqs), (wot_h, wot), (wos_h, wos), (wqt_h, wqt))
        )
    ]
    reads = [
        pltpu.make_async_copy(src, dst, iosem.at[i])
        for i, (src, dst) in enumerate(
            ((lat_h, lat), (mod_s_h, mod_s), (cot_h, cot), (mod_t_h, mod_t))
        )
    ]
    writes = [
        pltpu.make_async_copy(src, dst, iosem.at[4 + i])
        for i, (src, dst) in enumerate(
            ((gl, gl_h), (gqt, gqt_h), (got, got_h), (gos, gos_h), (gqs, gqs_h))
        )
    ]
    for read in reads[:2]:
        read.start()
    loads[0].start()
    for read in reads[2:]:
        read.start()

    barrier = pltpu.get_barrier_semaphore()

    def greet(i, carry):
        pl.semaphore_signal(
            barrier, inc=1, device_id={"frame": lax.rem(f + i, 16)}, device_id_type=MESH
        )
        pl.semaphore_signal(
            barrier, inc=1, device_id={"patch": lax.rem(p + i, 16)}, device_id_type=MESH
        )
        return carry

    lax.fori_loop(1, 16, greet, 0)

    def greet_far(i, carry):
        pl.semaphore_signal(
            barrier,
            inc=1,
            device_id={
                "frame": 4 * lax.rem(zl + 1 + lax.div(i, 15), 4) + y,
                "patch": lax.rem(p + 1 + lax.rem(i, 15), 16),
            },
            device_id_type=MESH,
        )
        return carry

    lax.fori_loop(0, 45, greet_far, 0)

    def on_patch(i):
        return {"patch": i}

    def on_frame(i):
        return {"frame": i}

    def on_x(i):
        return {"patch": 4 * i + 2 * zh + core}

    def on_y(i):
        return {"frame": 4 * zl + i}

    def on_column(i):
        return {"patch": 4 * lax.rem(i, 4) + 2 * zh + lax.div(i, 4)}

    def on_z(i):
        return {
            "frame": 4 * lax.rem(i, 4) + y,
            "patch": 4 * x + 2 * lax.div(i, 4) + core,
        }

    ex_a = Exchange(a_s, a_r, xsems.at[0, 0], xsems.at[0, 1], 16, p, on_patch)
    ex_b1 = Exchange(b1_s, b1_r, xsems.at[1, 0], xsems.at[1, 1], 16, p, on_patch)
    ex_t1 = Exchange(t1_s, t1_r, xsems.at[3, 0], xsems.at[3, 1], 16, f, on_frame)
    ex_t2 = Exchange(t2_s, t2_r, xsems.at[4, 0], xsems.at[4, 1], 16, f, on_frame)
    ex_c2 = Exchange(c2_s, c2_r, xsems.at[5, 0], xsems.at[5, 1], 16, f, on_frame)
    ex_c1 = Exchange(c1_s, c1_r, xsems.at[6, 0], xsems.at[6, 1], 16, p, on_patch)
    ex_dm = Exchange(dm_s, dm_r, xsems.at[7, 0], xsems.at[7, 1], 16, f, on_frame)
    ex_dq = Exchange(dq_s, dq_r, xsems.at[2, 0], xsems.at[2, 1], 16, p, on_patch)
    ex_d = Exchange(d_s, d_r, xsems.at[8, 0], xsems.at[8, 1], 16, p, on_patch)
    ex_dt = Exchange(dt_s, dt_r, dtsem.at[0], dtsem.at[1], 8, 4 * core + x, on_column)
    ex_yq = Exchange(syq, ryq, sem4.at[0, 0], sem4.at[0, 1], 4, y, on_y)
    ex_yo = Exchange(syo, ryo, sem4.at[1, 0], sem4.at[1, 1], 4, y, on_y)
    ex_xo = Exchange(sxo, rxo, sem4.at[2, 0], sem4.at[2, 1], 4, x, on_x)
    ex_xs = Exchange(sxs, rxs, sem4.at[4, 0], sem4.at[4, 1], 4, x, on_x)
    ex_ys = Exchange(sys, rys, sem4.at[5, 0], sem4.at[5, 1], 4, y, on_y)
    ex_gy = Exchange(gys, gyr, sem4.at[3, 0], sem4.at[3, 1], 4, y, on_y)
    ex_zq = Exchange(szq, rzq, sem8.at[0, 0], sem8.at[0, 1], 8, z, on_z)
    ex_zo = Exchange(szo, rzo, sem8.at[1, 0], sem8.at[1, 1], 8, z, on_z)

    reads[0].wait()
    reads[1].wait()
    for c in range(2):
        xh, _ = normalise(lat[c].astype(F32))
        normed[c] = (xh * (1.0 + mod_s[1, c : c + 1, :]) + mod_s[0, c : c + 1, :]).astype(BF)
    loads[0].wait()
    for load in loads[1:]:
        load.start()
    proj[...] = nt(normed[...].reshape(128, D), wqs[...])
    lane = lax.broadcasted_iota(jnp.int32, (128, 224), 1)
    for h in range(HEADS):
        q = proj[:, HD * h : HD * h + HD]
        k = proj[:, ATT + HD * h : ATT + HD * h + HD]
        v = proj[:, 2 * ATT + HD * h : 2 * ATT + HD * h + HD]
        rq = inverse_norm(q)
        rk = inverse_norm(k)
        row = jnp.concatenate([q * rq, k * rk, v, zeros(128, 8)], axis=-1)
        row = jnp.where(lane == 216, rq, row)
        row = jnp.where(lane == 217, rq - rounded(rq), row)
        row = jnp.where(lane == 218, rk, row)
        row = jnp.where(lane == 219, rk - rounded(rk), row)
        row = row.astype(BF).reshape(2, 4, 16, 224)
        for c in range(2):
            quarters = [row[c, j] for j in range(4)]
            a_s[owner(c, h)] = jnp.concatenate(quarters, axis=-1)
    pl.semaphore_wait(barrier, 75)
    ex_a.start()

    reads[2].wait()
    reads[3].wait()
    loads[1].wait()
    for c in range(2):
        scaled[c] = (cot[c].astype(F32) * mod_t[2, c : c + 1, :]).astype(BF)
    dout = nt(scaled[...].reshape(128, D), wot[...])
    for c in range(2):
        part = dout[64 * c : 64 * c + 64].reshape(8, 8, ATT)
        t2_s[8 * c : 8 * c + 8] = fold(part, 384).astype(BF)
    ng[core, x, zh] = normed[zh]
    gather_z = pltpu.make_async_remote_copy(
        src_ref=normed.at[1 - zh],
        dst_ref=ng.at[core, x, zh],
        send_sem=ngsem.at[0, 0],
        recv_sem=ngsem.at[1, 0],
        device_id={"patch": 4 * x + 2 * (1 - zh) + core},
        device_id_type=MESH,
    )
    ex_t2.start()
    ex_a.wait()
    gather_z.start()

    for part in range(4):
        rows = a_r[4 * part : 4 * part + 4]
        rows = [rows[:, :, 224 * j : 224 * j + 224] for j in range(4)]
        rows = jnp.stack(rows, axis=1).reshape(256, 224)
        at = pl.ds(256 * part, 256)
        q_b[at, :] = rows[:, 0:HD]
        k_b[at, :] = rows[:, HD : 2 * HD]
        v_b[at, :] = rows[:, 2 * HD : 3 * HD]
        r = rows[:, 216:220].astype(F32)
        rqk[at, 0:1] = r[:, 0:1] + r[:, 1:2]
        rqk[at, 1:2] = r[:, 2:3] + r[:, 3:4]

    def attend(i, carry):
        part = lax.rem(x + 1 + i, 4)
        at = pl.ds(pl.multiple_of(part * 256, 256), 256)
        e = jnp.exp2(nt(q_b[at, :], k_b[...]) * (SCALE * LOG2E))
        r = 1.0 / jnp.sum(e, axis=-1, keepdims=True)
        rl[at, :] = r
        pieces = (nn(e.astype(BF), v_b[...]) * r).astype(BF).reshape(4, 4, 16, HD)
        row = [pieces[:, j].reshape(64, HD) for j in range(4)] + [zeros(64, 96, dtype=BF)]
        row = jnp.concatenate(row, axis=-1).reshape(4, 16, 384)
        b1_s[pl.ds(4 * part, 4)] = row
        for j in range(4):
            to = 4 * part + j

            @pl.when(to != p)
            def _():
                ex_b1.copy(to, p).start()

        return carry

    lax.fori_loop(0, 4, attend, 0)
    b1_r[p] = b1_s[p]
    for part in range(4):
        at = pl.ds(256 * part, 256)
        rrow[:, at] = jnp.transpose(widen(rl[at, :], 128))[0:1, :]
    loads[2].wait()
    ex_b1.wait()
    atts = []
    for c in range(2):
        blocks = [b1_r[owner(c, h)] for h in range(HEADS)]
        rows = [
            jnp.concatenate([b[:, HD * j : HD * j + HD] for b in blocks], axis=-1)
            for j in range(4)
        ]
        atts.append(jnp.concatenate(rows, axis=0))
    att_s[...] = jnp.concatenate(atts, axis=0)
    added = nn(att_s[...], wos[...])
    for c in range(2):
        middle = lat[c].astype(F32) + mod_s[2, c : c + 1, :] * added[64 * c : 64 * c + 64]
        t1_s[8 * c : 8 * c + 8] = fold(middle.reshape(8, 8, D), 640).astype(BF)
    ex_t1.start()

    gather_z.wait()

    def gather_x(i, back):
        block = lax.rem(x + 4 - i, 4) if back else x
        return pltpu.make_async_remote_copy(
            src_ref=ng.at[core, block],
            dst_ref=ng.at[core, block],
            send_sem=ngsem.at[0, i],
            recv_sem=ngsem.at[1, i],
            device_id=on_x(lax.rem(x + i, 4)),
            device_id_type=MESH,
        )

    def gather_core(back):
        side = 1 - core if back else core
        return pltpu.make_async_remote_copy(
            src_ref=ng.at[side],
            dst_ref=ng.at[side],
            send_sem=ngsem.at[0, 4],
            recv_sem=ngsem.at[1, 4],
            device_id={"patch": p + 1 - 2 * core},
            device_id_type=MESH,
        )

    for i in range(1, 4):
        gather_x(i, False).start()

    def pick(ref, i):
        return jnp.where(clip_t == 0, ref[i, 0:1, :], ref[i, 1:2, :])

    shift_t, stretch_t = pick(mod_t, 0), pick(mod_t, 1)

    def spread_rows(a):
        parts = []
        for yy in range(4):
            for zz in range(4):
                at = 36 * (4 * zz + yy)
                parts += [a[:, at : at + 36], zeros(128, 4, dtype=BF)]
        return parts

    def core_columns(full, cc):
        parts = [full[:, HD * (2 * b + cc) : HD * (2 * b + cc) + HD] for b in range(8)]
        return jnp.concatenate(parts + [zeros(128, 64, dtype=BF)], axis=-1)

    xl[1, core] = jnp.concatenate(spread_rows(att_s[...]), axis=-1)
    for cc in range(2):
        xrv[0, cc] = core_columns(scaled[...].reshape(128, D), cc)
    xr[0, core] = xrv[0, core]

    def pair_copies(which, slot):
        there = {"patch": p + 1 - 2 * core}
        pairs = ((xl.at[which, core], xl), (xrv.at[which, 1 - core], xr))
        return [
            pltpu.make_async_remote_copy(
                src_ref=src,
                dst_ref=dst.at[which, slot],
                send_sem=xsem.at[0, 2 * which + i],
                recv_sem=xsem.at[1, 2 * which + i],
                device_id=there,
                device_id_type=MESH,
            )
            for i, (src, dst) in enumerate(pairs)
        ]

    for part in range(4):
        at = pl.ds(256 * part, 256)
        kt_b[:, at] = jnp.transpose(widen(k_b[at, :].astype(F32), 128)).astype(BF)
    loads[3].wait()
    ex_t1.wait()
    middle = unfold(t1_r[...].astype(F32), D).reshape(128, D)
    xh_t, r_t = normalise(middle)
    normed_t = (xh_t * (1.0 + stretch_t) + shift_t).astype(BF)
    xn[4 * core + x] = normed_t

    def normed_x(i, back):
        block = 4 * core + (lax.rem(x + 4 - i, 4) if back else x)
        return pltpu.make_async_remote_copy(
            src_ref=xn.at[block],
            dst_ref=xn.at[block],
            send_sem=xnsem.at[0, i],
            recv_sem=xnsem.at[1, i],
            device_id=on_x(lax.rem(x + i, 4)),
            device_id_type=MESH,
        )

    def normed_core(back):
        side = pl.ds(4 * (1 - core if back else core), 4)
        return pltpu.make_async_remote_copy(
            src_ref=xn.at[side],
            dst_ref=xn.at[side],
            send_sem=xnsem.at[0, 0],
            recv_sem=xnsem.at[1, 0],
            device_id={"patch": p + 1 - 2 * core},
            device_id_type=MESH,
        )

    for i in range(1, 4):
        normed_x(i, False).start()
    proj[...] = nt(normed_t, wqt[...])
    same = lax.rem(lax.broadcasted_iota(jnp.int32, (128, 128), 0), 8) == lax.rem(
        lax.broadcasted_iota(jnp.int32, (128, 128), 1), 8
    )
    heads, att_parts, dq_parts, dk_parts, dv_parts = [], [], [], [], []
    for h in range(HEADS):
        q = proj[:, HD * h : HD * h + HD]
        k = proj[:, ATT + HD * h : ATT + HD * h + HD]
        v = proj[:, 2 * ATT + HD * h : 2 * ATT + HD * h + HD].astype(BF)
        rq = inverse_norm(q)
        rk = inverse_norm(k)
        q = q * rq
        k = k * rk
        e = nt(q.astype(BF), k.astype(BF)) * (SCALE * LOG2E)
        e = jnp.where(same, jnp.exp2(e), 0.0)
        soft = e * (1.0 / jnp.sum(e, axis=-1, keepdims=True))
        att_parts.append(nn(soft.astype(BF), v))
        heads.append((q, k, v, rq, rk, soft))
    att_t = jnp.concatenate(att_parts, axis=-1)
    c2_s[...] = fold(att_t.reshape(16, 8, ATT), 384).astype(BF)
    ex_c2.start()
    ex_t2.wait()
    dout_t = unfold(t2_r[...].astype(F32), ATT).reshape(128, ATT)
    for h, (q, k, v, rq, rk, soft) in enumerate(heads):
        do = dout_t[:, HD * h : HD * h + HD].astype(BF)
        dp = nt(do, v)
        ds = (soft * (dp - jnp.sum(dp * soft, axis=-1, keepdims=True)) * SCALE).astype(BF)
        dq_parts.append(head_back(rounded(nn(ds, k.astype(BF))), q, rq))
        dk_parts.append(head_back(rounded(tn(ds, q.astype(BF))), k, rk))
        dv_parts.append(tn(soft.astype(BF), do))
    parts = [part.astype(BF) for part in dq_parts + dk_parts + dv_parts]
    dproj_t = jnp.concatenate(parts, axis=-1)
    dn = nn(dproj_t, wqt[...])
    back = normalise_back(dn, stretch_t, xh_t, r_t)
    dm_s[...] = fold(back.reshape(16, 8, D), 640).astype(BF)
    ex_dm.start()

    for cc in range(2):
        for xx in range(4):
            at = 108 * (4 * xx + cc)
            row = [dproj_t[:, at : at + 108], zeros(128, 20, dtype=BF)]
            row += [dproj_t[:, at + 216 : at + 324], zeros(128, 20, dtype=BF)]
            dt_s[4 * cc + xx] = jnp.concatenate(row, axis=-1)
    ex_dt.start()

    ex_c2.wait()
    att_t = unfold(c2_r[...].astype(F32), ATT).reshape(128, ATT)
    xl[0, core] = jnp.concatenate(spread_rows(att_t.astype(BF)), axis=-1)
    for copy in pair_copies(0, core):
        copy.start()
    for i in range(1, 4):
        gather_x(i, True).wait()
    gather_core(False).start()
    for copy in pair_copies(0, 1 - core):
        copy.wait()
    lt[...] = jnp.transpose(xl[0].reshape(256, 640).astype(F32)).astype(BF)
    g = nn(lt[...], xr[0].reshape(256, 640))
    for yy in range(4):
        syo[yy] = g[160 * yy : 160 * yy + 160].astype(BF)
    ex_yo.start()
    gather_core(True).wait()
    for i in range(8):
        block = ng[i // 4, i % 4].reshape(128, D).astype(F32)
        block = jnp.transpose(block).reshape(4, 4, HD, 128)
        for yy in range(4):
            rows = block[:, yy].reshape(288, 128)
            ngt[288 * yy : 288 * yy + 288, 128 * i : 128 * i + 128] = rows.astype(BF)

    ex_dm.wait()
    back = unfold(dm_r[...].astype(F32), D).reshape(2, 64, D)
    parts = []
    for c in range(2):
        total = rounded(cot[c].astype(F32) + back[c])
        dmid[c] = total.astype(BF)
        parts.append((total * mod_s[2, c : c + 1, :]).astype(BF))
    scaled_s = jnp.concatenate(parts, axis=0)
    tokens = nt(scaled_s, wos[...]).astype(BF).reshape(2, 64, ATT)
    for c in range(2):
        for h in range(HEADS):
            part = tokens[c][:, HD * h : HD * h + HD].reshape(4, 16, HD)
            row = [part[j] for j in range(4)] + [zeros(16, 96, dtype=BF)]
            c1_s[owner(c, h)] = jnp.concatenate(row, axis=-1)
    ex_c1.start()

    for cc in range(2):
        xrv[1, cc] = core_columns(scaled_s, cc)
    xr[1, core] = xrv[1, core]
    for copy in pair_copies(1, core):
        copy.start()
    for i in range(1, 4):
        normed_x(i, True).wait()
    normed_core(False).start()
    for copy in pair_copies(1, 1 - core):
        copy.wait()
    lt[...] = jnp.transpose(xr[1].reshape(256, 640).astype(F32)).astype(BF)
    g = nn(lt[...], xl[1].reshape(256, 640))
    for i in range(4):
        sxs[i] = g[144 * i : 144 * i + 144].astype(BF)
    ex_xs.start()
    normed_core(True).wait()
    ex_dt.wait()
    g = tn(xn[...].reshape(1024, D), dt_r[...].reshape(1024, 256)).reshape(4, 4, HD, 256)
    for yy in range(4):
        syq[yy] = g[:, yy].reshape(288, 256).astype(BF)
    ex_yq.start()
    ex_c1.wait()
    got_do = c1_r[...]
    parts = [got_do[:, :, HD * j : HD * j + HD] for j in range(4)]
    do_b[...] = (jnp.stack(parts, axis=1).reshape(1024, HD).astype(F32) * rl[...]).astype(BF)
    dk_f[...] = jnp.zeros_like(dk_f)
    dv_f[...] = jnp.zeros_like(dv_f)

    def attend_back(i, carry):
        part = lax.rem(lax.div(x, 2) + 1 + i, 2)
        at = pl.ds(pl.multiple_of(part * 512, 512), 512)
        qb, dob = q_b[at, :], do_b[at, :]
        e = jnp.exp2(nt(k_b[...], qb) * (SCALE * LOG2E))
        dp = nt(v_b[...], dob)
        shift = rrow[:, at] * jnp.sum(dp * e, axis=0, keepdims=True)
        ds = (e * (dp - shift)).astype(BF)
        dv_f[...] += nn(e.astype(BF), dob)
        dk_f[...] += nn(ds, qb)
        dq = rounded(jnp.transpose(nn(kt_b[...], ds))[:, :HD] * SCALE)
        dq = head_back(dq, qb.astype(F32), rqk[at, 0:1]).astype(BF)
        blocks = pl.ds(8 * part, 8)
        dgq[blocks] = dq.reshape(8, 64, HD)
        dq = dq.reshape(8, 4, 16, HD)
        row = [dq[:, j].reshape(128, HD) for j in range(4)] + [zeros(128, 96, dtype=BF)]
        dq_s[blocks] = jnp.concatenate(row, axis=-1).reshape(8, 16, 384)
        for j in range(8):
            to = 8 * part + j

            @pl.when(to != p)
            def _():
                ex_dq.copy(to, p).start()

        return carry

    lax.fori_loop(0, 2, attend_back, 0)
    dq_r[p] = dq_s[p]
    for part in range(4):
        at = pl.ds(256 * part, 256)
        dk = head_back(rounded(dk_f[at, :] * SCALE), k_b[at, :].astype(F32), rqk[at, 1:2])
        row = jnp.concatenate([dk.astype(BF), dv_f[at, :].astype(BF)], axis=-1)
        dg[4 * part : 4 * part + 4] = row.reshape(4, 64, 2 * HD)
        row = row.reshape(4, 4, 16, 2 * HD)
        row = [row[:, j].reshape(64, 2 * HD) for j in range(4)] + [zeros(64, 64, dtype=BF)]
        d_s[4 * part : 4 * part + 4] = jnp.concatenate(row, axis=-1).reshape(4, 16, 640)
    ex_d.start()

    order = [4 * xx + 2 * s + cc for cc in range(2) for xx in range(4) for s in range(2)]
    right = [jnp.concatenate([ref[i] for i in order], axis=0) for ref in (dgq, dg)]
    right = jnp.concatenate(right + [zeros(1024, 8, dtype=BF)], axis=-1)
    for i in range(1, 5):
        yy = lax.rem(y + i, 4)
        rows = pl.ds(pl.multiple_of(288 * yy, 288), 288)
        gys[yy] = nn(ngt[rows, :], right).astype(BF)
        if i < 4:
            ex_gy.copy(yy, y).start()
    gyr[y] = gys[y]
    ex_yo.wait()
    total = sum(ryo[i].astype(F32) for i in range(4))
    for i in range(4):
        sxo[i] = widen(total[:, 144 * i : 144 * i + 144], 256).astype(BF)
    ex_xo.start()
    ex_xs.wait()
    total = sum(rxs[i].astype(F32) for i in range(4))
    for i in range(4):
        part = total[:, 160 * i : 160 * i + 160]
        rest = [part[48 * j : 48 * j + 48, 128:] for j in range(3)] + [zeros(48, 32)]
        rest = jnp.concatenate(rest, axis=-1)
        sys[i] = jnp.concatenate([part[:, :128], rest], axis=0).astype(BF)
    ex_ys.start()
    ex_yq.wait()
    total = sum(ryq[i].astype(F32) for i in range(4))
    for i in range(8):
        zz, s = i % 4, i // 4
        part = total[HD * zz : HD * zz + HD, 128 * s : 128 * s + 108]
        rest = [part[64:, 18 * j : 18 * j + 18] for j in range(6)] + [zeros(16, 18)]
        rest = jnp.concatenate(rest, axis=0)
        szq[i] = jnp.concatenate([part[:64], rest, zeros(64, 2)], axis=-1).astype(BF)
    ex_zq.start()


    ex_gy.wait()
    total = sum(gyr[i].astype(F32) for i in range(4)).reshape(4, 3, 24, 224)
    for b in range(6):
        cols = [total[:, r, :, 36 * b : 36 * b + 36] for r in range(3)] + [zeros(4, 24, 20)]
        cols = jnp.concatenate(cols, axis=-1)
        fs[:, b] = jnp.concatenate([cols, zeros(4, 8, 128)], axis=1).astype(BF)

    def piece(i, b):
        to_z = lax.rem(zl + i, 4)
        block = 16 * (b // 2) + 2 * head + b % 2
        to, slot = lax.div(block, 3), lax.rem(block, 3)
        copy = pltpu.make_async_remote_copy(
            src_ref=fs.at[to_z, b],
            dst_ref=fr.at[slot, z],
            send_sem=fs_sem.at[b if i == 0 else 6],
            recv_sem=fr_sem.at[2 * slot + zh if i == 0 else 6],
            device_id={"frame": 4 * to_z + y, "patch": to},
            device_id_type=MESH,
        )
        return to, slot, copy

    for i in range(4):
        for b in range(6):
            to, slot, copy = piece(i, b)
            if i > 0:
                copy.start()
            else:

                @pl.when(to != p)
                def _():
                    copy.start()

                @pl.when(to == p)
                def _():
                    fr[slot, z] = fs[zl, b]

    ex_xo.wait()
    ex_ys.wait()
    total = sum(rxo[i].astype(F32) for i in range(4))
    other = sum(rys[i].astype(F32) for i in range(4))
    rest = jnp.concatenate([other[144:, 32 * j : 32 * j + 32] for j in range(3)], axis=0)
    other = widen(jnp.concatenate([other[:144], rest], axis=-1), 256)
    other = jnp.transpose(jnp.concatenate([other, zeros(112, 256)], axis=0))
    for i in range(8):
        zz, s = i % 4, i // 4
        rows, cols = slice(40 * zz, 40 * zz + 36), slice(HD * s, HD * s + HD)
        part = jnp.concatenate([total[rows, cols], other[rows, cols]], axis=0)
        rest = jnp.concatenate([part[48:, :36], part[48:, 36:]], axis=0)
        szo[i] = jnp.concatenate([part[:48], rest, zeros(48, 20)], axis=-1).astype(BF)
    ex_zo.start()

    ex_dq.wait()
    ex_d.wait()
    parts = []
    for c in range(2):
        firsts = [dq_r[owner(c, h)] for h in range(HEADS)]
        blocks = [d_r[owner(c, h)] for h in range(HEADS)]
        for i in range(4):
            row = [b[:, HD * i : HD * i + HD] for b in firsts]
            at = [2 * HD * i + HD * j for j in range(2)]
            row += [b[:, a : a + HD] for a in at for b in blocks]
            parts.append(jnp.concatenate(row, axis=-1))
    dn = nn(jnp.concatenate(parts, axis=0), wqs[...])
    for c in range(2):
        xh, r = normalise(lat[c].astype(F32))
        back = normalise_back(dn[64 * c : 64 * c + 64], mod_s[1, c : c + 1, :], xh, r)
        gl[c] = (dmid[c].astype(F32) + back).astype(BF)
    writes[0].start()


    ex_zq.wait()
    total = sum(rzq[i].astype(F32) for i in range(8))
    rest = [total[8 * j : 8 * j + 8, 108:126] for j in range(6)]
    rest = jnp.concatenate(rest, axis=-1)
    gqt[...] = jnp.concatenate([total[:, :108], rest], axis=0)
    writes[1].start()
    ex_zo.wait()
    total = sum(rzo[i].astype(F32) for i in range(8))
    rest = jnp.concatenate([total[:24, 72:108], total[24:, 72:108]], axis=-1)
    total = jnp.concatenate([total[:, :HD], rest], axis=0)
    got[...] = total[:36]
    gos[...] = total[36:]
    writes[2].start()
    writes[3].start()

    for b in range(6):
        to, slot, copy = piece(0, b)

        @pl.when(to != p)
        def _():
            copy.wait_send()

    for slot in range(3):
        left = lax.rem(3 * p + slot, 16)
        source = lax.div(left, 4) * 4 + lax.rem(lax.div(left, 2), 2)
        for c in range(2):
            at = 4 * c + zl
            copy = pltpu.make_async_remote_copy(
                src_ref=fs.at[0, 0],
                dst_ref=fr.at[slot, at],
                send_sem=fs_sem.at[0],
                recv_sem=fr_sem.at[2 * slot + c],
                device_id={"patch": source + 2 * c},
                device_id_type=MESH,
            )

            @pl.when(source + 2 * c != p)
            def _():
                copy.wait_recv()

    for ref, sem in ((fs.at[pl.ds(0, 3)], fs_sem.at[6]), (fr.at[:, pl.ds(0, 6)], fr_sem.at[6])):
        pltpu.make_async_copy(ref, ref, sem).wait()

    cols = []
    for slot in range(3):
        total = sum(fr[slot, i].astype(F32) for i in range(8))
        cols.append(
            jnp.concatenate([total[:24, 36 * r : 36 * r + 36] for r in range(3)], axis=0)
        )
    gqs[...] = jnp.concatenate(cols, axis=-1)
    writes[4].start()
    for write in writes:
        write.wait()


def hand_over(*refs):
    given, out, held, sem = refs[:5], refs[5:10], refs[10:15], refs[15]
    into = [pltpu.make_async_copy(given[i], held[i], sem.at[0, i]) for i in range(5)]
    back = [pltpu.make_async_copy(held[i], out[i], sem.at[1, i]) for i in range(5)]
    for copy in into:
        copy.start()
    for i in range(5):
        into[i].wait()
        back[i].start()
    for copy in back:
        copy.wait()


def body(lat, mod_s, mod_t, wqs, wos, wqt, wot, cot):
    hbm = pl.BlockSpec(memory_space=pl.ANY)
    dma = pltpu.SemaphoreType.DMA

    def buf(*shape):
        return pltpu.VMEM(shape, BF)

    def wide(*shape):
        return pltpu.VMEM(shape, F32)

    outs = pl.pallas_call(
        kernel,
        out_shape=(
            jax.ShapeDtypeStruct((2, 64, D), BF),
            jax.ShapeDtypeStruct((72, 108), F32),
            jax.ShapeDtypeStruct((36, 72), F32),
            jax.ShapeDtypeStruct((72, 108), F32),
            jax.ShapeDtypeStruct((36, 72), F32),
        ),
        in_specs=[hbm] * 8,
        out_specs=(hbm,) * 5,
        scratch_shapes=[
            buf(2, 64, D), buf(2, 64, D), wide(3, 2, D), wide(3, 2, D),
            buf(2, 64, D), wide(72, 108), wide(36, 72), wide(72, 108), wide(36, 72), dma((9,)),
            buf(QKV, D), buf(ATT, D), buf(QKV, D), buf(ATT, D), dma((4,)),
            buf(2, 64, D), wide(128, QKV),
            buf(16, 16, 896), buf(16, 16, 896),
            buf(16, 16, 384), buf(16, 16, 384),
            buf(128, ATT), buf(2, 64, D), buf(2, 64, D),
            buf(16, 16, 640), buf(16, 16, 640),
            buf(16, 16, 384), buf(16, 16, 384),
            buf(16, 16, 384), buf(16, 16, 384),
            buf(16, 16, 384), buf(16, 16, 384),
            buf(16, 16, 640), buf(16, 16, 640),
            buf(16, 16, 384), buf(16, 16, 384), buf(16, 16, 640), buf(16, 16, 640),
            buf(16, 64, HD), buf(16, 64, 2 * HD), buf(1152, 1024),
            dma((9, 2)),
            buf(1024, HD), buf(1024, HD), buf(1024, HD), wide(1024, 2), wide(1024, 1), wide(1, 1024),
            buf(1024, HD), buf(128, 1024), wide(1024, HD), wide(1024, HD),
            buf(2, 4, 2, 64, D), dma((2, 5)),
            buf(8, 128, D), dma((2, 4)), buf(8, 128, 256), buf(8, 128, 256), dma((2,)),
            buf(2, 2, 128, 640), buf(2, 2, 128, 640), buf(2, 2, 128, 640), dma((2, 4)),
            buf(640, 256),
            buf(4, 288, 256), buf(4, 288, 256),
            buf(4, 160, 640), buf(4, 160, 640),
            buf(4, 160, 256), buf(4, 160, 256),
            buf(4, 144, 640), buf(4, 144, 640),
            buf(4, 192, 128), buf(4, 192, 128),
            buf(4, 288, 224), buf(4, 288, 224),
            dma((6, 2)),
            buf(8, 64, 128), buf(8, 64, 128),
            buf(8, 48, 128), buf(8, 48, 128),
            dma((2, 2)),
            buf(4, 6, 32, 128), buf(3, 8, 32, 128), dma((7,)), dma((7,)),
        ],
        compiler_params=pltpu.CompilerParams(
            collective_id=0, has_side_effects=True, vmem_limit_bytes=60 * 1024 * 1024
        ),
    )(
        lat.reshape(2, 64, D),
        cot.reshape(2, 64, D),
        mod_s.transpose(1, 0, 2),
        mod_t.transpose(1, 0, 2),
        wqs.T,
        wos,
        wqt.T,
        wot,
    )
    outs = pl.pallas_call(
        hand_over,
        out_shape=tuple(jax.ShapeDtypeStruct(o.shape, o.dtype) for o in outs),
        in_specs=[hbm] * 5,
        out_specs=(hbm,) * 5,
        scratch_shapes=[pltpu.VMEM(o.shape, o.dtype) for o in outs] + [dma((2, 5))],
    )(*outs)
    return (outs[0].reshape(2, 1, 64, D),) + tuple(outs[1:])


def solution(mesh):
    tokens = P(None, "frame", "patch", None)
    return jax.shard_map(
        body,
        mesh=mesh,
        in_specs=(tokens,) + (P(),) * 6 + (tokens,),
        out_specs=(tokens,) + (P("frame", "patch"),) * 4,
        check_vma=False,
    )
```

```python
import jax
import jax.numpy as jnp
from jax import lax
from jax.experimental import pallas as pl
from jax.experimental.pallas import tpu as pltpu
from jax.sharding import PartitionSpec as P

F32 = jnp.float32
BF = jnp.bfloat16
MESH = pl.DeviceIdType.MESH
HD = 72
HEADS = 8
ATT = 576
D = 1152
QKV = 1728
EPS = 1e-06
SCALE = HD**-0.5
LOG2E = 1.4426950408889634


def nn(a, b):
    return lax.dot_general(a, b, (((1,), (0,)), ((), ())), preferred_element_type=F32)


def nt(a, b):
    return lax.dot_general(a, b, (((1,), (1,)), ((), ())), preferred_element_type=F32)


def tn(a, b):
    return lax.dot_general(a, b, (((0,), (0,)), ((), ())), preferred_element_type=F32)


def owner(c, h):
    return (h // 2) * 4 + c * 2 + h % 2


def normalise(x):
    centre = x - jnp.mean(x, axis=-1, keepdims=True)
    r = lax.rsqrt(jnp.mean(centre * centre, axis=-1, keepdims=True) + EPS)
    return centre * r, r


def normalise_back(dn, stretch, xh, r):
    dx = dn * (1.0 + stretch)
    dx = dx - xh * jnp.mean(dx * xh, axis=-1, keepdims=True)
    dx = r * dx
    return dx - jnp.mean(dx, axis=-1, keepdims=True)


def inverse_norm(x):
    return lax.rsqrt(jnp.sum(x * x, axis=-1, keepdims=True) * (1.0 / HD) + EPS)


def head_back(dy, y, r):
    return r * (dy - y * (jnp.sum(dy * y, axis=-1, keepdims=True) * (1.0 / HD)))


def rounded(x):
    return x.astype(BF).astype(F32)


def zeros(*shape, dtype=F32):
    return jnp.zeros(shape, dtype)


def fold(x, near):
    n, _, w = x.shape
    far = x[:, :, near:]
    pad = 2 * near - w
    far = jnp.concatenate([far, zeros(n, 8, pad)], axis=-1)
    return jnp.concatenate([x[:, :, :near], far], axis=1)


def unfold(x, w):
    near = x.shape[-1]
    return jnp.concatenate([x[:, :8, :], x[:, 8:, : w - near]], axis=-1)


def widen(x, width):
    return jnp.concatenate([x, zeros(x.shape[0], width - x.shape[1], dtype=x.dtype)], axis=-1)


class Exchange:
    def __init__(self, send, recv, ssem, rsem, n, me, place):
        self.send, self.recv, self.ssem, self.rsem = send, recv, ssem, rsem
        self.n, self.me, self.place = n, me, place

    def copy(self, to, slot):
        return pltpu.make_async_remote_copy(
            src_ref=self.send.at[to],
            dst_ref=self.recv.at[slot],
            send_sem=self.ssem,
            recv_sem=self.rsem,
            device_id=self.place(to),
            device_id_type=MESH,
        )

    def start(self):
        def step(i, carry):
            self.copy(lax.rem(self.me + i, self.n), self.me).start()
            return carry

        lax.fori_loop(1, self.n, step, 0)
        self.recv[self.me] = self.send[self.me]

    def wait(self):
        for ref, sem in ((self.send, self.ssem), (self.recv, self.rsem)):
            blocks = ref.at[pl.ds(0, self.n - 1)]
            pltpu.make_async_copy(blocks, blocks, sem).wait()


def kernel(
    lat_h, cot_h, mod_s_h, mod_t_h, wqs_h, wos_h, wqt_h, wot_h,
    gl_h, gqs_h, gos_h, gqt_h, got_h,
    lat, cot, mod_s, mod_t, gl, gqs, gos, gqt, got, iosem,
    wqs, wos, wqt, wot, wsem,
    normed, proj,
    a_s, a_r, b1_s, b1_r, att_s, scaled, dmid, t1_s, t1_r, t2_s, t2_r,
    c2_s, c2_r, c1_s, c1_r, dm_s, dm_r, dq_s, dq_r, d_s, d_r, dgq, dg, ngt, xsems,
    q_b, k_b, v_b, rqk, rl, rrow, do_b, kt_b, dk_f, dv_f,
    ng, ngsem, xn, xnsem, dt_s, dt_r, dtsem,
    xl, xrv, xr, xsem, lt,
    syq, ryq, syo, ryo, sxo, rxo, sxs, rxs, sys, rys, gys, gyr, sem4,
    szq, rzq, szo, rzo, sem8,
    fs, fr, fs_sem, fr_sem,
):
    f = lax.axis_index("frame")
    p = lax.axis_index("patch")
    core = lax.rem(p, 2)
    zh = lax.rem(lax.div(p, 2), 2)
    x = lax.div(p, 4)
    y = lax.rem(f, 4)
    zl = lax.div(f, 4)
    head = 2 * x + core
    clip_t = lax.div(f, 8)
    z = zh * 4 + zl

    loads = [
        pltpu.make_async_copy(src, dst, wsem.at[i])
        for i, (src, dst) in enumerate(
            ((wqs_h, wqs), (wot_h, wot), (wos_h, wos), (wqt_h, wqt))
        )
    ]
    reads = [
        pltpu.make_async_copy(src, dst, iosem.at[i])
        for i, (src, dst) in enumerate(
            ((lat_h, lat), (mod_s_h, mod_s), (cot_h, cot), (mod_t_h, mod_t))
        )
    ]
    writes = [
        pltpu.make_async_copy(src, dst, iosem.at[4 + i])
        for i, (src, dst) in enumerate(
            ((gl, gl_h), (gqt, gqt_h), (got, got_h), (gos, gos_h), (gqs, gqs_h))
        )
    ]
    for read in reads[:2]:
        read.start()
    loads[0].start()
    for read in reads[2:]:
        read.start()

    barrier = pltpu.get_barrier_semaphore()

    def greet(i, carry):
        pl.semaphore_signal(
            barrier, inc=1, device_id={"frame": lax.rem(f + i, 16)}, device_id_type=MESH
        )
        pl.semaphore_signal(
            barrier, inc=1, device_id={"patch": lax.rem(p + i, 16)}, device_id_type=MESH
        )
        return carry

    lax.fori_loop(1, 16, greet, 0)

    def greet_far(i, carry):
        pl.semaphore_signal(
            barrier,
            inc=1,
            device_id={
                "frame": 4 * lax.rem(zl + 1 + lax.div(i, 15), 4) + y,
                "patch": lax.rem(p + 1 + lax.rem(i, 15), 16),
            },
            device_id_type=MESH,
        )
        return carry

    lax.fori_loop(0, 45, greet_far, 0)

    def on_patch(i):
        return {"patch": i}

    def on_frame(i):
        return {"frame": i}

    def on_x(i):
        return {"patch": 4 * i + 2 * zh + core}

    def on_y(i):
        return {"frame": 4 * zl + i}

    def on_column(i):
        return {"patch": 4 * lax.rem(i, 4) + 2 * zh + lax.div(i, 4)}

    def on_z(i):
        return {
            "frame": 4 * lax.rem(i, 4) + y,
            "patch": 4 * x + 2 * lax.div(i, 4) + core,
        }

    ex_a = Exchange(a_s, a_r, xsems.at[0, 0], xsems.at[0, 1], 16, p, on_patch)
    ex_b1 = Exchange(b1_s, b1_r, xsems.at[1, 0], xsems.at[1, 1], 16, p, on_patch)
    ex_t1 = Exchange(t1_s, t1_r, xsems.at[3, 0], xsems.at[3, 1], 16, f, on_frame)
    ex_t2 = Exchange(t2_s, t2_r, xsems.at[4, 0], xsems.at[4, 1], 16, f, on_frame)
    ex_c2 = Exchange(c2_s, c2_r, xsems.at[5, 0], xsems.at[5, 1], 16, f, on_frame)
    ex_c1 = Exchange(c1_s, c1_r, xsems.at[6, 0], xsems.at[6, 1], 16, p, on_patch)
    ex_dm = Exchange(dm_s, dm_r, xsems.at[7, 0], xsems.at[7, 1], 16, f, on_frame)
    ex_dq = Exchange(dq_s, dq_r, xsems.at[2, 0], xsems.at[2, 1], 16, p, on_patch)
    ex_d = Exchange(d_s, d_r, xsems.at[8, 0], xsems.at[8, 1], 16, p, on_patch)
    ex_dt = Exchange(dt_s, dt_r, dtsem.at[0], dtsem.at[1], 8, 4 * core + x, on_column)
    ex_yq = Exchange(syq, ryq, sem4.at[0, 0], sem4.at[0, 1], 4, y, on_y)
    ex_yo = Exchange(syo, ryo, sem4.at[1, 0], sem4.at[1, 1], 4, y, on_y)
    ex_xo = Exchange(sxo, rxo, sem4.at[2, 0], sem4.at[2, 1], 4, x, on_x)
    ex_xs = Exchange(sxs, rxs, sem4.at[4, 0], sem4.at[4, 1], 4, x, on_x)
    ex_ys = Exchange(sys, rys, sem4.at[5, 0], sem4.at[5, 1], 4, y, on_y)
    ex_gy = Exchange(gys, gyr, sem4.at[3, 0], sem4.at[3, 1], 4, y, on_y)
    ex_zq = Exchange(szq, rzq, sem8.at[0, 0], sem8.at[0, 1], 8, z, on_z)
    ex_zo = Exchange(szo, rzo, sem8.at[1, 0], sem8.at[1, 1], 8, z, on_z)

    reads[0].wait()
    reads[1].wait()
    for c in range(2):
        xh, _ = normalise(lat[c].astype(F32))
        normed[c] = (xh * (1.0 + mod_s[1, c : c + 1, :]) + mod_s[0, c : c + 1, :]).astype(BF)
    loads[0].wait()
    for load in loads[1:]:
        load.start()
    proj[...] = nt(normed[...].reshape(128, D), wqs[...])
    lane = lax.broadcasted_iota(jnp.int32, (128, 224), 1)
    for h in range(HEADS):
        q = proj[:, HD * h : HD * h + HD]
        k = proj[:, ATT + HD * h : ATT + HD * h + HD]
        v = proj[:, 2 * ATT + HD * h : 2 * ATT + HD * h + HD]
        rq = inverse_norm(q)
        rk = inverse_norm(k)
        row = jnp.concatenate([q * rq, k * rk, v, zeros(128, 8)], axis=-1)
        row = jnp.where(lane == 216, rq, row)
        row = jnp.where(lane == 217, rq - rounded(rq), row)
        row = jnp.where(lane == 218, rk, row)
        row = jnp.where(lane == 219, rk - rounded(rk), row)
        row = row.astype(BF).reshape(2, 4, 16, 224)
        for c in range(2):
            quarters = [row[c, j] for j in range(4)]
            a_s[owner(c, h)] = jnp.concatenate(quarters, axis=-1)
    pl.semaphore_wait(barrier, 75)
    ex_a.start()

    reads[2].wait()
    reads[3].wait()
    loads[1].wait()
    for c in range(2):
        scaled[c] = (cot[c].astype(F32) * mod_t[2, c : c + 1, :]).astype(BF)
    dout = nt(scaled[...].reshape(128, D), wot[...])
    for c in range(2):
        part = dout[64 * c : 64 * c + 64].reshape(8, 8, ATT)
        t2_s[8 * c : 8 * c + 8] = fold(part, 384).astype(BF)
    ng[core, x, zh] = normed[zh]
    gather_z = pltpu.make_async_remote_copy(
        src_ref=normed.at[1 - zh],
        dst_ref=ng.at[core, x, zh],
        send_sem=ngsem.at[0, 0],
        recv_sem=ngsem.at[1, 0],
        device_id={"patch": 4 * x + 2 * (1 - zh) + core},
        device_id_type=MESH,
    )
    ex_t2.start()
    ex_a.wait()
    gather_z.start()

    for part in range(4):
        rows = a_r[4 * part : 4 * part + 4]
        rows = [rows[:, :, 224 * j : 224 * j + 224] for j in range(4)]
        rows = jnp.stack(rows, axis=1).reshape(256, 224)
        at = pl.ds(256 * part, 256)
        q_b[at, :] = rows[:, 0:HD]
        k_b[at, :] = rows[:, HD : 2 * HD]
        v_b[at, :] = rows[:, 2 * HD : 3 * HD]
        r = rows[:, 216:220].astype(F32)
        rqk[at, 0:1] = r[:, 0:1] + r[:, 1:2]
        rqk[at, 1:2] = r[:, 2:3] + r[:, 3:4]

    def attend(i, carry):
        part = lax.rem(x + 1 + i, 4)
        at = pl.ds(pl.multiple_of(part * 256, 256), 256)
        e = jnp.exp2(nt(q_b[at, :], k_b[...]) * (SCALE * LOG2E))
        r = 1.0 / jnp.sum(e, axis=-1, keepdims=True)
        rl[at, :] = r
        pieces = (nn(e.astype(BF), v_b[...]) * r).astype(BF).reshape(4, 4, 16, HD)
        row = [pieces[:, j].reshape(64, HD) for j in range(4)] + [zeros(64, 96, dtype=BF)]
        row = jnp.concatenate(row, axis=-1).reshape(4, 16, 384)
        b1_s[pl.ds(4 * part, 4)] = row
        for j in range(4):
            to = 4 * part + j

            @pl.when(to != p)
            def _():
                ex_b1.copy(to, p).start()

        return carry

    lax.fori_loop(0, 4, attend, 0)
    b1_r[p] = b1_s[p]
    for part in range(4):
        at = pl.ds(256 * part, 256)
        rrow[:, at] = jnp.transpose(widen(rl[at, :], 128))[0:1, :]
    loads[2].wait()
    ex_b1.wait()
    atts = []
    for c in range(2):
        blocks = [b1_r[owner(c, h)] for h in range(HEADS)]
        rows = [
            jnp.concatenate([b[:, HD * j : HD * j + HD] for b in blocks], axis=-1)
            for j in range(4)
        ]
        atts.append(jnp.concatenate(rows, axis=0))
    att_s[...] = jnp.concatenate(atts, axis=0)
    added = nn(att_s[...], wos[...])
    for c in range(2):
        middle = lat[c].astype(F32) + mod_s[2, c : c + 1, :] * added[64 * c : 64 * c + 64]
        t1_s[8 * c : 8 * c + 8] = fold(middle.reshape(8, 8, D), 640).astype(BF)
    ex_t1.start()

    gather_z.wait()

    def gather_x(i, back):
        block = lax.rem(x + 4 - i, 4) if back else x
        return pltpu.make_async_remote_copy(
            src_ref=ng.at[core, block],
            dst_ref=ng.at[core, block],
            send_sem=ngsem.at[0, i],
            recv_sem=ngsem.at[1, i],
            device_id=on_x(lax.rem(x + i, 4)),
            device_id_type=MESH,
        )

    def gather_core(back):
        side = 1 - core if back else core
        return pltpu.make_async_remote_copy(
            src_ref=ng.at[side],
            dst_ref=ng.at[side],
            send_sem=ngsem.at[0, 4],
            recv_sem=ngsem.at[1, 4],
            device_id={"patch": p + 1 - 2 * core},
            device_id_type=MESH,
        )

    for i in range(1, 4):
        gather_x(i, False).start()

    def pick(ref, i):
        return jnp.where(clip_t == 0, ref[i, 0:1, :], ref[i, 1:2, :])

    shift_t, stretch_t = pick(mod_t, 0), pick(mod_t, 1)

    def spread_rows(a):
        parts = []
        for yy in range(4):
            for zz in range(4):
                at = 36 * (4 * zz + yy)
                parts += [a[:, at : at + 36], zeros(128, 4, dtype=BF)]
        return parts

    def core_columns(full, cc):
        parts = [full[:, HD * (2 * b + cc) : HD * (2 * b + cc) + HD] for b in range(8)]
        return jnp.concatenate(parts + [zeros(128, 64, dtype=BF)], axis=-1)

    xl[1, core] = jnp.concatenate(spread_rows(att_s[...]), axis=-1)
    for cc in range(2):
        xrv[0, cc] = core_columns(scaled[...].reshape(128, D), cc)
    xr[0, core] = xrv[0, core]

    def pair_copies(which, slot):
        there = {"patch": p + 1 - 2 * core}
        pairs = ((xl.at[which, core], xl), (xrv.at[which, 1 - core], xr))
        return [
            pltpu.make_async_remote_copy(
                src_ref=src,
                dst_ref=dst.at[which, slot],
                send_sem=xsem.at[0, 2 * which + i],
                recv_sem=xsem.at[1, 2 * which + i],
                device_id=there,
                device_id_type=MESH,
            )
            for i, (src, dst) in enumerate(pairs)
        ]

    for part in range(4):
        at = pl.ds(256 * part, 256)
        kt_b[:, at] = jnp.transpose(widen(k_b[at, :].astype(F32), 128)).astype(BF)
    loads[3].wait()
    ex_t1.wait()
    middle = unfold(t1_r[...].astype(F32), D).reshape(128, D)
    xh_t, r_t = normalise(middle)
    normed_t = (xh_t * (1.0 + stretch_t) + shift_t).astype(BF)
    xn[4 * core + x] = normed_t

    def normed_x(i, back):
        block = 4 * core + (lax.rem(x + 4 - i, 4) if back else x)
        return pltpu.make_async_remote_copy(
            src_ref=xn.at[block],
            dst_ref=xn.at[block],
            send_sem=xnsem.at[0, i],
            recv_sem=xnsem.at[1, i],
            device_id=on_x(lax.rem(x + i, 4)),
            device_id_type=MESH,
        )

    def normed_core(back):
        side = pl.ds(4 * (1 - core if back else core), 4)
        return pltpu.make_async_remote_copy(
            src_ref=xn.at[side],
            dst_ref=xn.at[side],
            send_sem=xnsem.at[0, 0],
            recv_sem=xnsem.at[1, 0],
            device_id={"patch": p + 1 - 2 * core},
            device_id_type=MESH,
        )

    for i in range(1, 4):
        normed_x(i, False).start()
    proj[...] = nt(normed_t, wqt[...])
    same = lax.rem(lax.broadcasted_iota(jnp.int32, (128, 128), 0), 8) == lax.rem(
        lax.broadcasted_iota(jnp.int32, (128, 128), 1), 8
    )
    heads, att_parts, dq_parts, dk_parts, dv_parts = [], [], [], [], []
    for h in range(HEADS):
        q = proj[:, HD * h : HD * h + HD]
        k = proj[:, ATT + HD * h : ATT + HD * h + HD]
        v = proj[:, 2 * ATT + HD * h : 2 * ATT + HD * h + HD].astype(BF)
        rq = inverse_norm(q)
        rk = inverse_norm(k)
        q = q * rq
        k = k * rk
        e = nt(q.astype(BF), k.astype(BF)) * (SCALE * LOG2E)
        e = jnp.where(same, jnp.exp2(e), 0.0)
        soft = e * (1.0 / jnp.sum(e, axis=-1, keepdims=True))
        att_parts.append(nn(soft.astype(BF), v))
        heads.append((q, k, v, rq, rk, soft))
    att_t = jnp.concatenate(att_parts, axis=-1)
    c2_s[...] = fold(att_t.reshape(16, 8, ATT), 384).astype(BF)
    ex_c2.start()
    ex_t2.wait()
    dout_t = unfold(t2_r[...].astype(F32), ATT).reshape(128, ATT)
    for h, (q, k, v, rq, rk, soft) in enumerate(heads):
        do = dout_t[:, HD * h : HD * h + HD].astype(BF)
        dp = nt(do, v)
        ds = (soft * (dp - jnp.sum(dp * soft, axis=-1, keepdims=True)) * SCALE).astype(BF)
        dq_parts.append(head_back(rounded(nn(ds, k.astype(BF))), q, rq))
        dk_parts.append(head_back(rounded(tn(ds, q.astype(BF))), k, rk))
        dv_parts.append(tn(soft.astype(BF), do))
    parts = [part.astype(BF) for part in dq_parts + dk_parts + dv_parts]
    dproj_t = jnp.concatenate(parts, axis=-1)
    dn = nn(dproj_t, wqt[...])
    back = normalise_back(dn, stretch_t, xh_t, r_t)
    dm_s[...] = fold(back.reshape(16, 8, D), 640).astype(BF)
    ex_dm.start()

    for cc in range(2):
        for xx in range(4):
            at = 108 * (4 * xx + cc)
            row = [dproj_t[:, at : at + 108], zeros(128, 20, dtype=BF)]
            row += [dproj_t[:, at + 216 : at + 324], zeros(128, 20, dtype=BF)]
            dt_s[4 * cc + xx] = jnp.concatenate(row, axis=-1)
    ex_dt.start()

    ex_c2.wait()
    att_t = unfold(c2_r[...].astype(F32), ATT).reshape(128, ATT)
    xl[0, core] = jnp.concatenate(spread_rows(att_t.astype(BF)), axis=-1)
    for copy in pair_copies(0, core):
        copy.start()
    for i in range(1, 4):
        gather_x(i, True).wait()
    gather_core(False).start()
    for copy in pair_copies(0, 1 - core):
        copy.wait()
    lt[...] = jnp.transpose(xl[0].reshape(256, 640).astype(F32)).astype(BF)
    g = nn(lt[...], xr[0].reshape(256, 640))
    for yy in range(4):
        syo[yy] = g[160 * yy : 160 * yy + 160].astype(BF)
    ex_yo.start()
    gather_core(True).wait()
    for i in range(8):
        block = ng[i // 4, i % 4].reshape(128, D).astype(F32)
        block = jnp.transpose(block).reshape(4, 4, HD, 128)
        for yy in range(4):
            rows = block[:, yy].reshape(288, 128)
            ngt[288 * yy : 288 * yy + 288, 128 * i : 128 * i + 128] = rows.astype(BF)

    ex_dm.wait()
    back = unfold(dm_r[...].astype(F32), D).reshape(2, 64, D)
    parts = []
    for c in range(2):
        total = rounded(cot[c].astype(F32) + back[c])
        dmid[c] = total.astype(BF)
        parts.append((total * mod_s[2, c : c + 1, :]).astype(BF))
    scaled_s = jnp.concatenate(parts, axis=0)
    tokens = nt(scaled_s, wos[...]).astype(BF).reshape(2, 64, ATT)
    for c in range(2):
        for h in range(HEADS):
            part = tokens[c][:, HD * h : HD * h + HD].reshape(4, 16, HD)
            row = [part[j] for j in range(4)] + [zeros(16, 96, dtype=BF)]
            c1_s[owner(c, h)] = jnp.concatenate(row, axis=-1)
    ex_c1.start()

    for cc in range(2):
        xrv[1, cc] = core_columns(scaled_s, cc)
    xr[1, core] = xrv[1, core]
    for copy in pair_copies(1, core):
        copy.start()
    for i in range(1, 4):
        normed_x(i, True).wait()
    normed_core(False).start()
    for copy in pair_copies(1, 1 - core):
        copy.wait()
    lt[...] = jnp.transpose(xr[1].reshape(256, 640).astype(F32)).astype(BF)
    g = nn(lt[...], xl[1].reshape(256, 640))
    for i in range(4):
        sxs[i] = g[144 * i : 144 * i + 144].astype(BF)
    ex_xs.start()
    normed_core(True).wait()
    ex_dt.wait()
    g = tn(xn[...].reshape(1024, D), dt_r[...].reshape(1024, 256)).reshape(4, 4, HD, 256)
    for yy in range(4):
        syq[yy] = g[:, yy].reshape(288, 256).astype(BF)
    ex_yq.start()
    ex_c1.wait()
    got_do = c1_r[...]
    parts = [got_do[:, :, HD * j : HD * j + HD] for j in range(4)]
    do_b[...] = (jnp.stack(parts, axis=1).reshape(1024, HD).astype(F32) * rl[...]).astype(BF)
    dk_f[...] = jnp.zeros_like(dk_f)
    dv_f[...] = jnp.zeros_like(dv_f)

    def attend_back(i, carry):
        part = lax.rem(lax.div(x, 2) + 1 + i, 2)
        at = pl.ds(pl.multiple_of(part * 512, 512), 512)
        qb, dob = q_b[at, :], do_b[at, :]
        e = jnp.exp2(nt(k_b[...], qb) * (SCALE * LOG2E))
        dp = nt(v_b[...], dob)
        shift = rrow[:, at] * jnp.sum(dp * e, axis=0, keepdims=True)
        ds = (e * (dp - shift)).astype(BF)
        dv_f[...] += nn(e.astype(BF), dob)
        dk_f[...] += nn(ds, qb)
        dq = rounded(jnp.transpose(nn(kt_b[...], ds))[:, :HD] * SCALE)
        dq = head_back(dq, qb.astype(F32), rqk[at, 0:1]).astype(BF)
        blocks = pl.ds(8 * part, 8)
        dgq[blocks] = dq.reshape(8, 64, HD)
        dq = dq.reshape(8, 4, 16, HD)
        row = [dq[:, j].reshape(128, HD) for j in range(4)] + [zeros(128, 96, dtype=BF)]
        dq_s[blocks] = jnp.concatenate(row, axis=-1).reshape(8, 16, 384)
        for j in range(8):
            to = 8 * part + j

            @pl.when(to != p)
            def _():
                ex_dq.copy(to, p).start()

        return carry

    lax.fori_loop(0, 2, attend_back, 0)
    dq_r[p] = dq_s[p]
    for part in range(4):
        at = pl.ds(256 * part, 256)
        dk = head_back(rounded(dk_f[at, :] * SCALE), k_b[at, :].astype(F32), rqk[at, 1:2])
        row = jnp.concatenate([dk.astype(BF), dv_f[at, :].astype(BF)], axis=-1)
        dg[4 * part : 4 * part + 4] = row.reshape(4, 64, 2 * HD)
        row = row.reshape(4, 4, 16, 2 * HD)
        row = [row[:, j].reshape(64, 2 * HD) for j in range(4)] + [zeros(64, 64, dtype=BF)]
        d_s[4 * part : 4 * part + 4] = jnp.concatenate(row, axis=-1).reshape(4, 16, 640)
    ex_d.start()

    order = [4 * xx + 2 * s + cc for cc in range(2) for xx in range(4) for s in range(2)]
    right = [jnp.concatenate([ref[i] for i in order], axis=0) for ref in (dgq, dg)]
    right = jnp.concatenate(right + [zeros(1024, 8, dtype=BF)], axis=-1)
    for i in range(1, 5):
        yy = lax.rem(y + i, 4)
        rows = pl.ds(pl.multiple_of(288 * yy, 288), 288)
        gys[yy] = nn(ngt[rows, :], right).astype(BF)
        if i < 4:
            ex_gy.copy(yy, y).start()
    gyr[y] = gys[y]
    ex_xs.wait()
    total = sum(rxs[i].astype(F32) for i in range(4))
    for i in range(4):
        part = total[:, 160 * i : 160 * i + 160]
        rest = [part[48 * j : 48 * j + 48, 128:] for j in range(3)] + [zeros(48, 32)]
        rest = jnp.concatenate(rest, axis=-1)
        sys[i] = jnp.concatenate([part[:, :128], rest], axis=0).astype(BF)
    ex_ys.start()
    ex_yo.wait()
    total = sum(ryo[i].astype(F32) for i in range(4))
    for i in range(4):
        sxo[i] = widen(total[:, 144 * i : 144 * i + 144], 256).astype(BF)
    ex_xo.start()
    ex_yq.wait()
    total = sum(ryq[i].astype(F32) for i in range(4))
    for i in range(8):
        zz, s = i % 4, i // 4
        part = total[HD * zz : HD * zz + HD, 128 * s : 128 * s + 108]
        rest = [part[64:, 18 * j : 18 * j + 18] for j in range(6)] + [zeros(16, 18)]
        rest = jnp.concatenate(rest, axis=0)
        szq[i] = jnp.concatenate([part[:64], rest, zeros(64, 2)], axis=-1).astype(BF)
    ex_zq.start()


    ex_xo.wait()
    first = sum(rxo[i].astype(F32) for i in range(4))
    ex_gy.wait()
    total = sum(gyr[i].astype(F32) for i in range(4)).reshape(4, 3, 24, 224)
    for b in range(6):
        cols = [total[:, r, :, 36 * b : 36 * b + 36] for r in range(3)] + [zeros(4, 24, 20)]
        cols = jnp.concatenate(cols, axis=-1)
        fs[:, b] = jnp.concatenate([cols, zeros(4, 8, 128)], axis=1).astype(BF)

    def piece(i, b):
        to_z = lax.rem(zl + i, 4)
        block = 16 * (b // 2) + 2 * head + b % 2
        to, slot = lax.div(block, 3), lax.rem(block, 3)
        copy = pltpu.make_async_remote_copy(
            src_ref=fs.at[to_z, b],
            dst_ref=fr.at[slot, z],
            send_sem=fs_sem.at[b if i == 0 else 6],
            recv_sem=fr_sem.at[2 * slot + zh if i == 0 else 6],
            device_id={"frame": 4 * to_z + y, "patch": to},
            device_id_type=MESH,
        )
        return to, slot, copy

    for i in range(4):
        for b in range(6):
            to, slot, copy = piece(i, b)
            if i > 0:
                copy.start()
            else:

                @pl.when(to != p)
                def _():
                    copy.start()

                @pl.when(to == p)
                def _():
                    fr[slot, z] = fs[zl, b]

    ex_ys.wait()
    other = sum(rys[i].astype(F32) for i in range(4))
    rest = jnp.concatenate([other[144:, 32 * j : 32 * j + 32] for j in range(3)], axis=0)
    other = widen(jnp.concatenate([other[:144], rest], axis=-1), 256)
    other = jnp.transpose(jnp.concatenate([other, zeros(112, 256)], axis=0))
    for i in range(8):
        zz, s = i % 4, i // 4
        rows, cols = slice(40 * zz, 40 * zz + 36), slice(HD * s, HD * s + HD)
        part = jnp.concatenate([first[rows, cols], other[rows, cols]], axis=0)
        rest = jnp.concatenate([part[48:, :36], part[48:, 36:]], axis=0)
        szo[i] = jnp.concatenate([part[:48], rest, zeros(48, 20)], axis=-1).astype(BF)
    ex_zo.start()

    ex_dq.wait()
    ex_d.wait()
    parts = []
    for c in range(2):
        firsts = [dq_r[owner(c, h)] for h in range(HEADS)]
        blocks = [d_r[owner(c, h)] for h in range(HEADS)]
        for i in range(4):
            row = [b[:, HD * i : HD * i + HD] for b in firsts]
            at = [2 * HD * i + HD * j for j in range(2)]
            row += [b[:, a : a + HD] for a in at for b in blocks]
            parts.append(jnp.concatenate(row, axis=-1))
    dn = nn(jnp.concatenate(parts, axis=0), wqs[...])
    for c in range(2):
        xh, r = normalise(lat[c].astype(F32))
        back = normalise_back(dn[64 * c : 64 * c + 64], mod_s[1, c : c + 1, :], xh, r)
        gl[c] = (dmid[c].astype(F32) + back).astype(BF)
    writes[0].start()


    ex_zq.wait()
    total = sum(rzq[i].astype(F32) for i in range(8))
    rest = [total[8 * j : 8 * j + 8, 108:126] for j in range(6)]
    rest = jnp.concatenate(rest, axis=-1)
    gqt[...] = jnp.concatenate([total[:, :108], rest], axis=0)
    writes[1].start()
    ex_zo.wait()
    total = sum(rzo[i].astype(F32) for i in range(8))
    rest = jnp.concatenate([total[:24, 72:108], total[24:, 72:108]], axis=-1)
    total = jnp.concatenate([total[:, :HD], rest], axis=0)
    got[...] = total[:36]
    gos[...] = total[36:]
    writes[2].start()
    writes[3].start()

    for b in range(6):
        to, slot, copy = piece(0, b)

        @pl.when(to != p)
        def _():
            copy.wait_send()

    for slot in range(3):
        left = lax.rem(3 * p + slot, 16)
        source = lax.div(left, 4) * 4 + lax.rem(lax.div(left, 2), 2)
        for c in range(2):
            at = 4 * c + zl
            copy = pltpu.make_async_remote_copy(
                src_ref=fs.at[0, 0],
                dst_ref=fr.at[slot, at],
                send_sem=fs_sem.at[0],
                recv_sem=fr_sem.at[2 * slot + c],
                device_id={"patch": source + 2 * c},
                device_id_type=MESH,
            )

            @pl.when(source + 2 * c != p)
            def _():
                copy.wait_recv()

    for ref, sem in ((fs.at[pl.ds(0, 3)], fs_sem.at[6]), (fr.at[:, pl.ds(0, 6)], fr_sem.at[6])):
        pltpu.make_async_copy(ref, ref, sem).wait()

    cols = []
    for slot in range(3):
        total = sum(fr[slot, i].astype(F32) for i in range(8))
        cols.append(
            jnp.concatenate([total[:24, 36 * r : 36 * r + 36] for r in range(3)], axis=0)
        )
    gqs[...] = jnp.concatenate(cols, axis=-1)
    writes[4].start()
    for write in writes:
        write.wait()


def hand_over(*refs):
    given, out, held, sem = refs[:5], refs[5:10], refs[10:15], refs[15]
    into = [pltpu.make_async_copy(given[i], held[i], sem.at[0, i]) for i in range(5)]
    back = [pltpu.make_async_copy(held[i], out[i], sem.at[1, i]) for i in range(5)]
    for copy in into:
        copy.start()
    for i in range(5):
        into[i].wait()
        back[i].start()
    for copy in back:
        copy.wait()


def body(lat, mod_s, mod_t, wqs, wos, wqt, wot, cot):
    hbm = pl.BlockSpec(memory_space=pl.ANY)
    dma = pltpu.SemaphoreType.DMA

    def buf(*shape):
        return pltpu.VMEM(shape, BF)

    def wide(*shape):
        return pltpu.VMEM(shape, F32)

    outs = pl.pallas_call(
        kernel,
        out_shape=(
            jax.ShapeDtypeStruct((2, 64, D), BF),
            jax.ShapeDtypeStruct((72, 108), F32),
            jax.ShapeDtypeStruct((36, 72), F32),
            jax.ShapeDtypeStruct((72, 108), F32),
            jax.ShapeDtypeStruct((36, 72), F32),
        ),
        in_specs=[hbm] * 8,
        out_specs=(hbm,) * 5,
        scratch_shapes=[
            buf(2, 64, D), buf(2, 64, D), wide(3, 2, D), wide(3, 2, D),
            buf(2, 64, D), wide(72, 108), wide(36, 72), wide(72, 108), wide(36, 72), dma((9,)),
            buf(QKV, D), buf(ATT, D), buf(QKV, D), buf(ATT, D), dma((4,)),
            buf(2, 64, D), wide(128, QKV),
            buf(16, 16, 896), buf(16, 16, 896),
            buf(16, 16, 384), buf(16, 16, 384),
            buf(128, ATT), buf(2, 64, D), buf(2, 64, D),
            buf(16, 16, 640), buf(16, 16, 640),
            buf(16, 16, 384), buf(16, 16, 384),
            buf(16, 16, 384), buf(16, 16, 384),
            buf(16, 16, 384), buf(16, 16, 384),
            buf(16, 16, 640), buf(16, 16, 640),
            buf(16, 16, 384), buf(16, 16, 384), buf(16, 16, 640), buf(16, 16, 640),
            buf(16, 64, HD), buf(16, 64, 2 * HD), buf(1152, 1024),
            dma((9, 2)),
            buf(1024, HD), buf(1024, HD), buf(1024, HD), wide(1024, 2), wide(1024, 1), wide(1, 1024),
            buf(1024, HD), buf(128, 1024), wide(1024, HD), wide(1024, HD),
            buf(2, 4, 2, 64, D), dma((2, 5)),
            buf(8, 128, D), dma((2, 4)), buf(8, 128, 256), buf(8, 128, 256), dma((2,)),
            buf(2, 2, 128, 640), buf(2, 2, 128, 640), buf(2, 2, 128, 640), dma((2, 4)),
            buf(640, 256),
            buf(4, 288, 256), buf(4, 288, 256),
            buf(4, 160, 640), buf(4, 160, 640),
            buf(4, 160, 256), buf(4, 160, 256),
            buf(4, 144, 640), buf(4, 144, 640),
            buf(4, 192, 128), buf(4, 192, 128),
            buf(4, 288, 224), buf(4, 288, 224),
            dma((6, 2)),
            buf(8, 64, 128), buf(8, 64, 128),
            buf(8, 48, 128), buf(8, 48, 128),
            dma((2, 2)),
            buf(4, 6, 32, 128), buf(3, 8, 32, 128), dma((7,)), dma((7,)),
        ],
        compiler_params=pltpu.CompilerParams(
            collective_id=0, has_side_effects=True, vmem_limit_bytes=60 * 1024 * 1024
        ),
    )(
        lat.reshape(2, 64, D),
        cot.reshape(2, 64, D),
        mod_s.transpose(1, 0, 2),
        mod_t.transpose(1, 0, 2),
        wqs.T,
        wos,
        wqt.T,
        wot,
    )
    outs = pl.pallas_call(
        hand_over,
        out_shape=tuple(jax.ShapeDtypeStruct(o.shape, o.dtype) for o in outs),
        in_specs=[hbm] * 5,
        out_specs=(hbm,) * 5,
        scratch_shapes=[pltpu.VMEM(o.shape, o.dtype) for o in outs] + [dma((2, 5))],
    )(*outs)
    return (outs[0].reshape(2, 1, 64, D),) + tuple(outs[1:])


def solution(mesh):
    tokens = P(None, "frame", "patch", None)
    return jax.shard_map(
        body,
        mesh=mesh,
        in_specs=(tokens,) + (P(),) * 6 + (tokens,),
        out_specs=(tokens,) + (P("frame", "patch"),) * 4,
        check_vma=False,
    )
```
